32 devices in a mesh: groups: 2 (over x), state: 16 (over z, y, core).
Axes of the slice: x: 2, y: 2, z: 4, core: 2. Of those that a mesh axis runs over, the one named last changes fastest.
Arguments:
- background_draws_table: float32 [256, 65536], P('state', 'groups'), parts along dimension 1
- measurement_reading: float32 [512, 32], P('groups'), parts along dimension 0, may hold values from -8 to 8
- measurement_precision: float32 [512, 32], P('groups'), parts along dimension 0, may hold values from 0.25 to 4
- sensed_point_position: int32 [512, 32], P('groups'), parts along dimension 0, may hold values from 0 to 127
- measurement_tally: int32 [512], P('groups'), parts along dimension 0, may hold values from 1 to 32, as said below
- adjacent_tile_number: int32 [512, 5], P(('groups', 'state')), parts along dimension 0, may hold values from -1 to 255, as said below
Outputs:
- analysis: float32 [256, 65536], P('state', 'groups'), parts along dimension 1
The draws below stay inside these ranges and needn't reach their ends.
There are 2 independent parts, one for each index of `groups`. The reference program is written for one: setup_inputs(seed, part) draws one part's arguments, and reference() takes and returns one part's arrays. A program takes and returns all parts, laid end to end along the dimension named above; each array names one. Nothing has to cross between parts.
Inputs may be any that keep to these rules, and one draw needn't show every extreme that they name: `measurement_tally`: every block's count is at least 1 and at most 32; some block has exactly 32. `adjacent_tile_number`: entry j of row b is either b + j - 2 or -1; it is -1 where b + j - 2 lies outside the grid of blocks, and the middle entry is always b.
All inputs are finite; a program needn't handle non-finite values.
Results may differ from the reference program's by a relative error of at most 0.0003.
Values sent between devices are 32-bit elements; how exact they have to be, the bound alone decides.
No kernel may reach another device: no remote copies, remote signals or barrier semaphores. Data moves between devices by JAX's collectives and lax.ppermute only.
A program may use at most 128 MiB of HBM per device.

```python
import math
import jax
import jax.numpy as jnp
from jax import lax

K = 256
PARTITION_SPAN = 128
OB = 32
R = 2
NS_ITERS = 5
LOC = 128
LOCAL_PARTITIONS = 256
NCELL = 32768


def draw_background_draws_table(key, part):
    key = jax.random.fold_in(key, 11)
    key_mean, key_scale, key_noise = jax.random.split(key, 3)
    cell_mean = jax.random.normal(key_mean, (NCELL,), jnp.float32)
    cell_scale = jnp.exp(jax.random.uniform(key_scale, (NCELL,), jnp.float32, math.log(0.3), math.log(3.0)))
    noise_field = jax.random.normal(key_noise, (K, NCELL), jnp.float32)
    return cell_mean[None, :] + cell_scale[None, :] * noise_field


def draw_measurement_tally(key, part):
    key = jax.random.fold_in(key, 23)
    key_count, key_full = jax.random.split(key)
    counts = jax.random.randint(key_count, (LOCAL_PARTITIONS,), 1, OB + 1, dtype=jnp.int32)
    full_block = jax.random.randint(key_full, (), 0, LOCAL_PARTITIONS, dtype=jnp.int32)
    return jnp.where(jnp.arange(LOCAL_PARTITIONS, dtype=jnp.int32) == full_block, jnp.int32(OB), counts)


def draw_adjacent_tile_number(key, part):
    key = jax.random.fold_in(key, 37)
    keep_flag = jax.random.randint(key, (LOCAL_PARTITIONS, 2 * R + 1), 0, 10, dtype=jnp.int32) < 7
    blocks = jnp.arange(LOCAL_PARTITIONS, dtype=jnp.int32)[:, None] + jnp.arange(2 * R + 1, dtype=jnp.int32)[None, :] - R
    inside = (blocks >= 0) & (blocks < LOCAL_PARTITIONS)
    centre = jnp.arange(2 * R + 1, dtype=jnp.int32)[None, :] == R
    return jnp.where((keep_flag | centre) & inside, blocks, -1).astype(jnp.int32)


def plant(array, key, least, high):
    shape = array.shape
    spot = [jax.random.randint(jax.random.fold_in(key, axis), (), 0, shape[axis]) for axis in range(len(shape))]
    array = array.at[tuple(spot)].set(least)
    longest = shape.index(max(shape))
    spot[longest] = (spot[longest] + 1) % shape[longest]
    return array.at[tuple(spot)].set(high)


def normal_values(rng, shape, deviation, reach, kind=jnp.bfloat16):
    return jnp.clip(deviation * jax.random.normal(rng, shape, jnp.float32), -reach, reach).astype(kind)


def setup_inputs(seed: int = 0, part: int = 0) -> dict:
    splits = jax.random.split(jax.random.key(seed), 7)
    part_splits = jax.random.split(jax.random.fold_in(splits[6], part), 7)
    background_draws_table = draw_background_draws_table(jax.random.fold_in(jax.random.fold_in(splits[6], part), 71), part)
    measurement_reading = normal_values(part_splits[1], (LOCAL_PARTITIONS, OB), 1.5, 8.0, jnp.float32)
    measurement_precision = jnp.clip(jnp.exp(jax.random.uniform(part_splits[2], (LOCAL_PARTITIONS, OB), jnp.float32, math.log(0.25), math.log(4.0))), 0.25, 4.0)
    sensed_point_position = plant(jax.random.randint(part_splits[3], (LOCAL_PARTITIONS, OB), 0, PARTITION_SPAN), jax.random.fold_in(part_splits[3], 1), 0, PARTITION_SPAN - 1).astype(jnp.int32)
    measurement_tally = draw_measurement_tally(jax.random.fold_in(jax.random.fold_in(splits[6], part), 71), part)
    adjacent_tile_number = draw_adjacent_tile_number(jax.random.fold_in(jax.random.fold_in(splits[6], part), 71), part)
    return dict(background_draws_table=background_draws_table, measurement_reading=measurement_reading, measurement_precision=measurement_precision, sensed_point_position=sensed_point_position, measurement_tally=measurement_tally, adjacent_tile_number=adjacent_tile_number)


PRECISE = lax.Precision.HIGHEST

def transform(obs_anom, innovation, weight):
    sample_fields = obs_anom.shape[0]
    scaled = obs_anom * weight[None, :]
    spread = jnp.dot(scaled, obs_anom.T, precision=PRECISE) / (sample_fields - 1.0)
    norm_size = 1.0 + jnp.sqrt(jnp.sum(spread * spread))
    identity = jnp.eye(sample_fields, dtype=jnp.float32)
    forward = (identity + spread) / norm_size
    inverse = identity
    for sweep_index in range(NS_ITERS):
        middle = 1.5 * identity - 0.5 * jnp.dot(inverse, forward, precision=PRECISE)
        forward = jnp.dot(forward, middle, precision=PRECISE)
        inverse = jnp.dot(middle, inverse, precision=PRECISE)
    inv_root = inverse / jnp.sqrt(norm_size)
    pull_vec = jnp.dot(scaled, innovation, precision=PRECISE) / (sample_fields - 1.0)
    mean_weight = jnp.dot(inv_root, jnp.dot(inv_root, pull_vec, precision=PRECISE), precision=PRECISE)
    return inv_root + mean_weight[:, None]

def reference(background_draws_table, measurement_reading, measurement_precision, sensed_point_position, measurement_tally, adjacent_tile_number):
    sample_fields = background_draws_table.shape[0]
    expected_ocean_background = lax.optimization_barrier(jnp.mean(background_draws_table, axis=0))
    spread_departures = background_draws_table - expected_ocean_background[None, :]
    measured_readings = jnp.take_along_axis(background_draws_table.reshape(sample_fields, LOCAL_PARTITIONS, PARTITION_SPAN), sensed_point_position[None, :, :], axis=2)
    anom_blocks = spread_departures.reshape(sample_fields, LOCAL_PARTITIONS, PARTITION_SPAN)
    partition_centroids = expected_ocean_background.reshape(LOCAL_PARTITIONS, PARTITION_SPAN)
    slot_index = jnp.arange(OB, dtype=jnp.int32)

    def one_block(block_id):
        source = adjacent_tile_number[block_id]
        usable = source >= 0
        safe_index = jnp.where(usable, source, 0).astype(jnp.int32)
        obs_raw = measured_readings[:, safe_index, :]
        obs_mean = lax.optimization_barrier(jnp.mean(obs_raw, axis=0))
        obs_anom = obs_raw - obs_mean[None]
        innovation = measurement_reading[safe_index] - obs_mean
        counts = measurement_tally[safe_index]
        active = slot_index[None, :] < counts[:, None]
        distance = ((safe_index - block_id) * PARTITION_SPAN).astype(jnp.float32)[:, None] + sensed_point_position[safe_index].astype(jnp.float32) - 0.5 * (PARTITION_SPAN - 1)
        weight = measurement_precision[safe_index] * jnp.exp(-0.5 * (distance / LOC) ** 2) * active.astype(jnp.float32) * usable.astype(jnp.float32)[:, None]
        width_obs = (2 * R + 1) * OB
        matrix = transform(obs_anom.reshape(sample_fields, width_obs), innovation.reshape(width_obs), weight.reshape(width_obs))
        block_anom = lax.dynamic_index_in_dim(anom_blocks, block_id, 1, keepdims=False)
        block_mean = lax.dynamic_index_in_dim(partition_centroids, block_id, 0, keepdims=False)
        return block_mean[None, :] + jnp.einsum('jc,jk->kc', block_anom, matrix, precision=PRECISE)
    analysis_result_vectors = lax.map(one_block, jnp.arange(LOCAL_PARTITIONS, dtype=jnp.int32))
    return analysis_result_vectors.transpose(1, 0, 2).reshape(sample_fields, NCELL)
```

```python
import jax
import jax.numpy as jnp
from jax import lax
from jax.experimental import pallas as pl
from jax.experimental.pallas import tpu as pltpu
from jax.sharding import PartitionSpec as P

PARTITION_SPAN = 128
OB = 32
R = 2
NS_ITERS = 5
LOC = 128

QUAD = PARTITION_SPAN // OB
NN = (((1,), (0,)), ((), ()))
NT = (((1,), (1,)), ((), ()))


def halves(values):
    high = values.astype(jnp.bfloat16)
    return high, (values - high.astype(jnp.float32)).astype(jnp.bfloat16)


def times(left, right, dims):
    (left_high, left_low), (right_high, right_low) = left, right
    return lax.dot_general(
        jnp.concatenate([left_high, left_high, left_low], axis=1),
        jnp.concatenate([right_high, right_low, right_high], axis=dims[0][1][0]),
        dims,
        preferred_element_type=jnp.float32,
    )


def updated(blocks):
    scaled = []
    for fields, seen, root_weight, reading in blocks:
        seen_mean = jnp.mean(seen, axis=0, keepdims=True)
        pull = (reading - seen_mean) * root_weight
        scaled.append(
            (halves((seen - seen_mean) * root_weight), halves(jnp.broadcast_to(pull, (16, pull.shape[1]))))
        )
    products = [(times(root, root, NT), times(pull, root, NT)) for root, pull in scaled]
    states = []
    for (fields, *_), (spread, pull) in zip(blocks, products):
        squares = jnp.sum(jnp.sum(spread * spread, axis=0, keepdims=True), axis=1, keepdims=True)
        norm_size = 1.0 + jnp.sqrt(squares)
        unit = 1.0 / norm_size
        cells = fields.T
        centre = jnp.mean(cells, axis=1, keepdims=True)
        chain = jnp.concatenate([cells - centre, pull], axis=0)
        states.append((norm_size, centre, unit, spread * unit, chain))
    for sweep in range(NS_ITERS):
        last = sweep + 1 == NS_ITERS
        parts = [(halves(rest), halves(chain)) for *_, rest, chain in states]
        moved = [times(chain, rest, NN) for rest, chain in parts]
        square = [None if last else times(rest, rest, NN) for rest, _ in parts]
        gains = [1.5 - 0.5 * unit for _, _, unit, _, _ in states]
        chains = [gain * state[-1] - 0.5 * move for gain, state, move in zip(gains, states, moved)]
        if last:
            states = [(*state[:4], chain) for state, chain in zip(states, chains)]
            break
        middle = [
            (gain - 0.5 * unit) * rest - 0.5 * sq
            for gain, (_, _, unit, rest, _), sq in zip(gains, states, square)
        ]
        cubic = [times(halves(mid), rest, NN) for mid, (rest, _) in zip(middle, parts)]
        states = [
            (
                norm_size,
                centre,
                unit * gain * gain,
                gain * mid - (0.5 * unit * gain) * rest - 0.5 * cube,
                chain,
            )
            for (norm_size, centre, unit, rest, _), gain, mid, cube, chain in zip(
                states, gains, middle, cubic, chains
            )
        ]
    results = []
    for norm_size, centre, _, _, chain in states:
        chain = chain * lax.rsqrt(norm_size)
        moved = chain[:PARTITION_SPAN]
        shift = jnp.sum(moved * chain[PARTITION_SPAN : PARTITION_SPAN + 1], axis=1, keepdims=True)
        results.append((moved + (centre + shift)).T)
    return results


def pick_kernel(fields_ref, position_ref, seen_ref):
    members, width = fields_ref.shape
    span = PARTITION_SPAN
    amount = width // span
    lanes = lax.broadcasted_iota(jnp.int32, (members, span), 1)
    for quad in range(amount // QUAD):
        index = jnp.broadcast_to(position_ref[quad : quad + 1, :], (members, span))
        total = None
        for spot in range(QUAD):
            block = (quad * QUAD + spot - R) % amount
            found = jnp.take_along_axis(fields_ref[:, block * span : (block + 1) * span], index, axis=1)
            total = found if spot == 0 else jnp.where(lanes // OB == spot, found, total)
        seen_ref[:, quad * span : (quad + 1) * span] = total


def update_kernel(fields_ref, before_ref, own_ref, after_ref, weight_ref, reading_ref, result_ref):
    members, span = before_ref.shape
    step = pl.program_id(0)
    steps = pl.num_programs(0)
    lanes = lax.broadcasted_iota(jnp.int32, (members, span), 1)
    here = own_ref[:, pl.ds(pl.multiple_of(step * span, span), span)]
    following = own_ref[:, pl.ds(pl.multiple_of(lax.rem(step + 1, steps) * span, span), span)]
    first = jnp.where((step == 0) & (lanes < R * OB), before_ref[...], here)
    second = jnp.where((step == steps - 1) & (lanes >= R * OB), after_ref[...], following)
    seen = jnp.concatenate([first, second], axis=1)
    blocks = [
        (
            fields_ref[:, spot * span : (spot + 1) * span],
            seen,
            weight_ref[pl.ds(step * QUAD + spot, 1), :],
            reading_ref[pl.ds(step * QUAD + spot, 1), :],
        )
        for spot in range(QUAD)
    ]
    for spot, result in enumerate(updated(blocks)):
        result_ref[:, spot * span : (spot + 1) * span] = result


def windows(frame):
    quads = frame.reshape(-1, QUAD * OB)
    pairs = jnp.concatenate([quads[:-1], quads[1:]], axis=1)
    return jnp.broadcast_to(pairs[:, None, :], (pairs.shape[0], QUAD, pairs.shape[1])).reshape(-1, pairs.shape[1])


def body(
    background_draws_table,
    measurement_reading,
    measurement_precision,
    sensed_point_position,
    measurement_tally,
    adjacent_tile_number,
):
    devices = lax.axis_size("state")
    place = lax.axis_index("state")
    own_members, all_cells = background_draws_table.shape
    cells = all_cells // devices
    amount = cells // PARTITION_SPAN
    members = own_members * devices
    first_block = place * amount
    span = PARTITION_SPAN

    sent = background_draws_table.reshape(own_members, devices, cells).transpose(1, 0, 2)
    fields = lax.all_to_all(sent, "state", split_axis=0, concat_axis=0, tiled=True).reshape(members, cells)

    def frame(array):
        padded = jnp.pad(array, ((R, R),) + ((0, 0),) * (array.ndim - 1))
        return lax.dynamic_slice_in_dim(padded, first_block, amount + 2 * R, 0)

    position = windows(frame(sensed_point_position))
    reading = windows(frame(measurement_reading))
    precision = windows(frame(measurement_precision))
    tally = windows(jnp.broadcast_to(frame(measurement_tally)[:, None], (amount + 2 * R, OB)))
    lane = jnp.arange(2 * QUAD * OB, dtype=jnp.int32)[None, :]
    neighbour = lane // OB - (jnp.arange(amount, dtype=jnp.int32) % QUAD)[:, None]
    usable = jnp.zeros(neighbour.shape, jnp.bool_)
    for j in range(2 * R + 1):
        usable |= (neighbour == j) & (adjacent_tile_number[:, j : j + 1] >= 0)
    distance = (
        ((neighbour - R) * span).astype(jnp.float32) + position.astype(jnp.float32) - 0.5 * (span - 1)
    )
    weight = jnp.where(
        usable & (lane % OB < tally), precision * jnp.exp(-0.5 * (distance / LOC) ** 2), 0.0
    )
    root_weight = jnp.sqrt(weight / (members - 1.0))

    own_position = lax.dynamic_slice_in_dim(sensed_point_position, first_block, amount, 0)
    quad_position = jnp.roll(own_position, R, axis=0).reshape(amount // QUAD, QUAD * OB)
    vmem = pl.BlockSpec(memory_space=pltpu.VMEM)
    own_seen = pl.pallas_call(
        pick_kernel,
        out_shape=jax.ShapeDtypeStruct((members, amount * OB), jnp.float32),
        in_specs=[vmem, vmem],
        out_specs=vmem,
        compiler_params=pltpu.CompilerParams(vmem_limit_bytes=16 << 20),
    )(fields, quad_position)
    edge = own_seen[:, : QUAD * OB]
    before = lax.ppermute(edge, "state", [(i, i + 1) for i in range(devices - 1)])
    after = lax.ppermute(edge, "state", [(i + 1, i) for i in range(devices - 1)])
    steps = amount // QUAD

    def whole(*shape):
        return pl.BlockSpec(shape, lambda step: (0, 0))

    analysis = pl.pallas_call(
        update_kernel,
        grid=(steps,),
        out_shape=jax.ShapeDtypeStruct((members, cells), jnp.float32),
        in_specs=[
            pl.BlockSpec((members, QUAD * span), lambda step: (0, step)),
            whole(members, QUAD * OB),
            whole(members, amount * OB),
            whole(members, QUAD * OB),
            whole(amount, 2 * QUAD * OB),
            whole(amount, 2 * QUAD * OB),
        ],
        out_specs=pl.BlockSpec((members, QUAD * span), lambda step: (0, step)),
        compiler_params=pltpu.CompilerParams(vmem_limit_bytes=40 << 20),
    )(fields, before, own_seen, after, root_weight, reading)

    result = lax.all_to_all(
        analysis.reshape(devices, own_members, cells), "state", split_axis=0, concat_axis=0, tiled=True
    )
    return result.transpose(1, 0, 2).reshape(own_members, all_cells)


def solution(mesh):
    return jax.shard_map(
        body,
        mesh=mesh,
        in_specs=(
            P("state", "groups"),
            P("groups", None),
            P("groups", None),
            P("groups", None),
            P("groups"),
            P(("groups", "state"), None),
        ),
        out_specs=P("state", "groups"),
        check_vma=False,
    )
```

```python
import functools

import jax
import jax.numpy as jnp
from jax import lax
from jax.experimental import pallas as pl
from jax.experimental.pallas import tpu as pltpu
from jax.sharding import PartitionSpec as P

PARTITION_SPAN = 128
OB = 32
R = 2
NS_ITERS = 5
LOC = 128

QUAD = PARTITION_SPAN // OB
INNER = 4
NN = (((1,), (0,)), ((), ()))
NT = (((1,), (1,)), ((), ()))


def halves(values):
    high = values.astype(jnp.bfloat16)
    return high, (values - high.astype(jnp.float32)).astype(jnp.bfloat16)


def times(left, right, dims):
    (left_high, left_low), (right_high, right_low) = left, right
    return lax.dot_general(
        jnp.concatenate([left_high, left_high, left_low], axis=1),
        jnp.concatenate([right_high, right_low, right_high], axis=dims[0][1][0]),
        dims,
        preferred_element_type=jnp.float32,
    )


def updated(blocks):
    turns = [analysis(*block) for block in blocks]
    results = [None] * len(turns)
    while None in results:
        for index, turn in enumerate(turns):
            if results[index] is None:
                results[index] = next(turn)
    return results


def analysis(fields, seen, root_weight, reading):
    seen_mean = jnp.mean(seen, axis=0, keepdims=True)
    pull = (reading - seen_mean) * root_weight
    root = halves((seen - seen_mean) * root_weight)
    spread = times(root, root, NT)
    pull = times(halves(jnp.broadcast_to(pull, (16, pull.shape[1]))), root, NT)
    yield None
    squares = jnp.sum(jnp.sum(spread * spread, axis=0, keepdims=True), axis=1, keepdims=True)
    norm_size = 1.0 + jnp.sqrt(squares)
    unit = 1.0 / norm_size
    rest = spread * (-0.5 * unit)
    cells = fields.T
    centre = jnp.mean(cells, axis=1, keepdims=True)
    chain = jnp.concatenate([cells - centre, pull], axis=0)
    for sweep in range(NS_ITERS - 1):
        parts = halves(rest)
        gain = 1.5 - 0.5 * unit
        if sweep < NS_ITERS - 2:
            square = times(parts, parts, NN)
        moved = times(halves(chain), parts, NN)
        yield None
        if sweep < NS_ITERS - 2:
            once = (gain - 0.5 * unit) * rest + square
            cubic = times(halves(once), parts, NN)
        chain = gain * chain + moved
        if sweep < NS_ITERS - 2:
            yield None
            rest = gain * once - (0.5 * unit * gain) * rest + cubic
            unit = unit * gain * gain
    moved = times(halves(chain), parts, NN)
    yield None
    end = (-0.5 * unit) * chain + moved
    for _ in range(2):
        moved = times(halves(end), parts, NN)
        yield None
        end = gain * end + moved
    chain = (1.5 * chain + end) * lax.rsqrt(norm_size)
    moved = chain[:PARTITION_SPAN]
    shift = jnp.sum(moved * chain[PARTITION_SPAN : PARTITION_SPAN + 1], axis=1, keepdims=True)
    yield (moved + (centre + shift)).T


def picked(fields, position):
    members = fields[0].shape[0]
    span = PARTITION_SPAN
    index = jnp.broadcast_to(position, (members, span))
    lanes = lax.broadcasted_iota(jnp.int32, (members, span), 1)
    total = None
    for spot, field in enumerate(fields):
        found = jnp.take_along_axis(field, index, axis=1)
        total = found if spot == 0 else jnp.where(lanes // OB == spot, found, total)
    return total


def pick_kernel(fields_ref, position_ref, seen_ref):
    span = PARTITION_SPAN
    quads = position_ref.shape[0]
    amount = quads * QUAD
    for quad in range(quads):
        blocks = [(quad * QUAD + spot - R) % amount for spot in range(QUAD)]
        fields = [fields_ref[:, block * span : (block + 1) * span] for block in blocks]
        seen_ref[:, quad * span : (quad + 1) * span] = picked(fields, position_ref[quad : quad + 1, :])


def update_kernel(fields_ref, before_ref, own_ref, after_ref, weight_ref, reading_ref, result_ref):
    members, span = before_ref.shape
    step = pl.program_id(0)
    steps = pl.num_programs(0)
    lanes = lax.broadcasted_iota(jnp.int32, (members, span), 1)
    here = own_ref[:, pl.ds(pl.multiple_of(step * span, span), span)]
    following = own_ref[:, pl.ds(pl.multiple_of(lax.rem(step + 1, steps) * span, span), span)]
    first = jnp.where((step == 0) & (lanes < R * OB), before_ref[...], here)
    second = jnp.where((step == steps - 1) & (lanes >= R * OB), after_ref[...], following)
    seen = jnp.concatenate([first, second], axis=1)
    blocks = [
        (
            fields_ref[:, spot * span : (spot + 1) * span],
            seen,
            weight_ref[pl.ds(step * QUAD + spot, 1), :],
            reading_ref[pl.ds(step * QUAD + spot, 1), :],
        )
        for spot in range(QUAD)
    ]
    for spot, result in enumerate(updated(blocks)):
        result_ref[:, spot * span : (spot + 1) * span] = result


def terms_kernel(
    amount, members, reading_ref, precision_ref, position_ref, tally_ref, adjacent_ref, weight_ref, shown_ref, quad_ref
):
    first_block = lax.axis_index("state") * amount
    total = tally_ref.shape[0]
    quads = amount // QUAD
    span = PARTITION_SPAN
    lane = lax.broadcasted_iota(jnp.int32, (1, span), 1)
    low = lane < R * OB

    def tile(ref, quad):
        row = first_block // QUAD + quad
        before = ref[pl.ds(jnp.maximum(row - 1, 0), 1), :]
        after = ref[pl.ds(jnp.minimum(row, total // QUAD - 1), 1), :]
        return pltpu.roll(jnp.where(low, after, before), R * OB, 1)

    def counts(quad):
        found = jnp.zeros((1, span), jnp.int32)
        for spot in range(QUAD):
            block = jnp.clip(first_block + quad * QUAD + spot - R, 0, total - 1)
            found = jnp.where(lane // OB == spot, tally_ref[block], found)
        return found

    def pair(tiles, quad):
        return jnp.concatenate(tiles[quad : quad + 2], axis=1)

    positions = [tile(position_ref, quad) for quad in range(quads + 1)]
    readings = [tile(reading_ref, quad) for quad in range(quads + 1)]
    precisions = [tile(precision_ref, quad) for quad in range(quads + 1)]
    tallies = [counts(quad) for quad in range(quads + 1)]
    wide = lax.broadcasted_iota(jnp.int32, (1, 2 * span), 1)
    for block in range(amount):
        quad, spot = divmod(block, QUAD)
        neighbour = wide // OB - spot
        usable = jnp.zeros((1, 2 * span), jnp.float32)
        for j in range(2 * R + 1):
            there = jnp.where(adjacent_ref[block, j] >= 0, 1.0, 0.0)
            usable = jnp.where(neighbour == j, there, usable)
        distance = (
            ((neighbour - R) * span).astype(jnp.float32)
            + pair(positions, quad).astype(jnp.float32)
            - 0.5 * (span - 1)
        )
        decay = jnp.exp(-0.5 * (distance / LOC) ** 2)
        active = jnp.where(wide % OB < pair(tallies, quad), usable, 0.0)
        weight = pair(precisions, quad) * decay * active
        weight_ref[block : block + 1, :] = jnp.sqrt(weight / (members - 1.0))
        shown_ref[block : block + 1, :] = pair(readings, quad)
    edge = jnp.where(low, positions[quads], positions[0])
    for quad in range(quads):
        quad_ref[quad : quad + 1, :] = positions[quad] if quad else edge


def window_terms(reading, precision, position, tally, adjacent, members):
    amount = adjacent.shape[0]
    lanes = QUAD * OB
    vmem = pl.BlockSpec(memory_space=pltpu.VMEM)
    smem = pl.BlockSpec(memory_space=pltpu.SMEM)
    terms = jax.ShapeDtypeStruct((amount, 2 * lanes), jnp.float32)
    return pl.pallas_call(
        functools.partial(terms_kernel, amount, members),
        out_shape=[terms, terms, jax.ShapeDtypeStruct((amount // QUAD, lanes), jnp.int32)],
        in_specs=[vmem, vmem, vmem, smem, smem],
        out_specs=[vmem, vmem, vmem],
    )(*(array.reshape(-1, lanes) for array in (reading, precision, position)), tally, adjacent)


def part_kernel(fields_ref, position_ref, sent_ref, held_ref, sems):
    devices = sent_ref.shape[0]
    cells = fields_ref.shape[1] // devices
    span = PARTITION_SPAN
    half = R * span
    quads = cells // (QUAD * span)
    low = lax.broadcasted_iota(jnp.int32, (1, span), 1) < R * OB
    into, out = [], []
    for device in range(devices):
        source = fields_ref.at[:, pl.ds(device * cells, cells)]
        into.append(pltpu.make_async_copy(source, held_ref.at[device, :, pl.ds(0, cells)], sems.at[device]))
        out.append(pltpu.make_async_copy(held_ref.at[device], sent_ref.at[device], sems.at[devices + device]))
    for copy in into:
        copy.start()
    for copy in into:
        copy.wait()
    for device in range(devices):
        left, right = max(device - 1, 0), min(device + 1, devices - 1)
        before = position_ref[left * quads + quads - 1 : (left + 1) * quads, :]
        after = position_ref[right * quads : right * quads + 1, :]
        position = pltpu.roll(jnp.where(low, after, before), R * OB, 1)
        blocks = [(left, cells - half + spot * span) for spot in range(R)]
        blocks += [(right, spot * span) for spot in range(R)]
        fields = [held_ref[owner, :, start : start + span] for owner, start in blocks]
        held_ref[device, :, cells : cells + span] = picked(fields, position)
        out[device].start()
    for copy in out:
        copy.wait()


def turn_kernel(rows, parts, *refs):
    given, made = refs[:-parts], refs[-parts:]
    width = given[0].shape[1]
    many = made[0].shape[0] // rows
    for number, source in enumerate(given):
        side, i = divmod(number, many)
        for j, target in enumerate(made):
            target[i * rows : (i + 1) * rows, side * width : (side + 1) * width] = source[j * rows : (j + 1) * rows, :]


def place_kernel(distances, cells, starts, *refs):
    *parts, result_ref, sems = refs
    place = lax.axis_index("state")
    rows = result_ref.shape[0]
    width = QUAD * PARTITION_SPAN
    started = []
    for i, part in enumerate(parts):
        for j in range(part.shape[0] // rows):
            device = place ^ distances[i][j] if distances else j
            for k, start in enumerate(starts):
                source = part.at[pl.ds(j * rows, rows), pl.ds(k * width, width)]
                target = result_ref.at[:, pl.ds(pl.multiple_of(device * cells + start, width), width)]
                started.append(pltpu.make_async_copy(source, target, sems.at[len(started)]))
                started[-1].start()
    for copy in started:
        copy.wait()


def place_more_kernel(distances, cells, starts, *refs):
    *parts, _, result_ref, sems = refs
    place_kernel(distances, cells, starts, *parts, result_ref, sems)


def reordered(ref, devices):
    place = lax.axis_index("state")
    rows = ref.shape[0] // devices
    starts = [pl.multiple_of((place ^ distance) * rows, rows) for distance in range(devices)]
    return jnp.concatenate([ref[pl.ds(start, rows), :] for start in starts], axis=0)


def blocks_of(fields, here, there, first, weight_ref, reading_ref):
    span = PARTITION_SPAN
    seen = jnp.concatenate([here, there], axis=1)
    blocks = []
    for spot in range(QUAD):
        terms = [ref[pl.ds(first + spot, 1), :] for ref in (weight_ref, reading_ref)]
        blocks.append((fields[:, spot * span : (spot + 1) * span], seen, *terms))
    return blocks


def head_kernel(quad, devices, fields_ref, here_ref, there_ref, beyond_ref, weight_ref, reading_ref, *results):
    span = PARTITION_SPAN
    fields, here, there, beyond = [
        reordered(ref, devices) for ref in (fields_ref, here_ref, there_ref, beyond_ref)
    ]
    if quad == 0:
        left = lax.broadcasted_iota(jnp.int32, here.shape, 1) < R * OB
        here = jnp.where(left, beyond, here)
    for spot, result in enumerate(updated(blocks_of(fields, here, there, quad * QUAD, weight_ref, reading_ref))):
        start = 0
        for result_ref in results:
            rows = result_ref.shape[0]
            result_ref[:, spot * span : (spot + 1) * span] = result[start : start + rows]
            start += rows


def tail_kernel(fields_ref, here_ref, there_ref, beyond_ref, weight_ref, reading_ref, result_ref):
    span = PARTITION_SPAN
    step, steps = pl.program_id(0), pl.num_programs(0)
    right = lax.broadcasted_iota(jnp.int32, here_ref.shape, 1) >= R * OB
    there = jnp.where(right & (step == steps - 1), beyond_ref[...], there_ref[...])
    first = weight_ref.shape[0] + (step - steps) * QUAD
    blocks = blocks_of(fields_ref[...], here_ref[...], there, first, weight_ref, reading_ref)
    for spot, result in enumerate(updated(blocks)):
        result_ref[:, spot * span : (spot + 1) * span] = result


def in_stages(fields, positions, quad_position, root_weight, reading, devices):
    own_members, all_cells = fields.shape
    cells = all_cells // devices
    amount = cells // PARTITION_SPAN
    members = own_members * devices
    outer = devices // INNER
    quads = amount // QUAD
    width = QUAD * PARTITION_SPAN
    lanes = QUAD * OB
    early = quads // 2
    late = quads - early
    anywhere = pl.BlockSpec(memory_space=pl.ANY)
    vmem = pl.BlockSpec(memory_space=pltpu.VMEM)
    whole = jax.ShapeDtypeStruct((own_members, all_cells), jnp.float32)

    def call(kernel, inputs, outputs, grant=16, **options):
        return pl.pallas_call(
            kernel,
            out_shape=outputs,
            in_specs=inputs,
            compiler_params=pltpu.CompilerParams(vmem_limit_bytes=grant << 20),
            cost_estimate=pl.CostEstimate(flops=1, bytes_accessed=1, transcendentals=0),
            **options,
        )

    def columns(size, index):
        return pl.BlockSpec((members, size), lambda step: (0, index))

    def full(array):
        return pl.BlockSpec(array.shape, lambda step: (0, 0))

    def group(parts, size):
        return jax.ShapeDtypeStruct((members // parts, size), jnp.float32)

    def swapped(arrays, unit):
        pairs = [[(i, i ^ (unit * k)) for i in range(devices)] for k in range(len(arrays))]
        return [arrays[0]] + [lax.ppermute(arrays[k], "state", pairs[k]) for k in range(1, len(arrays))]

    def placed(parts, order, starts, result):
        options = dict(out_specs=anywhere, scratch_shapes=[pltpu.SemaphoreType.DMA((devices * len(starts),))])
        if result is None:
            kernel = functools.partial(place_kernel, order, cells, starts)
            return call(kernel, [vmem] * len(parts), whole, **options)(*parts)
        kernel = functools.partial(place_more_kernel, order, cells, starts)
        aliases = {len(parts): 0}
        return call(kernel, [vmem] * len(parts) + [anywhere], whole, input_output_aliases=aliases, **options)(
            *parts, result
        )

    def exchanged(array):
        return lax.all_to_all(array, "state", split_axis=0, concat_axis=0, tiled=True)

    sent = call(
        part_kernel,
        [anywhere, vmem],
        jax.ShapeDtypeStruct((devices, own_members, cells + lanes), jnp.float32),
        grant=56,
        out_specs=anywhere,
        scratch_shapes=[
            pltpu.VMEM((devices, own_members, cells + lanes), jnp.float32),
            pltpu.SemaphoreType.DMA((2 * devices,)),
        ],
    )(fields, positions.reshape(-1, lanes))
    fields = exchanged(sent).reshape(members, cells + lanes)
    terms = [root_weight, reading]
    seen = call(
        pick_kernel, [vmem, vmem], jax.ShapeDtypeStruct((members, quads * lanes), jnp.float32), out_specs=vmem
    )(fields, quad_position)

    sets = []
    for quad in range(early):
        groups = call(
            functools.partial(head_kernel, quad, devices),
            [
                columns(width, quad),
                columns(lanes, quad),
                columns(lanes, quad + 1),
                columns(lanes, cells // lanes),
                *[full(term) for term in terms],
            ],
            [group(outer, width)] * outer,
            grant=40,
            grid=(1,),
            out_specs=[pl.BlockSpec((members // outer, width), lambda step: (0, 0))] * outer,
        )(fields, seen, seen, fields, *terms)
        seen, groups = lax.optimization_barrier((seen, groups))
        sets.append(swapped(groups, INNER))

    ends = call(
        tail_kernel,
        [
            pl.BlockSpec((members, width), lambda step: (0, early + step)),
            pl.BlockSpec((members, lanes), lambda step: (0, early + step)),
            pl.BlockSpec((members, lanes), lambda step: (0, (early + step + 1) % quads)),
            columns(lanes, cells // lanes),
            *[full(term) for term in terms],
        ],
        jax.ShapeDtypeStruct((members, late * width), jnp.float32),
        grant=40,
        grid=(late,),
        out_specs=pl.BlockSpec((members, width), lambda step: (0, step)),
    )(fields, seen, seen, fields, *terms)
    ends, sets = lax.optimization_barrier((ends, sets))
    ends = exchanged(ends.reshape(devices, own_members, late * width)).reshape(members, late * width)

    near = call(
        functools.partial(turn_kernel, own_members, INNER),
        [vmem] * (outer * early),
        [group(INNER, early * width)] * INNER,
        out_specs=[vmem] * INNER,
    )(*[array for arrays in sets for array in arrays])
    order = [[far * INNER + close for far in range(outer)] for close in range(INNER)]
    result = placed(swapped(near, 1), order, [quad * width for quad in range(early)], None)
    return placed([ends], None, [quad * width for quad in range(early, quads)], result)


def by_all_to_all(fields, _, quad_position, root_weight, reading, devices):
    own_members, all_cells = fields.shape
    cells = all_cells // devices
    amount = cells // PARTITION_SPAN
    members = own_members * devices
    span = PARTITION_SPAN
    sent = fields.reshape(own_members, devices, cells).transpose(1, 0, 2)
    fields = lax.all_to_all(sent, "state", split_axis=0, concat_axis=0, tiled=True).reshape(members, cells)
    vmem = pl.BlockSpec(memory_space=pltpu.VMEM)
    own_seen = pl.pallas_call(
        pick_kernel,
        out_shape=jax.ShapeDtypeStruct((members, amount * OB), jnp.float32),
        in_specs=[vmem, vmem],
        out_specs=vmem,
        compiler_params=pltpu.CompilerParams(vmem_limit_bytes=16 << 20),
    )(fields, quad_position)
    edge = own_seen[:, : QUAD * OB]
    before = lax.ppermute(edge, "state", [(i, i + 1) for i in range(devices - 1)])
    after = lax.ppermute(edge, "state", [(i + 1, i) for i in range(devices - 1)])
    steps = amount // QUAD

    def whole(*shape):
        return pl.BlockSpec(shape, lambda step: (0, 0))

    analysis = pl.pallas_call(
        update_kernel,
        grid=(steps,),
        out_shape=jax.ShapeDtypeStruct((members, cells), jnp.float32),
        in_specs=[
            pl.BlockSpec((members, QUAD * span), lambda step: (0, step)),
            whole(members, QUAD * OB),
            whole(members, amount * OB),
            whole(members, QUAD * OB),
            whole(amount, 2 * QUAD * OB),
            whole(amount, 2 * QUAD * OB),
        ],
        out_specs=pl.BlockSpec((members, QUAD * span), lambda step: (0, step)),
        compiler_params=pltpu.CompilerParams(vmem_limit_bytes=40 << 20),
    )(fields, before, own_seen, after, root_weight, reading)
    result = lax.all_to_all(
        analysis.reshape(devices, own_members, cells), "state", split_axis=0, concat_axis=0, tiled=True
    )
    return result.transpose(1, 0, 2).reshape(own_members, all_cells)


def body(
    background_draws_table,
    measurement_reading,
    measurement_precision,
    sensed_point_position,
    measurement_tally,
    adjacent_tile_number,
):
    devices = lax.axis_size("state")
    root_weight, reading, quad_position = window_terms(
        measurement_reading,
        measurement_precision,
        sensed_point_position,
        measurement_tally,
        adjacent_tile_number,
        background_draws_table.shape[0] * devices,
    )
    way = in_stages if devices == INNER * INNER else by_all_to_all
    return way(background_draws_table, sensed_point_position, quad_position, root_weight, reading, devices)


def solution(mesh):
    return jax.shard_map(
        body,
        mesh=mesh,
        in_specs=(
            P("state", "groups"),
            P("groups", None),
            P("groups", None),
            P("groups", None),
            P("groups"),
            P(("groups", "state"), None),
        ),
        out_specs=P("state", "groups"),
        check_vma=False,
    )
```

```python
import functools

import jax
import jax.numpy as jnp
from jax import lax
from jax.experimental import pallas as pl
from jax.experimental.pallas import tpu as pltpu
from jax.sharding import PartitionSpec as P

PARTITION_SPAN = 128
OB = 32
R = 2
NS_ITERS = 5
LOC = 128

QUAD = PARTITION_SPAN // OB
INNER = 4
NN = (((1,), (0,)), ((), ()))
NT = (((1,), (1,)), ((), ()))


def halves(values):
    high = values.astype(jnp.bfloat16)
    return high, (values - high.astype(jnp.float32)).astype(jnp.bfloat16)


def times(left, right, dims):
    (left_high, left_low), (right_high, right_low) = left, right
    return lax.dot_general(
        jnp.concatenate([left_high, left_high, left_low], axis=1),
        jnp.concatenate([right_high, right_low, right_high], axis=dims[0][1][0]),
        dims,
        preferred_element_type=jnp.float32,
    )


def updated(blocks):
    turns = [analysis(*block) for block in blocks]
    results = [None] * len(turns)
    while None in results:
        for index, turn in enumerate(turns):
            if results[index] is None:
                results[index] = next(turn)
    return results


def analysis(fields, seen, root_weight, reading):
    seen_mean = jnp.mean(seen, axis=0, keepdims=True)
    pull = (reading - seen_mean) * root_weight
    root = halves((seen - seen_mean) * root_weight)
    spread = times(root, root, NT)
    pull = times(halves(jnp.broadcast_to(pull, (16, pull.shape[1]))), root, NT)
    yield None
    squares = jnp.sum(jnp.sum(spread * spread, axis=0, keepdims=True), axis=1, keepdims=True)
    norm_size = 1.0 + jnp.sqrt(squares)
    unit = 1.0 / norm_size
    rest = spread * (-0.5 * unit)
    cells = fields.T
    centre = jnp.mean(cells, axis=1, keepdims=True)
    chain = jnp.concatenate([cells - centre, pull], axis=0)
    for sweep in range(NS_ITERS - 1):
        parts = halves(rest)
        gain = 1.5 - 0.5 * unit
        if sweep < NS_ITERS - 2:
            square = times(parts, parts, NN)
        moved = times(halves(chain), parts, NN)
        yield None
        if sweep < NS_ITERS - 2:
            once = (gain - 0.5 * unit) * rest + square
            cubic = times(halves(once), parts, NN)
        chain = gain * chain + moved
        if sweep < NS_ITERS - 2:
            yield None
            rest = gain * once - (0.5 * unit * gain) * rest + cubic
            unit = unit * gain * gain
    moved = times(halves(chain), parts, NN)
    yield None
    end = (-0.5 * unit) * chain + moved
    for _ in range(2):
        moved = times(halves(end), parts, NN)
        yield None
        end = gain * end + moved
    chain = (1.5 * chain + end) * lax.rsqrt(norm_size)
    moved = chain[:PARTITION_SPAN]
    shift = jnp.sum(moved * chain[PARTITION_SPAN : PARTITION_SPAN + 1], axis=1, keepdims=True)
    yield (moved + (centre + shift)).T


def picked(fields, position):
    members = fields[0].shape[0]
    span = PARTITION_SPAN
    index = jnp.broadcast_to(position, (members, span))
    lanes = lax.broadcasted_iota(jnp.int32, (members, span), 1)
    total = None
    for spot, field in enumerate(fields):
        found = jnp.take_along_axis(field, index, axis=1)
        total = found if spot == 0 else jnp.where(lanes // OB == spot, found, total)
    return total


def pick_kernel(fields_ref, position_ref, seen_ref):
    span = PARTITION_SPAN
    quads = position_ref.shape[0]
    amount = quads * QUAD
    for quad in range(quads):
        blocks = [(quad * QUAD + spot - R) % amount for spot in range(QUAD)]
        fields = [fields_ref[:, block * span : (block + 1) * span] for block in blocks]
        seen_ref[:, quad * span : (quad + 1) * span] = picked(fields, position_ref[quad : quad + 1, :])


def pick_first_kernel(fields_ref, position_ref, seen_ref):
    span = PARTITION_SPAN
    amount = fields_ref.shape[1] // span - 1
    beyond = fields_ref[:, amount * span :]
    low = lax.broadcasted_iota(jnp.int32, beyond.shape, 1) < R * OB
    for quad in range(seen_ref.shape[1] // span):
        blocks = [max(quad * QUAD + spot - R, 0) for spot in range(QUAD)]
        fields = [fields_ref[:, block * span : (block + 1) * span] for block in blocks]
        found = picked(fields, position_ref[quad : quad + 1, :])
        seen_ref[:, quad * span : (quad + 1) * span] = found if quad else jnp.where(low, beyond, found)


def pick_second_kernel(fields_ref, beyond_ref, position_ref, seen_ref):
    span = PARTITION_SPAN
    quads = position_ref.shape[0]
    amount = fields_ref.shape[1] // span
    low = lax.broadcasted_iota(jnp.int32, beyond_ref.shape, 1) < R * OB
    for index in range(seen_ref.shape[1] // span):
        blocks = [min(index * QUAD + spot, amount - 1) for spot in range(QUAD)]
        fields = [fields_ref[:, block * span : (block + 1) * span] for block in blocks]
        quad = (quads - seen_ref.shape[1] // span + 1 + index) % quads
        found = picked(fields, position_ref[quad : quad + 1, :])
        seen_ref[:, index * span : (index + 1) * span] = found if quad else jnp.where(low, found, beyond_ref[...])


def update_kernel(fields_ref, before_ref, own_ref, after_ref, weight_ref, reading_ref, result_ref):
    members, span = before_ref.shape
    step = pl.program_id(0)
    steps = pl.num_programs(0)
    lanes = lax.broadcasted_iota(jnp.int32, (members, span), 1)
    here = own_ref[:, pl.ds(pl.multiple_of(step * span, span), span)]
    following = own_ref[:, pl.ds(pl.multiple_of(lax.rem(step + 1, steps) * span, span), span)]
    first = jnp.where((step == 0) & (lanes < R * OB), before_ref[...], here)
    second = jnp.where((step == steps - 1) & (lanes >= R * OB), after_ref[...], following)
    seen = jnp.concatenate([first, second], axis=1)
    blocks = [
        (
            fields_ref[:, spot * span : (spot + 1) * span],
            seen,
            weight_ref[pl.ds(step * QUAD + spot, 1), :],
            reading_ref[pl.ds(step * QUAD + spot, 1), :],
        )
        for spot in range(QUAD)
    ]
    for spot, result in enumerate(updated(blocks)):
        result_ref[:, spot * span : (spot + 1) * span] = result


def terms_kernel(
    amount, members, reading_ref, precision_ref, position_ref, tally_ref, adjacent_ref, weight_ref, shown_ref, quad_ref
):
    first_block = lax.axis_index("state") * amount
    total = tally_ref.shape[0]
    quads = amount // QUAD
    span = PARTITION_SPAN
    lane = lax.broadcasted_iota(jnp.int32, (1, span), 1)
    low = lane < R * OB

    def tile(ref, quad):
        row = first_block // QUAD + quad
        before = ref[pl.ds(jnp.maximum(row - 1, 0), 1), :]
        after = ref[pl.ds(jnp.minimum(row, total // QUAD - 1), 1), :]
        return pltpu.roll(jnp.where(low, after, before), R * OB, 1)

    def counts(quad):
        found = jnp.zeros((1, span), jnp.int32)
        for spot in range(QUAD):
            block = jnp.clip(first_block + quad * QUAD + spot - R, 0, total - 1)
            found = jnp.where(lane // OB == spot, tally_ref[block], found)
        return found

    def pair(tiles, quad):
        return jnp.concatenate(tiles[quad : quad + 2], axis=1)

    positions = [tile(position_ref, quad) for quad in range(quads + 1)]
    readings = [tile(reading_ref, quad) for quad in range(quads + 1)]
    precisions = [tile(precision_ref, quad) for quad in range(quads + 1)]
    tallies = [counts(quad) for quad in range(quads + 1)]
    wide = lax.broadcasted_iota(jnp.int32, (1, 2 * span), 1)
    for block in range(amount):
        quad, spot = divmod(block, QUAD)
        neighbour = wide // OB - spot
        usable = jnp.zeros((1, 2 * span), jnp.float32)
        for j in range(2 * R + 1):
            there = jnp.where(adjacent_ref[block, j] >= 0, 1.0, 0.0)
            usable = jnp.where(neighbour == j, there, usable)
        distance = (
            ((neighbour - R) * span).astype(jnp.float32)
            + pair(positions, quad).astype(jnp.float32)
            - 0.5 * (span - 1)
        )
        decay = jnp.exp(-0.5 * (distance / LOC) ** 2)
        active = jnp.where(wide % OB < pair(tallies, quad), usable, 0.0)
        weight = pair(precisions, quad) * decay * active
        weight_ref[block : block + 1, :] = jnp.sqrt(weight / (members - 1.0))
        shown_ref[block : block + 1, :] = pair(readings, quad)
    edge = jnp.where(low, positions[quads], positions[0])
    for quad in range(quads):
        quad_ref[quad : quad + 1, :] = positions[quad] if quad else edge


def window_terms(reading, precision, position, tally, adjacent, members):
    amount = adjacent.shape[0]
    lanes = QUAD * OB
    vmem = pl.BlockSpec(memory_space=pltpu.VMEM)
    smem = pl.BlockSpec(memory_space=pltpu.SMEM)
    terms = jax.ShapeDtypeStruct((amount, 2 * lanes), jnp.float32)
    return pl.pallas_call(
        functools.partial(terms_kernel, amount, members),
        out_shape=[terms, terms, jax.ShapeDtypeStruct((amount // QUAD, lanes), jnp.int32)],
        in_specs=[vmem, vmem, vmem, smem, smem],
        out_specs=[vmem, vmem, vmem],
    )(*(array.reshape(-1, lanes) for array in (reading, precision, position)), tally, adjacent)


def copied(copies):
    for copy in copies:
        copy.start()
    return copies


def into_held(fields_ref, held_ref, sems, start, size):
    devices = held_ref.shape[0]
    cells = fields_ref.shape[1] // devices
    sources = [fields_ref.at[:, pl.ds(device * cells + start, size)] for device in range(devices)]
    targets = [held_ref.at[device, :, pl.ds(0, size)] for device in range(devices)]
    return copied([pltpu.make_async_copy(*pair, sems.at[index]) for index, pair in enumerate(zip(sources, targets))])


def first_part_kernel(split, fields_ref, position_ref, sent_ref, held_ref, sems):
    devices, rows, _ = sent_ref.shape
    cells = fields_ref.shape[1] // devices
    span = PARTITION_SPAN
    amount = cells // span
    into = into_held(fields_ref, held_ref, sems, 0, cells)

    def out(number, some, start, size, to):
        source = held_ref.at[some, :, pl.ds(start, size)]
        target = sent_ref.at[some, :, pl.ds(to, size)]
        return copied([pltpu.make_async_copy(source, target, sems.at[devices + number])])

    away = []
    for device, copy in enumerate(into):
        copy.wait()
        if device % INNER == INNER - 1:
            away += out(len(away), pl.ds(device + 1 - INNER, INNER), 0, split, 0)

    def shifted(array, distance):
        if distance > 0:
            return jnp.concatenate([array[:distance], array[:-distance]], axis=0)
        return jnp.concatenate([array[-distance:], array[distance:]], axis=0)

    beyond = [(amount - R + spot, 1) for spot in range(R)] + [(spot, -1) for spot in range(R)]
    positions = position_ref[...].T.reshape(devices, amount, OB)
    position = jnp.concatenate([shifted(positions[:, block], distance) for block, distance in beyond], axis=1)
    position = jnp.broadcast_to(position[:, None], (devices, rows, span)).reshape(devices * rows, span)
    fields = [
        shifted(held_ref[:, :, block * span : (block + 1) * span].reshape(devices * rows, span), distance * rows)
        for block, distance in beyond
    ]
    held_ref[:, :, cells : cells + span] = picked(fields, position).reshape(devices, rows, span)
    away += out(len(away), pl.ds(0, devices), cells, span, split)
    for copy in away:
        copy.wait()


def second_part_kernel(split, fields_ref, sent_ref, held_ref, sems):
    devices, _, size = sent_ref.shape
    for copy in into_held(fields_ref, held_ref, sems, split, size):
        copy.wait()
    for copy in copied([pltpu.make_async_copy(held_ref, sent_ref, sems.at[devices])]):
        copy.wait()


def turn_kernel(rows, parts, *refs):
    given, made = refs[:-parts], refs[-parts:]
    width = given[0].shape[1]
    many = made[0].shape[0] // rows
    for number, source in enumerate(given):
        side, i = divmod(number, many)
        for j, target in enumerate(made):
            target[i * rows : (i + 1) * rows, side * width : (side + 1) * width] = source[j * rows : (j + 1) * rows, :]


def place_kernel(distances, cells, start, *refs):
    *parts, result_ref, sems = refs
    place = lax.axis_index("state")
    rows = result_ref.shape[0]
    width = parts[0].shape[1]
    started = []
    for i, part in enumerate(parts):
        for j in range(part.shape[0] // rows):
            device = place ^ distances[i][j] if distances else j
            source = part.at[pl.ds(j * rows, rows), :]
            target = result_ref.at[:, pl.ds(pl.multiple_of(device * cells + start, width), width)]
            started.append(pltpu.make_async_copy(source, target, sems.at[len(started)]))
            started[-1].start()
    for copy in started:
        copy.wait()


def place_more_kernel(distances, cells, start, *refs):
    *parts, _, result_ref, sems = refs
    place_kernel(distances, cells, start, *parts, result_ref, sems)


def reordered(ref, devices):
    place = lax.axis_index("state")
    rows = ref.shape[0] // devices
    starts = [pl.multiple_of((place ^ distance) * rows, rows) for distance in range(devices)]
    return jnp.concatenate([ref[pl.ds(start, rows), :] for start in starts], axis=0)


def blocks_of(fields, here, there, first, weight_ref, reading_ref):
    span = PARTITION_SPAN
    seen = jnp.concatenate([here, there], axis=1)
    blocks = []
    for spot in range(QUAD):
        terms = [ref[pl.ds(first + spot, 1), :] for ref in (weight_ref, reading_ref)]
        blocks.append((fields[:, spot * span : (spot + 1) * span], seen, *terms))
    return blocks


def head_kernel(quad, devices, fields_ref, here_ref, there_ref, weight_ref, reading_ref, *results):
    span = PARTITION_SPAN
    fields, here, there = [reordered(ref, devices) for ref in (fields_ref, here_ref, there_ref)]
    for spot, result in enumerate(updated(blocks_of(fields, here, there, quad * QUAD, weight_ref, reading_ref))):
        start = 0
        for result_ref in results:
            rows = result_ref.shape[0]
            result_ref[:, spot * span : (spot + 1) * span] = result[start : start + rows]
            start += rows


def tail_kernel(first_ref, begin_ref, end_ref, here_ref, tiles_ref, weight_ref, reading_ref, result_ref):
    span = PARTITION_SPAN
    step = pl.program_id(0)
    begin = jnp.where(step == 0, first_ref[...], begin_ref[...])
    fields = jnp.concatenate([begin, end_ref[...]], axis=1)
    here = jnp.where(step == 0, here_ref[...], tiles_ref[:, :span])
    there = jnp.where(step == 0, tiles_ref[:, :span], tiles_ref[:, span:])
    first = weight_ref.shape[0] + (step - 2) * QUAD
    for spot, result in enumerate(updated(blocks_of(fields, here, there, first, weight_ref, reading_ref))):
        result_ref[:, spot * span : (spot + 1) * span] = result


def in_stages(fields, positions, quad_position, root_weight, reading, devices):
    own_members, all_cells = fields.shape
    cells = all_cells // devices
    amount = cells // PARTITION_SPAN
    members = own_members * devices
    outer = devices // INNER
    quads = amount // QUAD
    width = QUAD * PARTITION_SPAN
    lanes = QUAD * OB
    early = quads - 2
    late = 2
    half = R * PARTITION_SPAN
    anywhere = pl.BlockSpec(memory_space=pl.ANY)
    vmem = pl.BlockSpec(memory_space=pltpu.VMEM)
    whole = jax.ShapeDtypeStruct((own_members, all_cells), jnp.float32)

    def call(kernel, inputs, outputs, grant=16, cost=1, **options):
        return pl.pallas_call(
            kernel,
            out_shape=outputs,
            in_specs=inputs,
            compiler_params=pltpu.CompilerParams(vmem_limit_bytes=grant << 20),
            cost_estimate=pl.CostEstimate(flops=cost, bytes_accessed=1, transcendentals=0),
            **options,
        )

    def columns(size, index):
        return pl.BlockSpec((members, size), lambda step: (0, index))

    def full(array):
        return pl.BlockSpec(array.shape, lambda step: (0, 0))

    def group(parts, size):
        return jax.ShapeDtypeStruct((members // parts, size), jnp.float32)

    def swapped(arrays, unit):
        pairs = [[(i, i ^ (unit * k)) for i in range(devices)] for k in range(len(arrays))]
        return [arrays[0]] + [lax.ppermute(arrays[k], "state", pairs[k]) for k in range(1, len(arrays))]

    def placed(parts, order, start, result):
        options = dict(out_specs=anywhere, scratch_shapes=[pltpu.SemaphoreType.DMA((devices,))])
        if result is None:
            kernel = functools.partial(place_kernel, order, cells, start)
            return call(kernel, [vmem] * len(parts), whole, **options)(*parts)
        kernel = functools.partial(place_more_kernel, order, cells, start)
        aliases = {len(parts): 0}
        return call(kernel, [vmem] * len(parts) + [anywhere], whole, input_output_aliases=aliases, **options)(
            *parts, result
        )

    def exchanged(array):
        return lax.all_to_all(array, "state", split_axis=0, concat_axis=0, tiled=True)

    split = early * width + half
    def part(kernel, arguments, size, held):
        return call(
            functools.partial(kernel, split),
            [anywhere] + [vmem] * (len(arguments) - 1),
            jax.ShapeDtypeStruct((devices, own_members, size), jnp.float32),
            grant=56,
            out_specs=anywhere,
            scratch_shapes=[
                pltpu.VMEM((devices, own_members, held), jnp.float32),
                pltpu.SemaphoreType.DMA((2 * devices,)),
            ],
        )(*arguments)

    first = part(first_part_kernel, [fields, positions.T], split + lanes, cells + lanes)
    second = part(second_part_kernel, [fields], cells - split, cells - split)
    first = exchanged(first).reshape(members, split + lanes)
    first, second, quad_position, root_weight, reading = lax.optimization_barrier(
        (first, second, quad_position, root_weight, reading)
    )
    second = exchanged(second).reshape(members, cells - split)
    terms = [root_weight, reading]
    seen = call(
        pick_first_kernel,
        [vmem, vmem],
        jax.ShapeDtypeStruct((members, (early + 1) * lanes), jnp.float32),
        out_specs=vmem,
    )(first, quad_position)

    sets = []
    for quad in range(early):
        groups = call(
            functools.partial(head_kernel, quad, devices),
            [columns(width, quad), columns(lanes, quad), columns(lanes, quad + 1), *[full(term) for term in terms]],
            [group(outer, width)] * outer,
            grant=40,
            grid=(1,),
            out_specs=[pl.BlockSpec((members // outer, width), lambda step: (0, 0))] * outer,
        )(first, seen, seen, *terms)
        if quad + 1 < early:
            seen, groups = lax.optimization_barrier((seen, groups))
        else:
            _, second = lax.optimization_barrier((groups, second))
        sets.append(swapped(groups, INNER))

    tiles = call(
        pick_second_kernel,
        [full(second), columns(lanes, split // lanes), full(quad_position)],
        jax.ShapeDtypeStruct((members, 2 * lanes), jnp.float32),
        grid=(1,),
        out_specs=columns(2 * lanes, 0),
    )(second, first, quad_position)
    ends = call(
        tail_kernel,
        [
            columns(half, split // half - 1),
            columns(half, 1),
            pl.BlockSpec((members, half), lambda step: (0, 2 * step)),
            columns(lanes, early),
            full(tiles),
            *[full(term) for term in terms],
        ],
        jax.ShapeDtypeStruct((members, late * width), jnp.float32),
        grant=40,
        grid=(late,),
        out_specs=pl.BlockSpec((members, width), lambda step: (0, step)),
    )(first, second, second, seen, tiles, *terms)
    ends = exchanged(ends.reshape(devices, own_members, late * width)).reshape(members, late * width)

    near = call(
        functools.partial(turn_kernel, own_members, INNER),
        [vmem] * (outer * early),
        [group(INNER, early * width)] * INNER,
        cost=1 << 36,
        out_specs=[vmem] * INNER,
    )(*[array for arrays in sets for array in arrays])
    order = [[far * INNER + close for far in range(outer)] for close in range(INNER)]
    result = placed([ends], None, early * width, None)
    return placed(swapped(near, 1), order, 0, result)


def by_all_to_all(fields, _, quad_position, root_weight, reading, devices):
    own_members, all_cells = fields.shape
    cells = all_cells // devices
    amount = cells // PARTITION_SPAN
    members = own_members * devices
    span = PARTITION_SPAN
    sent = fields.reshape(own_members, devices, cells).transpose(1, 0, 2)
    fields = lax.all_to_all(sent, "state", split_axis=0, concat_axis=0, tiled=True).reshape(members, cells)
    vmem = pl.BlockSpec(memory_space=pltpu.VMEM)
    own_seen = pl.pallas_call(
        pick_kernel,
        out_shape=jax.ShapeDtypeStruct((members, amount * OB), jnp.float32),
        in_specs=[vmem, vmem],
        out_specs=vmem,
        compiler_params=pltpu.CompilerParams(vmem_limit_bytes=16 << 20),
    )(fields, quad_position)
    edge = own_seen[:, : QUAD * OB]
    before = lax.ppermute(edge, "state", [(i, i + 1) for i in range(devices - 1)])
    after = lax.ppermute(edge, "state", [(i + 1, i) for i in range(devices - 1)])
    steps = amount // QUAD

    def whole(*shape):
        return pl.BlockSpec(shape, lambda step: (0, 0))

    analysis = pl.pallas_call(
        update_kernel,
        grid=(steps,),
        out_shape=jax.ShapeDtypeStruct((members, cells), jnp.float32),
        in_specs=[
            pl.BlockSpec((members, QUAD * span), lambda step: (0, step)),
            whole(members, QUAD * OB),
            whole(members, amount * OB),
            whole(members, QUAD * OB),
            whole(amount, 2 * QUAD * OB),
            whole(amount, 2 * QUAD * OB),
        ],
        out_specs=pl.BlockSpec((members, QUAD * span), lambda step: (0, step)),
        compiler_params=pltpu.CompilerParams(vmem_limit_bytes=40 << 20),
    )(fields, before, own_seen, after, root_weight, reading)
    result = lax.all_to_all(
        analysis.reshape(devices, own_members, cells), "state", split_axis=0, concat_axis=0, tiled=True
    )
    return result.transpose(1, 0, 2).reshape(own_members, all_cells)


def body(
    background_draws_table,
    measurement_reading,
    measurement_precision,
    sensed_point_position,
    measurement_tally,
    adjacent_tile_number,
):
    devices = lax.axis_size("state")
    root_weight, reading, quad_position = window_terms(
        measurement_reading,
        measurement_precision,
        sensed_point_position,
        measurement_tally,
        adjacent_tile_number,
        background_draws_table.shape[0] * devices,
    )
    way = in_stages if devices == INNER * INNER else by_all_to_all
    return way(background_draws_table, sensed_point_position, quad_position, root_weight, reading, devices)


def solution(mesh):
    return jax.shard_map(
        body,
        mesh=mesh,
        in_specs=(
            P("state", "groups"),
            P("groups", None),
            P("groups", None),
            P("groups", None),
            P("groups"),
            P(("groups", "state"), None),
        ),
        out_specs=P("state", "groups"),
        check_vma=False,
    )
```

```python
import functools

import jax
import jax.numpy as jnp
from jax import lax
from jax.experimental import pallas as pl
from jax.experimental.pallas import tpu as pltpu
from jax.sharding import PartitionSpec as P

PARTITION_SPAN = 128
OB = 32
R = 2
NS_ITERS = 5
LOC = 128

QUAD = PARTITION_SPAN // OB
INNER = 4
NN = (((1,), (0,)), ((), ()))
NT = (((1,), (1,)), ((), ()))


def halves(values):
    high = values.astype(jnp.bfloat16)
    return high, (values - high.astype(jnp.float32)).astype(jnp.bfloat16)


def times(left, right, dims):
    (left_high, left_low), (right_high, right_low) = left, right
    return lax.dot_general(
        jnp.concatenate([left_high, left_high, left_low], axis=1),
        jnp.concatenate([right_high, right_low, right_high], axis=dims[0][1][0]),
        dims,
        preferred_element_type=jnp.float32,
    )


def updated(blocks):
    turns = [analysis(*block) for block in blocks]
    results = [None] * len(turns)
    while None in results:
        for index, turn in enumerate(turns):
            if results[index] is None:
                results[index] = next(turn)
    return results


def analysis(fields, seen, root_weight, reading):
    seen_mean = jnp.mean(seen, axis=0, keepdims=True)
    pull = (reading - seen_mean) * root_weight
    root = halves((seen - seen_mean) * root_weight)
    spread = times(root, root, NT)
    pull = times(halves(jnp.broadcast_to(pull, (16, pull.shape[1]))), root, NT)
    yield None
    squares = jnp.sum(jnp.sum(spread * spread, axis=0, keepdims=True), axis=1, keepdims=True)
    norm_size = 1.0 + jnp.sqrt(squares)
    unit = 1.0 / norm_size
    rest = spread * (-0.5 * unit)
    cells = fields.T
    centre = jnp.mean(cells, axis=1, keepdims=True)
    chain = jnp.concatenate([cells - centre, pull], axis=0)
    for sweep in range(NS_ITERS - 1):
        parts = halves(rest)
        gain = 1.5 - 0.5 * unit
        if sweep < NS_ITERS - 2:
            square = times(parts, parts, NN)
        moved = times(halves(chain), parts, NN)
        yield None
        if sweep < NS_ITERS - 2:
            once = (gain - 0.5 * unit) * rest + square
            cubic = times(halves(once), parts, NN)
        chain = gain * chain + moved
        if sweep < NS_ITERS - 2:
            yield None
            rest = gain * once - (0.5 * unit * gain) * rest + cubic
            unit = unit * gain * gain
    moved = times(halves(chain), parts, NN)
    yield None
    end = (-0.5 * unit) * chain + moved
    for _ in range(2):
        moved = times(halves(end), parts, NN)
        yield None
        end = gain * end + moved
    chain = (1.5 * chain + end) * lax.rsqrt(norm_size)
    moved = chain[:PARTITION_SPAN]
    shift = jnp.sum(moved * chain[PARTITION_SPAN : PARTITION_SPAN + 1], axis=1, keepdims=True)
    yield (moved + (centre + shift)).T


def picked(fields, position):
    members = fields[0].shape[0]
    span = PARTITION_SPAN
    index = jnp.broadcast_to(position, (members, span))
    lanes = lax.broadcasted_iota(jnp.int32, (members, span), 1)
    total = None
    for spot, field in enumerate(fields):
        found = jnp.take_along_axis(field, index, axis=1)
        total = found if spot == 0 else jnp.where(lanes // OB == spot, found, total)
    return total


def pick_kernel(fields_ref, position_ref, seen_ref):
    span = PARTITION_SPAN
    quads = position_ref.shape[0]
    amount = quads * QUAD
    for quad in range(quads):
        blocks = [(quad * QUAD + spot - R) % amount for spot in range(QUAD)]
        fields = [fields_ref[:, block * span : (block + 1) * span] for block in blocks]
        seen_ref[:, quad * span : (quad + 1) * span] = picked(fields, position_ref[quad : quad + 1, :])


def pick_first_kernel(fields_ref, position_ref, seen_ref):
    span = PARTITION_SPAN
    amount = fields_ref.shape[1] // span - 1
    beyond = fields_ref[:, amount * span :]
    low = lax.broadcasted_iota(jnp.int32, beyond.shape, 1) < R * OB
    for quad in range(seen_ref.shape[1] // span):
        blocks = [max(quad * QUAD + spot - R, 0) for spot in range(QUAD)]
        fields = [fields_ref[:, block * span : (block + 1) * span] for block in blocks]
        found = picked(fields, position_ref[quad : quad + 1, :])
        seen_ref[:, quad * span : (quad + 1) * span] = found if quad else jnp.where(low, beyond, found)


def second_kernel(devices, beyond_ref, position_ref, *refs):
    *parts, fields_ref, seen_ref = refs
    place = lax.axis_index("state")
    span = PARTITION_SPAN
    quads = position_ref.shape[0]
    rows = fields_ref.shape[0] // devices
    for distance in range(devices):
        far, near = divmod(distance, INNER)
        start = pl.multiple_of((place ^ distance) * rows, rows)
        fields_ref[pl.ds(start, rows), :] = parts[far][near * rows : (near + 1) * rows, :]
    amount = fields_ref.shape[1] // span
    low = lax.broadcasted_iota(jnp.int32, beyond_ref.shape, 1) < R * OB
    for index in range(seen_ref.shape[1] // span):
        blocks = [min(index * QUAD + spot, amount - 1) for spot in range(QUAD)]
        fields = [fields_ref[:, block * span : (block + 1) * span] for block in blocks]
        quad = (quads - seen_ref.shape[1] // span + 1 + index) % quads
        found = picked(fields, position_ref[quad : quad + 1, :])
        seen_ref[:, index * span : (index + 1) * span] = found if quad else jnp.where(low, found, beyond_ref[...])


def update_kernel(fields_ref, before_ref, own_ref, after_ref, weight_ref, reading_ref, result_ref):
    members, span = before_ref.shape
    step = pl.program_id(0)
    steps = pl.num_programs(0)
    lanes = lax.broadcasted_iota(jnp.int32, (members, span), 1)
    here = own_ref[:, pl.ds(pl.multiple_of(step * span, span), span)]
    following = own_ref[:, pl.ds(pl.multiple_of(lax.rem(step + 1, steps) * span, span), span)]
    first = jnp.where((step == 0) & (lanes < R * OB), before_ref[...], here)
    second = jnp.where((step == steps - 1) & (lanes >= R * OB), after_ref[...], following)
    seen = jnp.concatenate([first, second], axis=1)
    blocks = [
        (
            fields_ref[:, spot * span : (spot + 1) * span],
            seen,
            weight_ref[pl.ds(step * QUAD + spot, 1), :],
            reading_ref[pl.ds(step * QUAD + spot, 1), :],
        )
        for spot in range(QUAD)
    ]
    for spot, result in enumerate(updated(blocks)):
        result_ref[:, spot * span : (spot + 1) * span] = result


def terms_kernel(
    amount, members, reading_ref, precision_ref, position_ref, tally_ref, adjacent_ref, weight_ref, shown_ref, quad_ref
):
    first_block = lax.axis_index("state") * amount
    total = tally_ref.shape[0]
    quads = amount // QUAD
    span = PARTITION_SPAN
    lane = lax.broadcasted_iota(jnp.int32, (1, span), 1)
    low = lane < R * OB

    def tile(ref, quad):
        row = first_block // QUAD + quad
        before = ref[pl.ds(jnp.maximum(row - 1, 0), 1), :]
        after = ref[pl.ds(jnp.minimum(row, total // QUAD - 1), 1), :]
        return pltpu.roll(jnp.where(low, after, before), R * OB, 1)

    def counts(quad):
        found = jnp.zeros((1, span), jnp.int32)
        for spot in range(QUAD):
            block = jnp.clip(first_block + quad * QUAD + spot - R, 0, total - 1)
            found = jnp.where(lane // OB == spot, tally_ref[block], found)
        return found

    def pair(tiles, quad):
        return jnp.concatenate(tiles[quad : quad + 2], axis=1)

    positions = [tile(position_ref, quad) for quad in range(quads + 1)]
    readings = [tile(reading_ref, quad) for quad in range(quads + 1)]
    precisions = [tile(precision_ref, quad) for quad in range(quads + 1)]
    tallies = [counts(quad) for quad in range(quads + 1)]
    wide = lax.broadcasted_iota(jnp.int32, (1, 2 * span), 1)
    for block in range(amount):
        quad, spot = divmod(block, QUAD)
        neighbour = wide // OB - spot
        usable = jnp.zeros((1, 2 * span), jnp.float32)
        for j in range(2 * R + 1):
            there = jnp.where(adjacent_ref[block, j] >= 0, 1.0, 0.0)
            usable = jnp.where(neighbour == j, there, usable)
        distance = (
            ((neighbour - R) * span).astype(jnp.float32)
            + pair(positions, quad).astype(jnp.float32)
            - 0.5 * (span - 1)
        )
        decay = jnp.exp(-0.5 * (distance / LOC) ** 2)
        active = jnp.where(wide % OB < pair(tallies, quad), usable, 0.0)
        weight = pair(precisions, quad) * decay * active
        weight_ref[block : block + 1, :] = jnp.sqrt(weight / (members - 1.0))
        shown_ref[block : block + 1, :] = pair(readings, quad)
    edge = jnp.where(low, positions[quads], positions[0])
    for quad in range(quads):
        quad_ref[quad : quad + 1, :] = positions[quad] if quad else edge


def window_terms(reading, precision, position, tally, adjacent, members):
    amount = adjacent.shape[0]
    lanes = QUAD * OB
    vmem = pl.BlockSpec(memory_space=pltpu.VMEM)
    smem = pl.BlockSpec(memory_space=pltpu.SMEM)
    terms = jax.ShapeDtypeStruct((amount, 2 * lanes), jnp.float32)
    return pl.pallas_call(
        functools.partial(terms_kernel, amount, members),
        out_shape=[terms, terms, jax.ShapeDtypeStruct((amount // QUAD, lanes), jnp.int32)],
        in_specs=[vmem, vmem, vmem, smem, smem],
        out_specs=[vmem, vmem, vmem],
    )(*(array.reshape(-1, lanes) for array in (reading, precision, position)), tally, adjacent)


def copied(copies):
    for copy in copies:
        copy.start()
    return copies


def into_held(fields_ref, held_ref, sems, start, size):
    devices = held_ref.shape[0]
    cells = fields_ref.shape[1] // devices
    sources = [fields_ref.at[:, pl.ds(device * cells + start, size)] for device in range(devices)]
    targets = [held_ref.at[device, :, pl.ds(0, size)] for device in range(devices)]
    return copied([pltpu.make_async_copy(*pair, sems.at[index]) for index, pair in enumerate(zip(sources, targets))])


def first_part_kernel(split, fields_ref, position_ref, sent_ref, held_ref, sems):
    devices, rows, _ = sent_ref.shape
    cells = fields_ref.shape[1] // devices
    span = PARTITION_SPAN
    amount = cells // span
    into = into_held(fields_ref, held_ref, sems, 0, cells)

    def out(number, some, start, size, to):
        source = held_ref.at[some, :, pl.ds(start, size)]
        target = sent_ref.at[some, :, pl.ds(to, size)]
        return copied([pltpu.make_async_copy(source, target, sems.at[devices + number])])

    away = []
    for device, copy in enumerate(into):
        copy.wait()
        if device % INNER == INNER - 1:
            away += out(len(away), pl.ds(device + 1 - INNER, INNER), 0, split, 0)

    def shifted(array, distance):
        if distance > 0:
            return jnp.concatenate([array[:distance], array[:-distance]], axis=0)
        return jnp.concatenate([array[-distance:], array[distance:]], axis=0)

    beyond = [(amount - R + spot, 1) for spot in range(R)] + [(spot, -1) for spot in range(R)]
    positions = position_ref[...].T.reshape(devices, amount, OB)
    position = jnp.concatenate([shifted(positions[:, block], distance) for block, distance in beyond], axis=1)
    position = jnp.broadcast_to(position[:, None], (devices, rows, span)).reshape(devices * rows, span)
    fields = [
        shifted(held_ref[:, :, block * span : (block + 1) * span].reshape(devices * rows, span), distance * rows)
        for block, distance in beyond
    ]
    held_ref[:, :, cells : cells + span] = picked(fields, position).reshape(devices, rows, span)
    away += out(len(away), pl.ds(0, devices), cells, span, split)
    for copy in away:
        copy.wait()


def second_part_kernel(split, fields_ref, *refs):
    *sent, sems = refs
    place = lax.axis_index("state")
    rows = fields_ref.shape[0]
    size = sent[0].shape[1]
    cells = split + size
    copies = []
    for near, array in enumerate(sent):
        for far in range(array.shape[0] // rows):
            start = (place ^ (far * INNER + near)) * cells + split
            source = fields_ref.at[:, pl.ds(pl.multiple_of(start, PARTITION_SPAN), size)]
            target = array.at[pl.ds(far * rows, rows), :]
            copies.append(pltpu.make_async_copy(source, target, sems.at[len(copies)]))
    for copy in copied(copies):
        copy.wait()


def turn_kernel(rows, *refs):
    given, made = refs[: len(refs) // 2], refs[len(refs) // 2 :]
    for i, source in enumerate(given):
        for j, target in enumerate(made):
            target[i * rows : (i + 1) * rows, :] = source[j * rows : (j + 1) * rows, :]


def place_kernel(cells, *refs):
    *parts, last_ref, result_ref, sems = refs
    place = lax.axis_index("state")
    rows = result_ref.shape[0]
    moves = []
    for near, part in enumerate(parts):
        width = part.shape[1]
        for far in range(part.shape[0] // rows):
            start = (place ^ (far * INNER + near)) * cells
            target = result_ref.at[:, pl.ds(pl.multiple_of(start, width), width)]
            moves.append((part.at[pl.ds(far * rows, rows), :], target))
    for device in range(last_ref.shape[0] // rows):
        size = last_ref.shape[1]
        target = result_ref.at[:, pl.ds((device + 1) * cells - size, size)]
        moves.append((last_ref.at[pl.ds(device * rows, rows), :], target))
    started = [pltpu.make_async_copy(*move, sems.at[index]) for index, move in enumerate(moves)]
    for copy in started:
        copy.start()
    for copy in started:
        copy.wait()


def reordered(ref, devices):
    place = lax.axis_index("state")
    rows = ref.shape[0] // devices
    starts = [pl.multiple_of((place ^ distance) * rows, rows) for distance in range(devices)]
    return jnp.concatenate([ref[pl.ds(start, rows), :] for start in starts], axis=0)


def blocks_of(fields, here, there, first, weight_ref, reading_ref):
    span = PARTITION_SPAN
    seen = jnp.concatenate([here, there], axis=1)
    blocks = []
    for spot in range(QUAD):
        terms = [ref[pl.ds(first + spot, 1), :] for ref in (weight_ref, reading_ref)]
        blocks.append((fields[:, spot * span : (spot + 1) * span], seen, *terms))
    return blocks


def head_kernel(devices, fields_ref, here_ref, there_ref, weight_ref, reading_ref, *results):
    span = PARTITION_SPAN
    first = pl.program_id(0) * QUAD
    fields, here, there = [reordered(ref, devices) for ref in (fields_ref, here_ref, there_ref)]
    for spot, result in enumerate(updated(blocks_of(fields, here, there, first, weight_ref, reading_ref))):
        start = 0
        for result_ref in results:
            rows = result_ref.shape[0]
            result_ref[:, spot * span : (spot + 1) * span] = result[start : start + rows]
            start += rows


def tail_kernel(first_ref, begin_ref, end_ref, here_ref, tiles_ref, weight_ref, reading_ref, result_ref):
    span = PARTITION_SPAN
    step = pl.program_id(0)
    begin = jnp.where(step == 0, first_ref[...], begin_ref[...])
    fields = jnp.concatenate([begin, end_ref[...]], axis=1)
    here = jnp.where(step == 0, here_ref[...], tiles_ref[:, :span])
    there = jnp.where(step == 0, tiles_ref[:, :span], tiles_ref[:, span:])
    first = weight_ref.shape[0] + (step - 2) * QUAD
    for spot, result in enumerate(updated(blocks_of(fields, here, there, first, weight_ref, reading_ref))):
        result_ref[:, spot * span : (spot + 1) * span] = result


def in_stages(fields, observations, devices):
    own_members, all_cells = fields.shape
    cells = all_cells // devices
    amount = cells // PARTITION_SPAN
    members = own_members * devices
    outer = devices // INNER
    quads = amount // QUAD
    width = QUAD * PARTITION_SPAN
    lanes = QUAD * OB
    early = quads - 2
    late = 2
    half = R * PARTITION_SPAN
    anywhere = pl.BlockSpec(memory_space=pl.ANY)
    vmem = pl.BlockSpec(memory_space=pltpu.VMEM)

    def call(kernel, inputs, outputs, grant=16, cost=1, **options):
        return pl.pallas_call(
            kernel,
            out_shape=outputs,
            in_specs=inputs,
            compiler_params=pltpu.CompilerParams(vmem_limit_bytes=grant << 20),
            cost_estimate=pl.CostEstimate(flops=cost, bytes_accessed=1, transcendentals=0),
            **options,
        )

    def columns(size, index):
        return pl.BlockSpec((members, size), lambda step: (0, index))

    def full(array):
        return pl.BlockSpec(array.shape, lambda step: (0, 0))

    def group(parts, size):
        return jax.ShapeDtypeStruct((members // parts, size), jnp.float32)

    def swapped(arrays, unit):
        pairs = [[(i, i ^ (unit * k)) for i in range(devices)] for k in range(len(arrays))]
        return [arrays[0]] + [lax.ppermute(arrays[k], "state", pairs[k]) for k in range(1, len(arrays))]

    def second_parts():
        return call(
            functools.partial(second_part_kernel, split),
            [anywhere],
            [group(INNER, cells - split)] * INNER,
            out_specs=[vmem] * INNER,
            scratch_shapes=[pltpu.SemaphoreType.DMA((devices,))],
        )(fields)

    def turned(arrays, parts, cost=1):
        return call(
            functools.partial(turn_kernel, own_members),
            [vmem] * len(arrays),
            [group(parts, arrays[0].shape[1])] * parts,
            cost=cost,
            out_specs=[vmem] * parts,
        )(*arrays)

    def exchanged(array):
        return lax.all_to_all(array, "state", split_axis=0, concat_axis=0, tiled=True)

    split = early * width + half
    sent = call(
        functools.partial(first_part_kernel, split),
        [anywhere, vmem],
        jax.ShapeDtypeStruct((devices, own_members, split + lanes), jnp.float32),
        grant=56,
        out_specs=anywhere,
        scratch_shapes=[
            pltpu.VMEM((devices, own_members, cells + lanes), jnp.float32),
            pltpu.SemaphoreType.DMA((2 * devices,)),
        ],
    )(fields, observations[2].T)
    first = exchanged(sent).reshape(members, split + lanes)
    second = turned(swapped(second_parts(), 1), outer)
    second, observations = lax.optimization_barrier((second, observations))
    root_weight, reading, quad_position = window_terms(*observations, members)
    second, root_weight, reading, quad_position = lax.optimization_barrier(
        (second, root_weight, reading, quad_position)
    )
    second = swapped(second, INNER)
    terms = [root_weight, reading]
    seen = call(
        pick_first_kernel,
        [vmem, vmem],
        jax.ShapeDtypeStruct((members, (early + 1) * lanes), jnp.float32),
        out_specs=vmem,
    )(first, quad_position)

    groups = call(
        functools.partial(head_kernel, devices),
        [
            pl.BlockSpec((members, width), lambda step: (0, step)),
            pl.BlockSpec((members, lanes), lambda step: (0, step)),
            pl.BlockSpec((members, lanes), lambda step: (0, step + 1)),
            *[full(term) for term in terms],
        ],
        [group(outer, early * width)] * outer,
        grant=40,
        grid=(early,),
        out_specs=[pl.BlockSpec((members // outer, width), lambda step: (0, step))] * outer,
    )(first, seen, seen, *terms)
    groups, second = lax.optimization_barrier((groups, second))
    beyond = swapped(groups, INNER)

    second, tiles = call(
        functools.partial(second_kernel, devices),
        [columns(lanes, split // lanes), *[full(array) for array in (quad_position, *second)]],
        [
            jax.ShapeDtypeStruct((members, cells - split), jnp.float32),
            jax.ShapeDtypeStruct((members, 2 * lanes), jnp.float32),
        ],
        grid=(1,),
        out_specs=[columns(cells - split, 0), columns(2 * lanes, 0)],
    )(first, quad_position, *second)
    ends = call(
        tail_kernel,
        [
            columns(half, split // half - 1),
            columns(half, 1),
            pl.BlockSpec((members, half), lambda step: (0, 2 * step)),
            columns(lanes, early),
            full(tiles),
            *[full(term) for term in terms],
        ],
        jax.ShapeDtypeStruct((members, late * width), jnp.float32),
        grant=60,
        grid=(late,),
        out_specs=pl.BlockSpec((members, width), lambda step: (0, step)),
    )(first, second, second, seen, tiles, *terms)
    ends = exchanged(ends.reshape(devices, own_members, late * width)).reshape(members, late * width)

    near = turned(beyond, INNER, cost=1 << 36)
    return call(
        functools.partial(place_kernel, cells),
        [vmem] * (INNER + 1),
        jax.ShapeDtypeStruct((own_members, all_cells), jnp.float32),
        out_specs=anywhere,
        scratch_shapes=[pltpu.SemaphoreType.DMA((2 * devices,))],
    )(*swapped(near, 1), ends)


def by_all_to_all(fields, observations, devices):
    own_members, all_cells = fields.shape
    cells = all_cells // devices
    amount = cells // PARTITION_SPAN
    members = own_members * devices
    span = PARTITION_SPAN
    root_weight, reading, quad_position = window_terms(*observations, members)
    sent = fields.reshape(own_members, devices, cells).transpose(1, 0, 2)
    fields = lax.all_to_all(sent, "state", split_axis=0, concat_axis=0, tiled=True).reshape(members, cells)
    vmem = pl.BlockSpec(memory_space=pltpu.VMEM)
    own_seen = pl.pallas_call(
        pick_kernel,
        out_shape=jax.ShapeDtypeStruct((members, amount * OB), jnp.float32),
        in_specs=[vmem, vmem],
        out_specs=vmem,
        compiler_params=pltpu.CompilerParams(vmem_limit_bytes=16 << 20),
    )(fields, quad_position)
    edge = own_seen[:, : QUAD * OB]
    before = lax.ppermute(edge, "state", [(i, i + 1) for i in range(devices - 1)])
    after = lax.ppermute(edge, "state", [(i + 1, i) for i in range(devices - 1)])
    steps = amount // QUAD

    def whole(*shape):
        return pl.BlockSpec(shape, lambda step: (0, 0))

    analysis = pl.pallas_call(
        update_kernel,
        grid=(steps,),
        out_shape=jax.ShapeDtypeStruct((members, cells), jnp.float32),
        in_specs=[
            pl.BlockSpec((members, QUAD * span), lambda step: (0, step)),
            whole(members, QUAD * OB),
            whole(members, amount * OB),
            whole(members, QUAD * OB),
            whole(amount, 2 * QUAD * OB),
            whole(amount, 2 * QUAD * OB),
        ],
        out_specs=pl.BlockSpec((members, QUAD * span), lambda step: (0, step)),
        compiler_params=pltpu.CompilerParams(vmem_limit_bytes=40 << 20),
    )(fields, before, own_seen, after, root_weight, reading)
    result = lax.all_to_all(
        analysis.reshape(devices, own_members, cells), "state", split_axis=0, concat_axis=0, tiled=True
    )
    return result.transpose(1, 0, 2).reshape(own_members, all_cells)


def body(
    background_draws_table,
    measurement_reading,
    measurement_precision,
    sensed_point_position,
    measurement_tally,
    adjacent_tile_number,
):
    devices = lax.axis_size("state")
    observations = (
        measurement_reading,
        measurement_precision,
        sensed_point_position,
        measurement_tally,
        adjacent_tile_number,
    )
    way = in_stages if devices == INNER * INNER else by_all_to_all
    return way(background_draws_table, observations, devices)


def solution(mesh):
    return jax.shard_map(
        body,
        mesh=mesh,
        in_specs=(
            P("state", "groups"),
            P("groups", None),
            P("groups", None),
            P("groups", None),
            P("groups"),
            P(("groups", "state"), None),
        ),
        out_specs=P("state", "groups"),
        check_vma=False,
    )
```

```python
import functools

import jax
import jax.numpy as jnp
from jax import lax
from jax.experimental import pallas as pl
from jax.experimental.pallas import tpu as pltpu
from jax.sharding import PartitionSpec as P

PARTITION_SPAN = 128
OB = 32
R = 2
NS_ITERS = 5
LOC = 128

QUAD = PARTITION_SPAN // OB
INNER = 4
NN = (((1,), (0,)), ((), ()))
NT = (((1,), (1,)), ((), ()))


def halves(values):
    high = values.astype(jnp.bfloat16)
    return high, (values - high.astype(jnp.float32)).astype(jnp.bfloat16)


def times(left, right, dims):
    (left_high, left_low), (right_high, right_low) = left, right
    return lax.dot_general(
        jnp.concatenate([left_high, left_high, left_low], axis=1),
        jnp.concatenate([right_high, right_low, right_high], axis=dims[0][1][0]),
        dims,
        preferred_element_type=jnp.float32,
    )


def updated(blocks):
    turns = [analysis(*block) for block in blocks]
    results = [None] * len(turns)
    while None in results:
        for index, turn in enumerate(turns):
            if results[index] is None:
                results[index] = next(turn)
    return results


def analysis(fields, seen, root_weight, reading):
    seen_mean = jnp.mean(seen, axis=0, keepdims=True)
    pull = (reading - seen_mean) * root_weight
    root = halves((seen - seen_mean) * root_weight)
    spread = times(root, root, NT)
    pull = times(halves(jnp.broadcast_to(pull, (16, pull.shape[1]))), root, NT)
    yield None
    squares = jnp.sum(jnp.sum(spread * spread, axis=0, keepdims=True), axis=1, keepdims=True)
    norm_size = 1.0 + jnp.sqrt(squares)
    unit = 1.0 / norm_size
    rest = spread * (-0.5 * unit)
    cells = fields.T
    centre = jnp.mean(cells, axis=1, keepdims=True)
    chain = jnp.concatenate([cells - centre, pull], axis=0)
    for sweep in range(NS_ITERS - 1):
        parts = halves(rest)
        gain = 1.5 - 0.5 * unit
        if sweep < NS_ITERS - 2:
            square = times(parts, parts, NN)
        moved = times(halves(chain), parts, NN)
        yield None
        if sweep < NS_ITERS - 2:
            once = (gain - 0.5 * unit) * rest + square
            cubic = times(halves(once), parts, NN)
        chain = gain * chain + moved
        if sweep < NS_ITERS - 2:
            yield None
            rest = gain * once - (0.5 * unit * gain) * rest + cubic
            unit = unit * gain * gain
    moved = times(halves(chain), parts, NN)
    yield None
    end = (-0.5 * unit) * chain + moved
    for _ in range(2):
        moved = times(halves(end), parts, NN)
        yield None
        end = gain * end + moved
    chain = (1.5 * chain + end) * lax.rsqrt(norm_size)
    moved = chain[:PARTITION_SPAN]
    shift = jnp.sum(moved * chain[PARTITION_SPAN : PARTITION_SPAN + 1], axis=1, keepdims=True)
    yield (moved + (centre + shift)).T


def picked(fields, position):
    members = fields[0].shape[0]
    span = PARTITION_SPAN
    index = jnp.broadcast_to(position, (members, span))
    lanes = lax.broadcasted_iota(jnp.int32, (members, span), 1)
    total = None
    for spot, field in enumerate(fields):
        found = jnp.take_along_axis(field, index, axis=1)
        total = found if spot == 0 else jnp.where(lanes // OB == spot, found, total)
    return total


def pick_kernel(fields_ref, position_ref, seen_ref):
    span = PARTITION_SPAN
    quads = position_ref.shape[0]
    amount = quads * QUAD
    for quad in range(quads):
        blocks = [(quad * QUAD + spot - R) % amount for spot in range(QUAD)]
        fields = [fields_ref[:, block * span : (block + 1) * span] for block in blocks]
        seen_ref[:, quad * span : (quad + 1) * span] = picked(fields, position_ref[quad : quad + 1, :])


def pick_first_kernel(fields_ref, position_ref, seen_ref):
    span = PARTITION_SPAN
    amount = fields_ref.shape[1] // span - 1
    beyond = fields_ref[:, amount * span :]
    low = lax.broadcasted_iota(jnp.int32, beyond.shape, 1) < R * OB
    for quad in range(seen_ref.shape[1] // span):
        blocks = [max(quad * QUAD + spot - R, 0) for spot in range(QUAD)]
        fields = [fields_ref[:, block * span : (block + 1) * span] for block in blocks]
        found = picked(fields, position_ref[quad : quad + 1, :])
        seen_ref[:, quad * span : (quad + 1) * span] = found if quad else jnp.where(low, beyond, found)


def second_kernel(devices, beyond_ref, position_ref, *refs):
    *parts, fields_ref, seen_ref = refs
    place = lax.axis_index("state")
    span = PARTITION_SPAN
    quads = position_ref.shape[0]
    rows = fields_ref.shape[0] // devices
    for distance in range(devices):
        far, near = divmod(distance, INNER)
        start = pl.multiple_of((place ^ distance) * rows, rows)
        fields_ref[pl.ds(start, rows), :] = parts[far][near * rows : (near + 1) * rows, :]
    amount = fields_ref.shape[1] // span
    low = lax.broadcasted_iota(jnp.int32, beyond_ref.shape, 1) < R * OB
    for index in range(seen_ref.shape[1] // span):
        blocks = [min(index * QUAD + spot, amount - 1) for spot in range(QUAD)]
        fields = [fields_ref[:, block * span : (block + 1) * span] for block in blocks]
        quad = (quads - seen_ref.shape[1] // span + 1 + index) % quads
        found = picked(fields, position_ref[quad : quad + 1, :])
        seen_ref[:, index * span : (index + 1) * span] = found if quad else jnp.where(low, found, beyond_ref[...])


def update_kernel(fields_ref, before_ref, own_ref, after_ref, weight_ref, reading_ref, result_ref):
    members, span = before_ref.shape
    step = pl.program_id(0)
    steps = pl.num_programs(0)
    lanes = lax.broadcasted_iota(jnp.int32, (members, span), 1)
    here = own_ref[:, pl.ds(pl.multiple_of(step * span, span), span)]
    following = own_ref[:, pl.ds(pl.multiple_of(lax.rem(step + 1, steps) * span, span), span)]
    first = jnp.where((step == 0) & (lanes < R * OB), before_ref[...], here)
    second = jnp.where((step == steps - 1) & (lanes >= R * OB), after_ref[...], following)
    seen = jnp.concatenate([first, second], axis=1)
    blocks = [
        (
            fields_ref[:, spot * span : (spot + 1) * span],
            seen,
            weight_ref[pl.ds(step * QUAD + spot, 1), :],
            reading_ref[pl.ds(step * QUAD + spot, 1), :],
        )
        for spot in range(QUAD)
    ]
    for spot, result in enumerate(updated(blocks)):
        result_ref[:, spot * span : (spot + 1) * span] = result


def terms_kernel(
    amount, members, reading_ref, precision_ref, position_ref, tally_ref, adjacent_ref, terms_ref, quad_ref
):
    first_block = lax.axis_index("state") * amount
    total = tally_ref.shape[0]
    quads = amount // QUAD
    span = PARTITION_SPAN
    lane = lax.broadcasted_iota(jnp.int32, (1, span), 1)
    low = lane < R * OB

    def tile(ref, quad):
        row = first_block // QUAD + quad
        before = ref[pl.ds(jnp.maximum(row - 1, 0), 1), :]
        after = ref[pl.ds(jnp.minimum(row, total // QUAD - 1), 1), :]
        return pltpu.roll(jnp.where(low, after, before), R * OB, 1)

    def counts(quad):
        found = jnp.zeros((1, span), jnp.int32)
        for spot in range(QUAD):
            block = jnp.clip(first_block + quad * QUAD + spot - R, 0, total - 1)
            found = jnp.where(lane // OB == spot, tally_ref[block], found)
        return found

    def pair(tiles, quad):
        return jnp.concatenate(tiles[quad : quad + 2], axis=1)

    positions = [tile(position_ref, quad) for quad in range(quads + 1)]
    readings = [tile(reading_ref, quad) for quad in range(quads + 1)]
    precisions = [tile(precision_ref, quad) for quad in range(quads + 1)]
    tallies = [counts(quad) for quad in range(quads + 1)]
    wide = lax.broadcasted_iota(jnp.int32, (1, 2 * span), 1)
    for block in range(amount):
        quad, spot = divmod(block, QUAD)
        neighbour = wide // OB - spot
        usable = jnp.zeros((1, 2 * span), jnp.float32)
        for j in range(2 * R + 1):
            there = jnp.where(adjacent_ref[block, j] >= 0, 1.0, 0.0)
            usable = jnp.where(neighbour == j, there, usable)
        distance = (
            ((neighbour - R) * span).astype(jnp.float32)
            + pair(positions, quad).astype(jnp.float32)
            - 0.5 * (span - 1)
        )
        decay = jnp.exp(-0.5 * (distance / LOC) ** 2)
        active = jnp.where(wide % OB < pair(tallies, quad), usable, 0.0)
        weight = pair(precisions, quad) * decay * active
        terms_ref[0, block : block + 1, :] = jnp.sqrt(weight / (members - 1.0))
        terms_ref[1, block : block + 1, :] = pair(readings, quad)
    edge = jnp.where(low, positions[quads], positions[0])
    for quad in range(quads):
        quad_ref[quad : quad + 1, :] = positions[quad] if quad else edge


def window_terms(reading, precision, position, tally, adjacent, members):
    amount = adjacent.shape[0]
    lanes = QUAD * OB
    vmem = pl.BlockSpec(memory_space=pltpu.VMEM)
    smem = pl.BlockSpec(memory_space=pltpu.SMEM)
    terms = jax.ShapeDtypeStruct((2, amount, 2 * lanes), jnp.float32)
    return pl.pallas_call(
        functools.partial(terms_kernel, amount, members),
        out_shape=[terms, jax.ShapeDtypeStruct((amount // QUAD, lanes), jnp.int32)],
        in_specs=[vmem, vmem, vmem, smem, smem],
        out_specs=[vmem, vmem],
    )(*(array.reshape(-1, lanes) for array in (reading, precision, position)), tally, adjacent)


def copied(copies):
    for copy in copies:
        copy.start()
    return copies


def into_held(fields_ref, held_ref, sems, start, size):
    devices = held_ref.shape[0]
    cells = fields_ref.shape[1] // devices
    sources = [fields_ref.at[:, pl.ds(device * cells + start, size)] for device in range(devices)]
    targets = [held_ref.at[device, :, pl.ds(0, size)] for device in range(devices)]
    return copied([pltpu.make_async_copy(*pair, sems.at[index]) for index, pair in enumerate(zip(sources, targets))])


def first_part_kernel(split, fields_ref, position_ref, sent_ref, held_ref, sems):
    devices, rows, _ = sent_ref.shape
    cells = fields_ref.shape[1] // devices
    span = PARTITION_SPAN
    amount = cells // span
    into = into_held(fields_ref, held_ref, sems, 0, cells)

    def out(number, some, start, size, to):
        source = held_ref.at[some, :, pl.ds(start, size)]
        target = sent_ref.at[some, :, pl.ds(to, size)]
        return copied([pltpu.make_async_copy(source, target, sems.at[devices + number])])

    away = []
    for device, copy in enumerate(into):
        copy.wait()
        if device % INNER == INNER - 1:
            away += out(len(away), pl.ds(device + 1 - INNER, INNER), 0, split, 0)

    def shifted(array, distance):
        if distance > 0:
            return jnp.concatenate([array[:distance], array[:-distance]], axis=0)
        return jnp.concatenate([array[-distance:], array[distance:]], axis=0)

    beyond = [(amount - R + spot, 1) for spot in range(R)] + [(spot, -1) for spot in range(R)]
    positions = position_ref[...].T.reshape(devices, amount, OB)
    position = jnp.concatenate([shifted(positions[:, block], distance) for block, distance in beyond], axis=1)
    position = jnp.broadcast_to(position[:, None], (devices, rows, span)).reshape(devices * rows, span)
    fields = [
        shifted(held_ref[:, :, block * span : (block + 1) * span].reshape(devices * rows, span), distance * rows)
        for block, distance in beyond
    ]
    held_ref[:, :, cells : cells + span] = picked(fields, position).reshape(devices, rows, span)
    away += out(len(away), pl.ds(0, devices), cells, span, split)
    for copy in away:
        copy.wait()


def second_part_kernel(split, fields_ref, *refs):
    *sent, sems = refs
    place = lax.axis_index("state")
    rows = fields_ref.shape[0]
    size = sent[0].shape[1]
    cells = split + size
    copies = []
    for near, array in enumerate(sent):
        for far in range(array.shape[0] // rows):
            start = (place ^ (far * INNER + near)) * cells + split
            source = fields_ref.at[:, pl.ds(pl.multiple_of(start, PARTITION_SPAN), size)]
            target = array.at[pl.ds(far * rows, rows), :]
            copies.append(pltpu.make_async_copy(source, target, sems.at[len(copies)]))
    for copy in copied(copies):
        copy.wait()


def turn_kernel(rows, *refs):
    given, made = refs[: len(refs) // 2], refs[len(refs) // 2 :]
    for i, source in enumerate(given):
        for j, target in enumerate(made):
            target[i * rows : (i + 1) * rows, :] = source[j * rows : (j + 1) * rows, :]


def place_kernel(cells, *refs):
    *parts, last_ref, result_ref, sems = refs
    place = lax.axis_index("state")
    rows = result_ref.shape[0]
    moves = []
    for near, part in enumerate(parts):
        width = part.shape[1]
        for far in range(part.shape[0] // rows):
            start = (place ^ (far * INNER + near)) * cells
            target = result_ref.at[:, pl.ds(pl.multiple_of(start, width), width)]
            moves.append((part.at[pl.ds(far * rows, rows), :], target))
    for device in range(last_ref.shape[0] // rows):
        size = last_ref.shape[1]
        target = result_ref.at[:, pl.ds((device + 1) * cells - size, size)]
        moves.append((last_ref.at[pl.ds(device * rows, rows), :], target))
    started = [pltpu.make_async_copy(*move, sems.at[index]) for index, move in enumerate(moves)]
    for copy in started:
        copy.start()
    for copy in started:
        copy.wait()


def reordered(ref, devices):
    place = lax.axis_index("state")
    rows = ref.shape[0] // devices
    starts = [pl.multiple_of((place ^ distance) * rows, rows) for distance in range(devices)]
    return jnp.concatenate([ref[pl.ds(start, rows), :] for start in starts], axis=0)


def blocks_of(fields, here, there, first, terms_ref):
    span = PARTITION_SPAN
    seen = jnp.concatenate([here, there], axis=1)
    blocks = []
    for spot in range(QUAD):
        root_weight, reading = (terms_ref[term, pl.ds(first + spot, 1), :] for term in range(2))
        blocks.append((fields[:, spot * span : (spot + 1) * span], seen, root_weight, reading))
    return blocks


def head_kernel(devices, fields_ref, here_ref, there_ref, terms_ref, *results):
    span = PARTITION_SPAN
    first = pl.program_id(0) * QUAD
    fields, here, there = [reordered(ref, devices) for ref in (fields_ref, here_ref, there_ref)]
    for spot, result in enumerate(updated(blocks_of(fields, here, there, first, terms_ref))):
        start = 0
        for result_ref in results:
            rows = result_ref.shape[0]
            result_ref[:, spot * span : (spot + 1) * span] = result[start : start + rows]
            start += rows


def tail_kernel(first_ref, begin_ref, end_ref, here_ref, tiles_ref, terms_ref, result_ref):
    span = PARTITION_SPAN
    step = pl.program_id(0)
    begin = jnp.where(step == 0, first_ref[...], begin_ref[...])
    fields = jnp.concatenate([begin, end_ref[...]], axis=1)
    here = jnp.where(step == 0, here_ref[...], tiles_ref[:, :span])
    there = jnp.where(step == 0, tiles_ref[:, :span], tiles_ref[:, span:])
    first = terms_ref.shape[1] + (step - 2) * QUAD
    for spot, result in enumerate(updated(blocks_of(fields, here, there, first, terms_ref))):
        result_ref[:, spot * span : (spot + 1) * span] = result


def in_stages(fields, observations, devices):
    own_members, all_cells = fields.shape
    cells = all_cells // devices
    amount = cells // PARTITION_SPAN
    members = own_members * devices
    outer = devices // INNER
    quads = amount // QUAD
    width = QUAD * PARTITION_SPAN
    lanes = QUAD * OB
    early = quads - 2
    late = 2
    half = R * PARTITION_SPAN
    anywhere = pl.BlockSpec(memory_space=pl.ANY)
    vmem = pl.BlockSpec(memory_space=pltpu.VMEM)

    def call(kernel, inputs, outputs, grant=16, cost=1, **options):
        return pl.pallas_call(
            kernel,
            out_shape=outputs,
            in_specs=inputs,
            compiler_params=pltpu.CompilerParams(vmem_limit_bytes=grant << 20),
            cost_estimate=pl.CostEstimate(flops=cost, bytes_accessed=1, transcendentals=0),
            **options,
        )

    def columns(size, index):
        return pl.BlockSpec((members, size), lambda step: (0, index))

    def full(array):
        return pl.BlockSpec(array.shape, lambda step: (0,) * array.ndim)

    def group(parts, size):
        return jax.ShapeDtypeStruct((members // parts, size), jnp.float32)

    def swapped(arrays, unit):
        pairs = [[(i, i ^ (unit * k)) for i in range(devices)] for k in range(len(arrays))]
        return [arrays[0]] + [lax.ppermute(arrays[k], "state", pairs[k]) for k in range(1, len(arrays))]

    def second_parts():
        return call(
            functools.partial(second_part_kernel, split),
            [anywhere],
            [group(INNER, cells - split)] * INNER,
            out_specs=[vmem] * INNER,
            scratch_shapes=[pltpu.SemaphoreType.DMA((devices,))],
        )(fields)

    def turned(arrays, parts, cost=1):
        return call(
            functools.partial(turn_kernel, own_members),
            [vmem] * len(arrays),
            [group(parts, arrays[0].shape[1])] * parts,
            cost=cost,
            out_specs=[vmem] * parts,
        )(*arrays)

    def exchanged(array):
        return lax.all_to_all(array, "state", split_axis=0, concat_axis=0, tiled=True)

    split = early * width + half
    sent = call(
        functools.partial(first_part_kernel, split),
        [anywhere, vmem],
        jax.ShapeDtypeStruct((devices, own_members, split + lanes), jnp.float32),
        grant=56,
        out_specs=anywhere,
        scratch_shapes=[
            pltpu.VMEM((devices, own_members, cells + lanes), jnp.float32),
            pltpu.SemaphoreType.DMA((2 * devices,)),
        ],
    )(fields, observations[2].T)
    first = exchanged(sent).reshape(members, split + lanes)
    second = turned(swapped(second_parts(), 1), outer)
    second, tied = lax.optimization_barrier((second, [observations[0],observations[3]]))
    observations = [tied[0], observations[1], observations[2], tied[1], observations[4]]
    terms, quad_position = window_terms(*observations, members)
    second, terms, quad_position = lax.optimization_barrier((second, terms, quad_position))
    second = swapped(second, INNER)
    seen = call(
        pick_first_kernel,
        [vmem, vmem],
        jax.ShapeDtypeStruct((members, (early + 1) * lanes), jnp.float32),
        out_specs=vmem,
    )(first, quad_position)

    groups = call(
        functools.partial(head_kernel, devices),
        [
            pl.BlockSpec((members, width), lambda step: (0, step)),
            pl.BlockSpec((members, lanes), lambda step: (0, step)),
            pl.BlockSpec((members, lanes), lambda step: (0, step + 1)),
            full(terms),
        ],
        [group(outer, early * width)] * outer,
        grant=40,
        grid=(early,),
        out_specs=[pl.BlockSpec((members // outer, width), lambda step: (0, step))] * outer,
    )(first, seen, seen, terms)
    groups, second = lax.optimization_barrier((groups, second))
    beyond = swapped(groups, INNER)

    second, tiles = call(
        functools.partial(second_kernel, devices),
        [columns(lanes, split // lanes), *[full(array) for array in (quad_position, *second)]],
        [
            jax.ShapeDtypeStruct((members, cells - split), jnp.float32),
            jax.ShapeDtypeStruct((members, 2 * lanes), jnp.float32),
        ],
        grid=(1,),
        out_specs=[columns(cells - split, 0), columns(2 * lanes, 0)],
    )(first, quad_position, *second)
    ends = call(
        tail_kernel,
        [
            columns(half, split // half - 1),
            columns(half, 1),
            pl.BlockSpec((members, half), lambda step: (0, 2 * step)),
            columns(lanes, early),
            full(tiles),
            full(terms),
        ],
        jax.ShapeDtypeStruct((members, late * width), jnp.float32),
        grant=60,
        grid=(late,),
        out_specs=pl.BlockSpec((members, width), lambda step: (0, step)),
    )(first, second, second, seen, tiles, terms)
    ends = exchanged(ends.reshape(devices, own_members, late * width)).reshape(members, late * width)

    near = turned(beyond, INNER, cost=1 << 36)
    return call(
        functools.partial(place_kernel, cells),
        [vmem] * (INNER + 1),
        jax.ShapeDtypeStruct((own_members, all_cells), jnp.float32),
        out_specs=anywhere,
        scratch_shapes=[pltpu.SemaphoreType.DMA((2 * devices,))],
    )(*swapped(near, 1), ends)


def by_all_to_all(fields, observations, devices):
    own_members, all_cells = fields.shape
    cells = all_cells // devices
    amount = cells // PARTITION_SPAN
    members = own_members * devices
    span = PARTITION_SPAN
    (root_weight, reading), quad_position = window_terms(*observations, members)
    sent = fields.reshape(own_members, devices, cells).transpose(1, 0, 2)
    fields = lax.all_to_all(sent, "state", split_axis=0, concat_axis=0, tiled=True).reshape(members, cells)
    vmem = pl.BlockSpec(memory_space=pltpu.VMEM)
    own_seen = pl.pallas_call(
        pick_kernel,
        out_shape=jax.ShapeDtypeStruct((members, amount * OB), jnp.float32),
        in_specs=[vmem, vmem],
        out_specs=vmem,
        compiler_params=pltpu.CompilerParams(vmem_limit_bytes=16 << 20),
    )(fields, quad_position)
    edge = own_seen[:, : QUAD * OB]
    before = lax.ppermute(edge, "state", [(i, i + 1) for i in range(devices - 1)])
    after = lax.ppermute(edge, "state", [(i + 1, i) for i in range(devices - 1)])
    steps = amount // QUAD

    def whole(*shape):
        return pl.BlockSpec(shape, lambda step: (0, 0))

    analysis = pl.pallas_call(
        update_kernel,
        grid=(steps,),
        out_shape=jax.ShapeDtypeStruct((members, cells), jnp.float32),
        in_specs=[
            pl.BlockSpec((members, QUAD * span), lambda step: (0, step)),
            whole(members, QUAD * OB),
            whole(members, amount * OB),
            whole(members, QUAD * OB),
            whole(amount, 2 * QUAD * OB),
            whole(amount, 2 * QUAD * OB),
        ],
        out_specs=pl.BlockSpec((members, QUAD * span), lambda step: (0, step)),
        compiler_params=pltpu.CompilerParams(vmem_limit_bytes=40 << 20),
    )(fields, before, own_seen, after, root_weight, reading)
    result = lax.all_to_all(
        analysis.reshape(devices, own_members, cells), "state", split_axis=0, concat_axis=0, tiled=True
    )
    return result.transpose(1, 0, 2).reshape(own_members, all_cells)


def body(
    background_draws_table,
    measurement_reading,
    measurement_precision,
    sensed_point_position,
    measurement_tally,
    adjacent_tile_number,
):
    devices = lax.axis_size("state")
    observations = (
        measurement_reading,
        measurement_precision,
        sensed_point_position,
        measurement_tally,
        adjacent_tile_number,
    )
    way = in_stages if devices == INNER * INNER else by_all_to_all
    return way(background_draws_table, observations, devices)


def solution(mesh):
    return jax.shard_map(
        body,
        mesh=mesh,
        in_specs=(
            P("state", "groups"),
            P("groups", None),
            P("groups", None),
            P("groups", None),
            P("groups"),
            P(("groups", "state"), None),
        ),
        out_specs=P("state", "groups"),
        check_vma=False,
    )
```

```python
import functools

import jax
import jax.numpy as jnp
from jax import lax
from jax.experimental import pallas as pl
from jax.experimental.pallas import tpu as pltpu
from jax.sharding import PartitionSpec as P

PARTITION_SPAN = 128
OB = 32
R = 2
NS_ITERS = 5
LOC = 128

QUAD = PARTITION_SPAN // OB
INNER = 4
NN = (((1,), (0,)), ((), ()))
NT = (((1,), (1,)), ((), ()))


def halves(values):
    high = values.astype(jnp.bfloat16)
    return high, (values - high.astype(jnp.float32)).astype(jnp.bfloat16)


def times(left, right, dims):
    (left_high, left_low), (right_high, right_low) = left, right
    return lax.dot_general(
        jnp.concatenate([left_high, left_high, left_low], axis=1),
        jnp.concatenate([right_high, right_low, right_high], axis=dims[0][1][0]),
        dims,
        preferred_element_type=jnp.float32,
    )


def updated(blocks):
    turns = [analysis(*block) for block in blocks]
    results = [None] * len(turns)
    while None in results:
        for index, turn in enumerate(turns):
            if results[index] is None:
                results[index] = next(turn)
    return results


def analysis(fields, seen, root_weight, reading):
    seen_mean = jnp.mean(seen, axis=0, keepdims=True)
    pull = (reading - seen_mean) * root_weight
    root = halves((seen - seen_mean) * root_weight)
    spread = times(root, root, NT)
    pull = times(halves(jnp.broadcast_to(pull, (16, pull.shape[1]))), root, NT)
    yield None
    squares = jnp.sum(jnp.sum(spread * spread, axis=0, keepdims=True), axis=1, keepdims=True)
    norm_size = 1.0 + jnp.sqrt(squares)
    unit = 1.0 / norm_size
    rest = spread * (-0.5 * unit)
    cells = fields.T
    centre = jnp.mean(cells, axis=1, keepdims=True)
    chain = jnp.concatenate([cells - centre, pull], axis=0)
    for sweep in range(NS_ITERS - 1):
        parts = halves(rest)
        gain = 1.5 - 0.5 * unit
        if sweep < NS_ITERS - 2:
            square = times(parts, parts, NN)
        moved = times(halves(chain), parts, NN)
        yield None
        if sweep < NS_ITERS - 2:
            once = (gain - 0.5 * unit) * rest + square
            cubic = times(halves(once), parts, NN)
        chain = gain * chain + moved
        if sweep < NS_ITERS - 2:
            yield None
            rest = gain * once - (0.5 * unit * gain) * rest + cubic
            unit = unit * gain * gain
    moved = times(halves(chain), parts, NN)
    yield None
    end = (-0.5 * unit) * chain + moved
    for _ in range(2):
        moved = times(halves(end), parts, NN)
        yield None
        end = gain * end + moved
    chain = (1.5 * chain + end) * lax.rsqrt(norm_size)
    moved = chain[:PARTITION_SPAN]
    shift = jnp.sum(moved * chain[PARTITION_SPAN : PARTITION_SPAN + 1], axis=1, keepdims=True)
    yield (moved + (centre + shift)).T


def picked(fields, position):
    members = fields[0].shape[0]
    span = PARTITION_SPAN
    index = jnp.broadcast_to(position, (members, span))
    lanes = lax.broadcasted_iota(jnp.int32, (members, span), 1)
    total = None
    for spot, field in enumerate(fields):
        found = jnp.take_along_axis(field, index, axis=1)
        total = found if spot == 0 else jnp.where(lanes // OB == spot, found, total)
    return total


def pick_kernel(fields_ref, position_ref, seen_ref):
    span = PARTITION_SPAN
    quads = position_ref.shape[0]
    amount = quads * QUAD
    for quad in range(quads):
        blocks = [(quad * QUAD + spot - R) % amount for spot in range(QUAD)]
        fields = [fields_ref[:, block * span : (block + 1) * span] for block in blocks]
        seen_ref[:, quad * span : (quad + 1) * span] = picked(fields, position_ref[quad : quad + 1, :])


def pick_first_kernel(fields_ref, position_ref, seen_ref):
    span = PARTITION_SPAN
    amount = fields_ref.shape[1] // span - 1
    beyond = fields_ref[:, amount * span :]
    low = lax.broadcasted_iota(jnp.int32, beyond.shape, 1) < R * OB
    for quad in range(seen_ref.shape[1] // span):
        blocks = [max(quad * QUAD + spot - R, 0) for spot in range(QUAD)]
        fields = [fields_ref[:, block * span : (block + 1) * span] for block in blocks]
        found = picked(fields, position_ref[quad : quad + 1, :])
        seen_ref[:, quad * span : (quad + 1) * span] = found if quad else jnp.where(low, beyond, found)


def second_kernel(devices, beyond_ref, position_ref, *refs):
    *parts, fields_ref, seen_ref = refs
    place = lax.axis_index("state")
    span = PARTITION_SPAN
    quads = position_ref.shape[0]
    rows = fields_ref.shape[0] // devices
    for distance in range(devices):
        far, near = divmod(distance, INNER)
        start = pl.multiple_of((place ^ distance) * rows, rows)
        fields_ref[pl.ds(start, rows), :] = parts[far][near * rows : (near + 1) * rows, :]
    amount = fields_ref.shape[1] // span
    low = lax.broadcasted_iota(jnp.int32, beyond_ref.shape, 1) < R * OB
    for index in range(seen_ref.shape[1] // span):
        blocks = [min(index * QUAD + spot, amount - 1) for spot in range(QUAD)]
        fields = [fields_ref[:, block * span : (block + 1) * span] for block in blocks]
        quad = (quads - seen_ref.shape[1] // span + 1 + index) % quads
        found = picked(fields, position_ref[quad : quad + 1, :])
        seen_ref[:, index * span : (index + 1) * span] = found if quad else jnp.where(low, found, beyond_ref[...])


def update_kernel(fields_ref, before_ref, own_ref, after_ref, weight_ref, reading_ref, result_ref):
    members, span = before_ref.shape
    step = pl.program_id(0)
    steps = pl.num_programs(0)
    lanes = lax.broadcasted_iota(jnp.int32, (members, span), 1)
    here = own_ref[:, pl.ds(pl.multiple_of(step * span, span), span)]
    following = own_ref[:, pl.ds(pl.multiple_of(lax.rem(step + 1, steps) * span, span), span)]
    first = jnp.where((step == 0) & (lanes < R * OB), before_ref[...], here)
    second = jnp.where((step == steps - 1) & (lanes >= R * OB), after_ref[...], following)
    seen = jnp.concatenate([first, second], axis=1)
    blocks = [
        (
            fields_ref[:, spot * span : (spot + 1) * span],
            seen,
            weight_ref[pl.ds(step * QUAD + spot, 1), :],
            reading_ref[pl.ds(step * QUAD + spot, 1), :],
        )
        for spot in range(QUAD)
    ]
    for spot, result in enumerate(updated(blocks)):
        result_ref[:, spot * span : (spot + 1) * span] = result


def terms_kernel(
    amount, members, reading_ref, precision_ref, position_ref, tally_ref, adjacent_ref, terms_ref, quad_ref
):
    first_block = lax.axis_index("state") * amount
    total = tally_ref.shape[0]
    quads = amount // QUAD
    span = PARTITION_SPAN
    lane = lax.broadcasted_iota(jnp.int32, (1, span), 1)
    low = lane < R * OB

    def tile(ref, quad):
        row = first_block // QUAD + quad
        before = ref[pl.ds(jnp.maximum(row - 1, 0), 1), :]
        after = ref[pl.ds(jnp.minimum(row, total // QUAD - 1), 1), :]
        return pltpu.roll(jnp.where(low, after, before), R * OB, 1)

    def counts(quad):
        found = jnp.zeros((1, span), jnp.int32)
        for spot in range(QUAD):
            block = jnp.clip(first_block + quad * QUAD + spot - R, 0, total - 1)
            found = jnp.where(lane // OB == spot, tally_ref[block], found)
        return found

    def pair(tiles, quad):
        return jnp.concatenate(tiles[quad : quad + 2], axis=1)

    positions = [tile(position_ref, quad) for quad in range(quads + 1)]
    readings = [tile(reading_ref, quad) for quad in range(quads + 1)]
    precisions = [tile(precision_ref, quad) for quad in range(quads + 1)]
    tallies = [counts(quad) for quad in range(quads + 1)]
    wide = lax.broadcasted_iota(jnp.int32, (1, 2 * span), 1)
    for block in range(amount):
        quad, spot = divmod(block, QUAD)
        neighbour = wide // OB - spot
        usable = jnp.zeros((1, 2 * span), jnp.float32)
        for j in range(2 * R + 1):
            there = jnp.where(adjacent_ref[block, j] >= 0, 1.0, 0.0)
            usable = jnp.where(neighbour == j, there, usable)
        distance = (
            ((neighbour - R) * span).astype(jnp.float32)
            + pair(positions, quad).astype(jnp.float32)
            - 0.5 * (span - 1)
        )
        decay = jnp.exp(-0.5 * (distance / LOC) ** 2)
        active = jnp.where(wide % OB < pair(tallies, quad), usable, 0.0)
        weight = pair(precisions, quad) * decay * active
        terms_ref[0, block : block + 1, :] = jnp.sqrt(weight / (members - 1.0))
        terms_ref[1, block : block + 1, :] = pair(readings, quad)
    edge = jnp.where(low, positions[quads], positions[0])
    for quad in range(quads):
        quad_ref[quad : quad + 1, :] = positions[quad] if quad else edge


def window_terms(reading, precision, position, tally, adjacent, members):
    amount = adjacent.shape[0]
    lanes = QUAD * OB
    vmem = pl.BlockSpec(memory_space=pltpu.VMEM)
    smem = pl.BlockSpec(memory_space=pltpu.SMEM)
    terms = jax.ShapeDtypeStruct((2, amount, 2 * lanes), jnp.float32)
    return pl.pallas_call(
        functools.partial(terms_kernel, amount, members),
        out_shape=[terms, jax.ShapeDtypeStruct((amount // QUAD, lanes), jnp.int32)],
        in_specs=[vmem, vmem, vmem, smem, smem],
        out_specs=[vmem, vmem],
    )(*(array.reshape(-1, lanes) for array in (reading, precision, position)), tally, adjacent)


def copied(copies):
    for copy in copies:
        copy.start()
    return copies


def first_part_kernel(fields_ref, given_ref, sent_ref, held_ref, edges_ref, position_ref, sems):
    devices, rows, size = sent_ref.shape
    cells = fields_ref.shape[1] // devices
    span = PARTITION_SPAN
    half = R * span
    split = size - span
    amount = cells // span
    copies = []

    def add(start, length, target):
        source = fields_ref.at[:, pl.ds(start, length)]
        copies.append(pltpu.make_async_copy(source, target, sems.at[len(copies)]))

    for device in range(devices):
        add((device + 1) * cells - half, half, edges_ref.at[device, :, pl.ds(0, half)])
        add(device * cells, half, edges_ref.at[device, :, pl.ds(half, half)])
    copies.append(pltpu.make_async_copy(given_ref, position_ref, sems.at[len(copies)]))
    ahead = len(copies)
    for device in range(devices):
        add(device * cells, split, held_ref.at[device, :, pl.ds(0, split)])
    copied(copies)
    for copy in copies[:ahead]:
        copy.wait()

    def shifted(array, distance):
        if distance > 0:
            return jnp.concatenate([array[:distance], array[:-distance]], axis=0)
        return jnp.concatenate([array[-distance:], array[distance:]], axis=0)

    beyond = [(amount - R + spot, 1) for spot in range(R)] + [(spot, -1) for spot in range(R)]
    positions = position_ref[...].T.reshape(devices, amount, OB)
    position = jnp.concatenate([shifted(positions[:, block], distance) for block, distance in beyond], axis=1)
    position = jnp.broadcast_to(position[:, None], (devices, rows, span)).reshape(devices * rows, span)
    fields = [
        shifted(edges_ref[:, :, spot * span : (spot + 1) * span].reshape(devices * rows, span), distance * rows)
        for spot, (_, distance) in enumerate(beyond)
    ]
    held_ref[:, :, split:] = picked(fields, position).reshape(devices, rows, span)
    out = []
    for device, copy in enumerate(copies[ahead:]):
        copy.wait()
        if device % INNER == INNER - 1:
            some = pl.ds(device + 1 - INNER, INNER)
            sem = sems.at[len(copies) + len(out)]
            out += copied([pltpu.make_async_copy(held_ref.at[some], sent_ref.at[some], sem)])
    for copy in out:
        copy.wait()


def second_part_kernel(split, fields_ref, *refs):
    *sent, sems = refs
    place = lax.axis_index("state")
    rows = fields_ref.shape[0]
    size = sent[0].shape[1]
    cells = split + size
    copies = []
    for near, array in enumerate(sent):
        for far in range(array.shape[0] // rows):
            start = (place ^ (far * INNER + near)) * cells + split
            source = fields_ref.at[:, pl.ds(pl.multiple_of(start, PARTITION_SPAN), size)]
            target = array.at[pl.ds(far * rows, rows), :]
            copies.append(pltpu.make_async_copy(source, target, sems.at[len(copies)]))
    for copy in copied(copies):
        copy.wait()


def turn_kernel(rows, *refs):
    given, made = refs[: len(refs) // 2], refs[len(refs) // 2 :]
    for i, source in enumerate(given):
        for j, target in enumerate(made):
            target[i * rows : (i + 1) * rows, :] = source[j * rows : (j + 1) * rows, :]


def place_moves(moves, sems):
    started = [pltpu.make_async_copy(*move, sems.at[index]) for index, move in enumerate(moves)]
    for copy in started:
        copy.start()
    for copy in started:
        copy.wait()


def place_kernel(cells, *refs):
    *parts, result_ref, sems = refs
    firsts, seconds = parts[:-INNER], parts[-INNER:]
    place = lax.axis_index("state")
    rows = result_ref.shape[0]
    width = QUAD * PARTITION_SPAN
    moves = []

    def add(source, distance, start):
        target = result_ref.at[:, pl.ds(pl.multiple_of((place ^ distance) * cells + start, width), width)]
        moves.append((source, target))

    for far, part in enumerate(firsts):
        for near in range(INNER):
            add(part.at[pl.ds(near * rows, rows), pl.ds(0, width)], far * INNER + near, 0)
    for near, part in enumerate(seconds):
        for far in range(len(firsts)):
            add(part.at[pl.ds(far * rows, rows), :], far * INNER + near, width)
    place_moves(moves, sems)


def place_last_kernel(cells, last_ref, _, result_ref, sems):
    rows = result_ref.shape[0]
    size = last_ref.shape[1]
    moves = []
    for device in range(last_ref.shape[0] // rows):
        target = result_ref.at[:, pl.ds((device + 1) * cells - size, size)]
        moves.append((last_ref.at[pl.ds(device * rows, rows), :], target))
    place_moves(moves, sems)


def join_kernel(rows, *refs):
    near, refs = refs[:INNER], refs[INNER:]
    given, made = refs[: len(refs) // 2], refs[len(refs) // 2 :]
    width = near[0].shape[1]
    for far, (source, target) in enumerate(zip(given, made)):
        for i, part in enumerate(near):
            target[i * rows : (i + 1) * rows, :width] = part[far * rows : (far + 1) * rows, :]
        target[:, width:] = source[...]


def reordered(ref, devices, near_first):
    place = lax.axis_index("state")
    rows = ref.shape[0] // devices
    order = list(range(devices))
    if near_first:
        order.sort(key=lambda distance: (distance % INNER, distance // INNER))
    starts = [pl.multiple_of((place ^ distance) * rows, rows) for distance in order]
    return jnp.concatenate([ref[pl.ds(start, rows), :] for start in starts], axis=0)


def blocks_of(fields, here, there, first, terms_ref):
    span = PARTITION_SPAN
    seen = jnp.concatenate([here, there], axis=1)
    blocks = []
    for spot in range(QUAD):
        root_weight, reading = (terms_ref[term, pl.ds(first + spot, 1), :] for term in range(2))
        blocks.append((fields[:, spot * span : (spot + 1) * span], seen, root_weight, reading))
    return blocks


def head_kernel(quad, devices, fields_ref, here_ref, there_ref, terms_ref, *results):
    span = PARTITION_SPAN
    fields, here, there = [reordered(ref, devices, quad == 0) for ref in (fields_ref, here_ref, there_ref)]
    for spot, result in enumerate(updated(blocks_of(fields, here, there, quad * QUAD, terms_ref))):
        start = 0
        for result_ref in results:
            rows = result_ref.shape[0]
            result_ref[:, spot * span : (spot + 1) * span] = result[start : start + rows]
            start += rows


def tail_kernel(first_ref, begin_ref, end_ref, here_ref, tiles_ref, terms_ref, result_ref):
    span = PARTITION_SPAN
    step = pl.program_id(0)
    begin = jnp.where(step == 0, first_ref[...], begin_ref[...])
    fields = jnp.concatenate([begin, end_ref[...]], axis=1)
    here = jnp.where(step == 0, here_ref[...], tiles_ref[:, :span])
    there = jnp.where(step == 0, tiles_ref[:, :span], tiles_ref[:, span:])
    first = terms_ref.shape[1] + (step - 2) * QUAD
    for spot, result in enumerate(updated(blocks_of(fields, here, there, first, terms_ref))):
        result_ref[:, spot * span : (spot + 1) * span] = result


def in_stages(fields, observations, devices):
    own_members, all_cells = fields.shape
    cells = all_cells // devices
    amount = cells // PARTITION_SPAN
    members = own_members * devices
    outer = devices // INNER
    quads = amount // QUAD
    width = QUAD * PARTITION_SPAN
    lanes = QUAD * OB
    early = quads - 2
    late = 2
    half = R * PARTITION_SPAN
    anywhere = pl.BlockSpec(memory_space=pl.ANY)
    vmem = pl.BlockSpec(memory_space=pltpu.VMEM)

    def call(kernel, inputs, outputs, grant=16, cost=1, **options):
        return pl.pallas_call(
            kernel,
            out_shape=outputs,
            in_specs=inputs,
            compiler_params=pltpu.CompilerParams(vmem_limit_bytes=grant << 20),
            cost_estimate=pl.CostEstimate(flops=cost, bytes_accessed=1, transcendentals=0),
            **options,
        )

    def columns(size, index):
        return pl.BlockSpec((members, size), lambda step: (0, index))

    def full(array):
        return pl.BlockSpec(array.shape, lambda step: (0,) * array.ndim)

    def group(parts, size):
        return jax.ShapeDtypeStruct((members // parts, size), jnp.float32)

    def swapped(arrays, unit):
        pairs = [[(i, i ^ (unit * k)) for i in range(devices)] for k in range(len(arrays))]
        return [arrays[0]] + [lax.ppermute(arrays[k], "state", pairs[k]) for k in range(1, len(arrays))]

    def second_parts():
        return call(
            functools.partial(second_part_kernel, split),
            [anywhere],
            [group(INNER, cells - split)] * INNER,
            out_specs=[vmem] * INNER,
            scratch_shapes=[pltpu.SemaphoreType.DMA((devices,))],
        )(fields)

    def turned(arrays, parts, cost=1):
        return call(
            functools.partial(turn_kernel, own_members),
            [vmem] * len(arrays),
            [group(parts, arrays[0].shape[1])] * parts,
            cost=cost,
            out_specs=[vmem] * parts,
        )(*arrays)

    def exchanged(array):
        return lax.all_to_all(array, "state", split_axis=0, concat_axis=0, tiled=True)

    split = early * width + half
    sent = call(
        first_part_kernel,
        [anywhere, anywhere],
        jax.ShapeDtypeStruct((devices, own_members, split + lanes), jnp.float32),
        grant=56,
        out_specs=anywhere,
        scratch_shapes=[
            pltpu.VMEM((devices, own_members, split + lanes), jnp.float32),
            pltpu.VMEM((devices, own_members, 2 * half), jnp.float32),
            pltpu.VMEM(observations[2].shape[::-1], jnp.int32),
            pltpu.SemaphoreType.DMA((3 * devices + outer + 1,)),
        ],
    )(fields, observations[2].T)
    first = exchanged(sent).reshape(members, split + lanes)
    second = turned(swapped(second_parts(), 1), outer)
    second, tied = lax.optimization_barrier((second, [observations[0],observations[3]]))
    observations = [tied[0], observations[1], observations[2], tied[1], observations[4]]
    terms, quad_position = window_terms(*observations, members)
    second, terms, quad_position = lax.optimization_barrier((second, terms, quad_position))
    second = swapped(second, INNER)
    seen = call(
        pick_first_kernel,
        [vmem, vmem],
        jax.ShapeDtypeStruct((members, (early + 1) * lanes), jnp.float32),
        out_specs=vmem,
    )(first, quad_position)

    def head(quad, parts, seen):
        return call(
            functools.partial(head_kernel, quad, devices),
            [columns(width, quad), columns(lanes, quad), columns(lanes, quad + 1), full(terms)],
            [group(parts, width)] * parts,
            grant=40,
            grid=(1,),
            out_specs=[pl.BlockSpec((members // parts, width), lambda step: (0, 0))] * parts,
        )(first, seen, seen, terms)

    groups = head(0, INNER, seen)
    seen, groups, second[1] = lax.optimization_barrier((seen, groups, second[1]))
    near = swapped(groups, 1)
    groups = head(1, outer, seen)
    away = call(
        functools.partial(join_kernel, own_members),
        [vmem] * (INNER + outer),
        [group(outer, 2 * width)] * outer,
        out_specs=[vmem] * outer,
    )(*near, *groups)
    away, second = lax.optimization_barrier((away, second))
    away = swapped(away, INNER)

    second, tiles = call(
        functools.partial(second_kernel, devices),
        [columns(lanes, split // lanes), *[full(array) for array in (quad_position, *second)]],
        [
            jax.ShapeDtypeStruct((members, cells - split), jnp.float32),
            jax.ShapeDtypeStruct((members, 2 * lanes), jnp.float32),
        ],
        grid=(1,),
        out_specs=[columns(cells - split, 0), columns(2 * lanes, 0)],
    )(first, quad_position, *second)
    ends = call(
        tail_kernel,
        [
            columns(half, split // half - 1),
            columns(half, 1),
            pl.BlockSpec((members, half), lambda step: (0, 2 * step)),
            columns(lanes, early),
            full(tiles),
            full(terms),
        ],
        jax.ShapeDtypeStruct((members, late * width), jnp.float32),
        grant=60,
        grid=(late,),
        out_specs=pl.BlockSpec((members, width), lambda step: (0, step)),
    )(first, second, second, seen, tiles, terms)
    ends = exchanged(ends.reshape(devices, own_members, late * width)).reshape(members, late * width)

    near = call(
        functools.partial(turn_kernel, own_members),
        [pl.BlockSpec((members // outer, width), lambda step: (0, 1))] * outer,
        [group(INNER, width)] * INNER,
        cost=1 << 36,
        grid=(1,),
        out_specs=[pl.BlockSpec((members // INNER, width), lambda step: (0, 0))] * INNER,
    )(*away)
    whole = jax.ShapeDtypeStruct((own_members, all_cells), jnp.float32)
    result = call(
        functools.partial(place_kernel, cells),
        [vmem] * (outer + INNER),
        whole,
        out_specs=anywhere,
        scratch_shapes=[pltpu.SemaphoreType.DMA((2 * devices,))],
    )(*away, *swapped(near, 1))
    return call(
        functools.partial(place_last_kernel, cells),
        [vmem, anywhere],
        whole,
        input_output_aliases={1: 0},
        out_specs=anywhere,
        scratch_shapes=[pltpu.SemaphoreType.DMA((devices,))],
    )(ends, result)


def by_all_to_all(fields, observations, devices):
    own_members, all_cells = fields.shape
    cells = all_cells // devices
    amount = cells // PARTITION_SPAN
    members = own_members * devices
    span = PARTITION_SPAN
    (root_weight, reading), quad_position = window_terms(*observations, members)
    sent = fields.reshape(own_members, devices, cells).transpose(1, 0, 2)
    fields = lax.all_to_all(sent, "state", split_axis=0, concat_axis=0, tiled=True).reshape(members, cells)
    vmem = pl.BlockSpec(memory_space=pltpu.VMEM)
    own_seen = pl.pallas_call(
        pick_kernel,
        out_shape=jax.ShapeDtypeStruct((members, amount * OB), jnp.float32),
        in_specs=[vmem, vmem],
        out_specs=vmem,
        compiler_params=pltpu.CompilerParams(vmem_limit_bytes=16 << 20),
    )(fields, quad_position)
    edge = own_seen[:, : QUAD * OB]
    before = lax.ppermute(edge, "state", [(i, i + 1) for i in range(devices - 1)])
    after = lax.ppermute(edge, "state", [(i + 1, i) for i in range(devices - 1)])
    steps = amount // QUAD

    def whole(*shape):
        return pl.BlockSpec(shape, lambda step: (0, 0))

    analysis = pl.pallas_call(
        update_kernel,
        grid=(steps,),
        out_shape=jax.ShapeDtypeStruct((members, cells), jnp.float32),
        in_specs=[
            pl.BlockSpec((members, QUAD * span), lambda step: (0, step)),
            whole(members, QUAD * OB),
            whole(members, amount * OB),
            whole(members, QUAD * OB),
            whole(amount, 2 * QUAD * OB),
            whole(amount, 2 * QUAD * OB),
        ],
        out_specs=pl.BlockSpec((members, QUAD * span), lambda step: (0, step)),
        compiler_params=pltpu.CompilerParams(vmem_limit_bytes=40 << 20),
    )(fields, before, own_seen, after, root_weight, reading)
    result = lax.all_to_all(
        analysis.reshape(devices, own_members, cells), "state", split_axis=0, concat_axis=0, tiled=True
    )
    return result.transpose(1, 0, 2).reshape(own_members, all_cells)


def body(
    background_draws_table,
    measurement_reading,
    measurement_precision,
    sensed_point_position,
    measurement_tally,
    adjacent_tile_number,
):
    devices = lax.axis_size("state")
    observations = (
        measurement_reading,
        measurement_precision,
        sensed_point_position,
        measurement_tally,
        adjacent_tile_number,
    )
    way = in_stages if devices == INNER * INNER else by_all_to_all
    return way(background_draws_table, observations, devices)


def solution(mesh):
    return jax.shard_map(
        body,
        mesh=mesh,
        in_specs=(
            P("state", "groups"),
            P("groups", None),
            P("groups", None),
            P("groups", None),
            P("groups"),
            P(("groups", "state"), None),
        ),
        out_specs=P("state", "groups"),
        check_vma=False,
    )
```

```python
import functools

import jax
import jax.numpy as jnp
from jax import lax
from jax.experimental import pallas as pl
from jax.experimental.pallas import tpu as pltpu
from jax.sharding import PartitionSpec as P

PARTITION_SPAN = 128
OB = 32
R = 2
NS_ITERS = 5
LOC = 128

QUAD = PARTITION_SPAN // OB
INNER = 4
NN = (((1,), (0,)), ((), ()))
NT = (((1,), (1,)), ((), ()))


def halves(values):
    high = values.astype(jnp.bfloat16)
    return high, (values - high.astype(jnp.float32)).astype(jnp.bfloat16)


def times(left, right, dims):
    (left_high, left_low), (right_high, right_low) = left, right
    return lax.dot_general(
        jnp.concatenate([left_high, left_high, left_low], axis=1),
        jnp.concatenate([right_high, right_low, right_high], axis=dims[0][1][0]),
        dims,
        preferred_element_type=jnp.float32,
    )


def updated(blocks):
    turns = [analysis(*block) for block in blocks]
    results = [None] * len(turns)
    while None in results:
        for index, turn in enumerate(turns):
            if results[index] is None:
                results[index] = next(turn)
    return results


def analysis(fields, seen, root_weight, reading):
    seen_mean = jnp.mean(seen, axis=0, keepdims=True)
    pull = (reading - seen_mean) * root_weight
    root = halves((seen - seen_mean) * root_weight)
    spread = times(root, root, NT)
    pull = times(halves(jnp.broadcast_to(pull, (16, pull.shape[1]))), root, NT)
    yield None
    squares = jnp.sum(jnp.sum(spread * spread, axis=0, keepdims=True), axis=1, keepdims=True)
    norm_size = 1.0 + jnp.sqrt(squares)
    unit = 1.0 / norm_size
    rest = spread * (-0.5 * unit)
    cells = fields.T
    centre = jnp.mean(cells, axis=1, keepdims=True)
    chain = jnp.concatenate([cells - centre, pull], axis=0)
    for sweep in range(NS_ITERS - 1):
        parts = halves(rest)
        gain = 1.5 - 0.5 * unit
        if sweep < NS_ITERS - 2:
            square = times(parts, parts, NN)
        moved = times(halves(chain), parts, NN)
        yield None
        if sweep < NS_ITERS - 2:
            once = (gain - 0.5 * unit) * rest + square
            cubic = times(halves(once), parts, NN)
        chain = gain * chain + moved
        if sweep < NS_ITERS - 2:
            yield None
            rest = gain * once - (0.5 * unit * gain) * rest + cubic
            unit = unit * gain * gain
    moved = times(halves(chain), parts, NN)
    yield None
    end = (-0.5 * unit) * chain + moved
    for _ in range(2):
        moved = times(halves(end), parts, NN)
        yield None
        end = gain * end + moved
    chain = (1.5 * chain + end) * lax.rsqrt(norm_size)
    moved = chain[:PARTITION_SPAN]
    shift = jnp.sum(moved * chain[PARTITION_SPAN : PARTITION_SPAN + 1], axis=1, keepdims=True)
    yield (moved + (centre + shift)).T


def picked(fields, position):
    members = fields[0].shape[0]
    span = PARTITION_SPAN
    index = jnp.broadcast_to(position, (members, span))
    lanes = lax.broadcasted_iota(jnp.int32, (members, span), 1)
    total = None
    for spot, field in enumerate(fields):
        found = jnp.take_along_axis(field, index, axis=1)
        total = found if spot == 0 else jnp.where(lanes // OB == spot, found, total)
    return total


def pick_kernel(fields_ref, position_ref, seen_ref):
    span = PARTITION_SPAN
    quads = position_ref.shape[0]
    amount = quads * QUAD
    for quad in range(quads):
        blocks = [(quad * QUAD + spot - R) % amount for spot in range(QUAD)]
        fields = [fields_ref[:, block * span : (block + 1) * span] for block in blocks]
        seen_ref[:, quad * span : (quad + 1) * span] = picked(fields, position_ref[quad : quad + 1, :])


def pick_first_kernel(fields_ref, position_ref, seen_ref):
    span = PARTITION_SPAN
    amount = fields_ref.shape[1] // span - 1
    beyond = fields_ref[:, amount * span :]
    low = lax.broadcasted_iota(jnp.int32, beyond.shape, 1) < R * OB
    for quad in range(seen_ref.shape[1] // span):
        blocks = [max(quad * QUAD + spot - R, 0) for spot in range(QUAD)]
        fields = [fields_ref[:, block * span : (block + 1) * span] for block in blocks]
        found = picked(fields, position_ref[quad : quad + 1, :])
        seen_ref[:, quad * span : (quad + 1) * span] = found if quad else jnp.where(low, beyond, found)


def second_kernel(devices, beyond_ref, position_ref, *refs):
    *parts, fields_ref, seen_ref = refs
    parts = parts[::-1]
    place = lax.axis_index("state")
    span = PARTITION_SPAN
    quads = position_ref.shape[0]
    rows = fields_ref.shape[0] // devices
    for distance in range(devices):
        far, near = divmod(distance, INNER)
        start = pl.multiple_of((place ^ distance) * rows, rows)
        fields_ref[pl.ds(start, rows), :] = parts[far][near * rows : (near + 1) * rows, :]
    amount = fields_ref.shape[1] // span
    low = lax.broadcasted_iota(jnp.int32, beyond_ref.shape, 1) < R * OB
    for index in range(seen_ref.shape[1] // span):
        blocks = [min(index * QUAD + spot, amount - 1) for spot in range(QUAD)]
        fields = [fields_ref[:, block * span : (block + 1) * span] for block in blocks]
        quad = (quads - seen_ref.shape[1] // span + 1 + index) % quads
        found = picked(fields, position_ref[quad : quad + 1, :])
        seen_ref[:, index * span : (index + 1) * span] = found if quad else jnp.where(low, found, beyond_ref[...])


def update_kernel(fields_ref, before_ref, own_ref, after_ref, weight_ref, reading_ref, result_ref):
    members, span = before_ref.shape
    step = pl.program_id(0)
    steps = pl.num_programs(0)
    lanes = lax.broadcasted_iota(jnp.int32, (members, span), 1)
    here = own_ref[:, pl.ds(pl.multiple_of(step * span, span), span)]
    following = own_ref[:, pl.ds(pl.multiple_of(lax.rem(step + 1, steps) * span, span), span)]
    first = jnp.where((step == 0) & (lanes < R * OB), before_ref[...], here)
    second = jnp.where((step == steps - 1) & (lanes >= R * OB), after_ref[...], following)
    seen = jnp.concatenate([first, second], axis=1)
    blocks = [
        (
            fields_ref[:, spot * span : (spot + 1) * span],
            seen,
            weight_ref[pl.ds(step * QUAD + spot, 1), :],
            reading_ref[pl.ds(step * QUAD + spot, 1), :],
        )
        for spot in range(QUAD)
    ]
    for spot, result in enumerate(updated(blocks)):
        result_ref[:, spot * span : (spot + 1) * span] = result


def terms_kernel(
    amount, members, reading_ref, precision_ref, position_ref, tally_ref, adjacent_ref, terms_ref, quad_ref
):
    first_block = lax.axis_index("state") * amount
    total = tally_ref.shape[0]
    quads = amount // QUAD
    span = PARTITION_SPAN
    lane = lax.broadcasted_iota(jnp.int32, (1, span), 1)
    low = lane < R * OB

    def tile(ref, quad):
        row = first_block // QUAD + quad
        before = ref[pl.ds(jnp.maximum(row - 1, 0), 1), :]
        after = ref[pl.ds(jnp.minimum(row, total // QUAD - 1), 1), :]
        return pltpu.roll(jnp.where(low, after, before), R * OB, 1)

    def counts(quad):
        found = jnp.zeros((1, span), jnp.int32)
        for spot in range(QUAD):
            block = jnp.clip(first_block + quad * QUAD + spot - R, 0, total - 1)
            found = jnp.where(lane // OB == spot, tally_ref[block], found)
        return found

    def pair(tiles, quad):
        return jnp.concatenate(tiles[quad : quad + 2], axis=1)

    positions = [tile(position_ref, quad) for quad in range(quads + 1)]
    readings = [tile(reading_ref, quad) for quad in range(quads + 1)]
    precisions = [tile(precision_ref, quad) for quad in range(quads + 1)]
    tallies = [counts(quad) for quad in range(quads + 1)]
    wide = lax.broadcasted_iota(jnp.int32, (1, 2 * span), 1)
    for block in range(amount):
        quad, spot = divmod(block, QUAD)
        neighbour = wide // OB - spot
        usable = jnp.zeros((1, 2 * span), jnp.float32)
        for j in range(2 * R + 1):
            there = jnp.where(adjacent_ref[block, j] >= 0, 1.0, 0.0)
            usable = jnp.where(neighbour == j, there, usable)
        distance = (
            ((neighbour - R) * span).astype(jnp.float32)
            + pair(positions, quad).astype(jnp.float32)
            - 0.5 * (span - 1)
        )
        decay = jnp.exp(-0.5 * (distance / LOC) ** 2)
        active = jnp.where(wide % OB < pair(tallies, quad), usable, 0.0)
        weight = pair(precisions, quad) * decay * active
        terms_ref[0, block : block + 1, :] = jnp.sqrt(weight / (members - 1.0))
        terms_ref[1, block : block + 1, :] = pair(readings, quad)
    edge = jnp.where(low, positions[quads], positions[0])
    for quad in range(quads):
        quad_ref[quad : quad + 1, :] = positions[quad] if quad else edge


def window_terms(reading, precision, position, tally, adjacent, members):
    amount = adjacent.shape[0]
    lanes = QUAD * OB
    vmem = pl.BlockSpec(memory_space=pltpu.VMEM)
    smem = pl.BlockSpec(memory_space=pltpu.SMEM)
    terms = jax.ShapeDtypeStruct((2, amount, 2 * lanes), jnp.float32)
    return pl.pallas_call(
        functools.partial(terms_kernel, amount, members),
        out_shape=[terms, jax.ShapeDtypeStruct((amount // QUAD, lanes), jnp.int32)],
        in_specs=[vmem, vmem, vmem, smem, smem],
        out_specs=[vmem, vmem],
    )(*(array.reshape(-1, lanes) for array in (reading, precision, position)), tally, adjacent)


def copied(copies):
    for copy in copies:
        copy.start()
    return copies


def first_part_kernel(fields_ref, given_ref, sent_ref, held_ref, edges_ref, position_ref, sems):
    devices, rows, size = sent_ref.shape
    cells = fields_ref.shape[1] // devices
    span = PARTITION_SPAN
    half = R * span
    split = size - span
    amount = cells // span
    copies = []

    def add(start, length, target):
        source = fields_ref.at[:, pl.ds(start, length)]
        copies.append(pltpu.make_async_copy(source, target, sems.at[len(copies)]))

    for device in range(devices):
        add((device + 1) * cells - half, half, edges_ref.at[device, :, pl.ds(0, half)])
        add(device * cells, half, edges_ref.at[device, :, pl.ds(half, half)])
    copies.append(pltpu.make_async_copy(given_ref, position_ref, sems.at[len(copies)]))
    ahead = len(copies)
    for device in range(devices):
        add(device * cells, split, held_ref.at[device, :, pl.ds(0, split)])
    copied(copies)
    for copy in copies[:ahead]:
        copy.wait()

    def shifted(array, distance):
        if distance > 0:
            return jnp.concatenate([array[:distance], array[:-distance]], axis=0)
        return jnp.concatenate([array[-distance:], array[distance:]], axis=0)

    beyond = [(amount - R + spot, 1) for spot in range(R)] + [(spot, -1) for spot in range(R)]
    positions = position_ref[...].T.reshape(devices, amount, OB)
    position = jnp.concatenate([shifted(positions[:, block], distance) for block, distance in beyond], axis=1)
    position = jnp.broadcast_to(position[:, None], (devices, rows, span)).reshape(devices * rows, span)
    fields = [
        shifted(edges_ref[:, :, spot * span : (spot + 1) * span].reshape(devices * rows, span), distance * rows)
        for spot, (_, distance) in enumerate(beyond)
    ]
    held_ref[:, :, split:] = picked(fields, position).reshape(devices, rows, span)
    out = []
    for device, copy in enumerate(copies[ahead:]):
        copy.wait()
        if device % INNER == INNER - 1:
            some = pl.ds(device + 1 - INNER, INNER)
            sem = sems.at[len(copies) + len(out)]
            out += copied([pltpu.make_async_copy(held_ref.at[some], sent_ref.at[some], sem)])
    for copy in out:
        copy.wait()


def second_part_kernel(split, fields_ref, *refs):
    *sent, sems = refs
    place = lax.axis_index("state")
    rows = fields_ref.shape[0]
    size = sent[0].shape[1]
    cells = split + size
    copies = []
    for near, array in enumerate(sent):
        for far in range(array.shape[0] // rows):
            start = (place ^ (far * INNER + near)) * cells + split
            source = fields_ref.at[:, pl.ds(pl.multiple_of(start, PARTITION_SPAN), size)]
            target = array.at[pl.ds(far * rows, rows), :]
            copies.append(pltpu.make_async_copy(source, target, sems.at[len(copies)]))
    for copy in copied(copies):
        copy.wait()


def turn_kernel(rows, *refs):
    given, made = refs[: len(refs) // 2][::-1], refs[len(refs) // 2 :]
    for i, source in enumerate(given):
        for j, target in enumerate(made):
            target[i * rows : (i + 1) * rows, :] = source[j * rows : (j + 1) * rows, :]


def place_moves(moves, sems):
    started = [pltpu.make_async_copy(*move, sems.at[index]) for index, move in enumerate(moves)]
    for copy in started:
        copy.start()
    for copy in started:
        copy.wait()


def place_kernel(cells, *refs):
    *parts, result_ref, sems = refs
    firsts, seconds = parts[:-INNER], parts[-INNER:]
    place = lax.axis_index("state")
    rows = result_ref.shape[0]
    width = QUAD * PARTITION_SPAN
    moves = []

    def add(source, distance, start):
        target = result_ref.at[:, pl.ds(pl.multiple_of((place ^ distance) * cells + start, width), width)]
        moves.append((source, target))

    for far, part in enumerate(firsts):
        for near in range(INNER):
            add(part.at[pl.ds(near * rows, rows), pl.ds(0, width)], far * INNER + near, 0)
    for near, part in enumerate(seconds):
        for far in range(len(firsts)):
            add(part.at[pl.ds(far * rows, rows), :], far * INNER + near, width)
    place_moves(moves, sems)


def place_last_kernel(cells, last_ref, _, result_ref, sems):
    rows = result_ref.shape[0]
    size = last_ref.shape[1]
    moves = []
    for device in range(last_ref.shape[0] // rows):
        target = result_ref.at[:, pl.ds((device + 1) * cells - size, size)]
        moves.append((last_ref.at[pl.ds(device * rows, rows), :], target))
    place_moves(moves, sems)


def join_kernel(rows, *refs):
    near, refs = refs[:INNER], refs[INNER:]
    given, made = refs[: len(refs) // 2], refs[len(refs) // 2 :]
    width = near[0].shape[1]
    for far, (source, target) in enumerate(zip(given, made)):
        for i, part in enumerate(near):
            target[i * rows : (i + 1) * rows, :width] = part[far * rows : (far + 1) * rows, :]
        target[:, width:] = source[...]


def reordered(ref, devices, near_first):
    place = lax.axis_index("state")
    rows = ref.shape[0] // devices
    order = list(range(devices))
    if near_first:
        order.sort(key=lambda distance: (distance % INNER, distance // INNER))
    starts = [pl.multiple_of((place ^ distance) * rows, rows) for distance in order]
    return jnp.concatenate([ref[pl.ds(start, rows), :] for start in starts], axis=0)


def blocks_of(fields, here, there, first, terms_ref):
    span = PARTITION_SPAN
    seen = jnp.concatenate([here, there], axis=1)
    blocks = []
    for spot in range(QUAD):
        root_weight, reading = (terms_ref[term, pl.ds(first + spot, 1), :] for term in range(2))
        blocks.append((fields[:, spot * span : (spot + 1) * span], seen, root_weight, reading))
    return blocks


def head_kernel(quad, devices, fields_ref, here_ref, there_ref, terms_ref, *results):
    span = PARTITION_SPAN
    fields, here, there = [reordered(ref, devices, quad == 0) for ref in (fields_ref, here_ref, there_ref)]
    for spot, result in enumerate(updated(blocks_of(fields, here, there, quad * QUAD, terms_ref))):
        start = 0
        for result_ref in results:
            rows = result_ref.shape[0]
            result_ref[:, spot * span : (spot + 1) * span] = result[start : start + rows]
            start += rows


def tail_kernel(first_ref, begin_ref, end_ref, here_ref, tiles_ref, terms_ref, result_ref):
    span = PARTITION_SPAN
    step = pl.program_id(0)
    begin = jnp.where(step == 0, first_ref[...], begin_ref[...])
    fields = jnp.concatenate([begin, end_ref[...]], axis=1)
    here = jnp.where(step == 0, here_ref[...], tiles_ref[:, :span])
    there = jnp.where(step == 0, tiles_ref[:, :span], tiles_ref[:, span:])
    first = terms_ref.shape[1] + (step - 2) * QUAD
    for spot, result in enumerate(updated(blocks_of(fields, here, there, first, terms_ref))):
        result_ref[:, spot * span : (spot + 1) * span] = result


def in_stages(fields, observations, devices):
    own_members, all_cells = fields.shape
    cells = all_cells // devices
    amount = cells // PARTITION_SPAN
    members = own_members * devices
    outer = devices // INNER
    quads = amount // QUAD
    width = QUAD * PARTITION_SPAN
    lanes = QUAD * OB
    early = quads - 2
    late = 2
    half = R * PARTITION_SPAN
    anywhere = pl.BlockSpec(memory_space=pl.ANY)
    vmem = pl.BlockSpec(memory_space=pltpu.VMEM)

    def call(kernel, inputs, outputs, grant=16, cost=1, **options):
        return pl.pallas_call(
            kernel,
            out_shape=outputs,
            in_specs=inputs,
            compiler_params=pltpu.CompilerParams(vmem_limit_bytes=grant << 20),
            cost_estimate=pl.CostEstimate(flops=cost, bytes_accessed=1, transcendentals=0),
            **options,
        )

    def columns(size, index):
        return pl.BlockSpec((members, size), lambda step: (0, index))

    def full(array):
        return pl.BlockSpec(array.shape, lambda step: (0,) * array.ndim)

    def group(parts, size):
        return jax.ShapeDtypeStruct((members // parts, size), jnp.float32)

    def swapped(arrays, unit):
        pairs = [[(i, i ^ (unit * k)) for i in range(devices)] for k in range(len(arrays))]
        far_first = [lax.ppermute(arrays[k], "state", pairs[k]) for k in reversed(range(1, len(arrays)))]
        return [arrays[0]] + far_first[::-1]

    def second_parts():
        return call(
            functools.partial(second_part_kernel, split),
            [anywhere],
            [group(INNER, cells - split)] * INNER,
            out_specs=[vmem] * INNER,
            scratch_shapes=[pltpu.SemaphoreType.DMA((devices,))],
        )(fields)

    def turned(arrays, parts, cost=1):
        return call(
            functools.partial(turn_kernel, own_members),
            [vmem] * len(arrays),
            [group(parts, arrays[0].shape[1])] * parts,
            cost=cost,
            out_specs=[vmem] * parts,
        )(*arrays[::-1])

    def exchanged(array):
        return lax.all_to_all(array, "state", split_axis=0, concat_axis=0, tiled=True)

    split = early * width + half
    sent = call(
        first_part_kernel,
        [anywhere, anywhere],
        jax.ShapeDtypeStruct((devices, own_members, split + lanes), jnp.float32),
        grant=56,
        out_specs=anywhere,
        scratch_shapes=[
            pltpu.VMEM((devices, own_members, split + lanes), jnp.float32),
            pltpu.VMEM((devices, own_members, 2 * half), jnp.float32),
            pltpu.VMEM(observations[2].shape[::-1], jnp.int32),
            pltpu.SemaphoreType.DMA((3 * devices + outer + 1,)),
        ],
    )(fields, observations[2].T)
    first = exchanged(sent).reshape(members, split + lanes)
    second = turned(swapped(second_parts(), 1), outer)
    second, tied = lax.optimization_barrier((second, [observations[0],observations[3]]))
    observations = [tied[0], observations[1], observations[2], tied[1], observations[4]]
    terms, quad_position = window_terms(*observations, members)
    second, terms, quad_position = lax.optimization_barrier((second, terms, quad_position))
    second = swapped(second, INNER)
    seen = call(
        pick_first_kernel,
        [vmem, vmem],
        jax.ShapeDtypeStruct((members, (early + 1) * lanes), jnp.float32),
        out_specs=vmem,
    )(first, quad_position)

    def head(quad, parts, seen):
        return call(
            functools.partial(head_kernel, quad, devices),
            [columns(width, quad), columns(lanes, quad), columns(lanes, quad + 1), full(terms)],
            [group(parts, width)] * parts,
            grant=40,
            grid=(1,),
            out_specs=[pl.BlockSpec((members // parts, width), lambda step: (0, 0))] * parts,
        )(first, seen, seen, terms)

    groups = head(0, INNER, seen)
    seen, groups, second[1] = lax.optimization_barrier((seen, groups, second[1]))
    near = swapped(groups, 1)
    groups = head(1, outer, seen)
    away = call(
        functools.partial(join_kernel, own_members),
        [vmem] * (INNER + outer),
        [group(outer, 2 * width)] * outer,
        out_specs=[vmem] * outer,
    )(*near, *groups)
    away, second = lax.optimization_barrier((away, second))
    away = swapped(away, INNER)

    second, tiles = call(
        functools.partial(second_kernel, devices),
        [columns(lanes, split // lanes), *[full(array) for array in (quad_position, *second[::-1])]],
        [
            jax.ShapeDtypeStruct((members, cells - split), jnp.float32),
            jax.ShapeDtypeStruct((members, 2 * lanes), jnp.float32),
        ],
        grid=(1,),
        out_specs=[columns(cells - split, 0), columns(2 * lanes, 0)],
    )(first, quad_position, *second[::-1])
    ends = call(
        tail_kernel,
        [
            columns(half, split // half - 1),
            columns(half, 1),
            pl.BlockSpec((members, half), lambda step: (0, 2 * step)),
            columns(lanes, early),
            full(tiles),
            full(terms),
        ],
        jax.ShapeDtypeStruct((members, late * width), jnp.float32),
        grant=40,
        grid=(late,),
        out_specs=pl.BlockSpec((members, width), lambda step: (0, step)),
    )(first, second, second, seen, tiles, terms)
    ends = exchanged(ends.reshape(devices, own_members, late * width)).reshape(members, late * width)

    near = call(
        functools.partial(turn_kernel, own_members),
        [pl.BlockSpec((members // outer, width), lambda step: (0, 1))] * outer,
        [group(INNER, width)] * INNER,
        cost=1 << 36,
        grid=(1,),
        out_specs=[pl.BlockSpec((members // INNER, width), lambda step: (0, 0))] * INNER,
    )(*away[::-1])
    whole = jax.ShapeDtypeStruct((own_members, all_cells), jnp.float32)
    result = call(
        functools.partial(place_kernel, cells),
        [vmem] * (outer + INNER),
        whole,
        out_specs=anywhere,
        scratch_shapes=[pltpu.SemaphoreType.DMA((2 * devices,))],
    )(*away, *swapped(near, 1))
    return call(
        functools.partial(place_last_kernel, cells),
        [vmem, anywhere],
        whole,
        input_output_aliases={1: 0},
        out_specs=anywhere,
        scratch_shapes=[pltpu.SemaphoreType.DMA((devices,))],
    )(ends, result)


def by_all_to_all(fields, observations, devices):
    own_members, all_cells = fields.shape
    cells = all_cells // devices
    amount = cells // PARTITION_SPAN
    members = own_members * devices
    span = PARTITION_SPAN
    (root_weight, reading), quad_position = window_terms(*observations, members)
    sent = fields.reshape(own_members, devices, cells).transpose(1, 0, 2)
    fields = lax.all_to_all(sent, "state", split_axis=0, concat_axis=0, tiled=True).reshape(members, cells)
    vmem = pl.BlockSpec(memory_space=pltpu.VMEM)
    own_seen = pl.pallas_call(
        pick_kernel,
        out_shape=jax.ShapeDtypeStruct((members, amount * OB), jnp.float32),
        in_specs=[vmem, vmem],
        out_specs=vmem,
        compiler_params=pltpu.CompilerParams(vmem_limit_bytes=16 << 20),
    )(fields, quad_position)
    edge = own_seen[:, : QUAD * OB]
    before = lax.ppermute(edge, "state", [(i, i + 1) for i in range(devices - 1)])
    after = lax.ppermute(edge, "state", [(i + 1, i) for i in range(devices - 1)])
    steps = amount // QUAD

    def whole(*shape):
        return pl.BlockSpec(shape, lambda step: (0, 0))

    analysis = pl.pallas_call(
        update_kernel,
        grid=(steps,),
        out_shape=jax.ShapeDtypeStruct((members, cells), jnp.float32),
        in_specs=[
            pl.BlockSpec((members, QUAD * span), lambda step: (0, step)),
            whole(members, QUAD * OB),
            whole(members, amount * OB),
            whole(members, QUAD * OB),
            whole(amount, 2 * QUAD * OB),
            whole(amount, 2 * QUAD * OB),
        ],
        out_specs=pl.BlockSpec((members, QUAD * span), lambda step: (0, step)),
        compiler_params=pltpu.CompilerParams(vmem_limit_bytes=40 << 20),
    )(fields, before, own_seen, after, root_weight, reading)
    result = lax.all_to_all(
        analysis.reshape(devices, own_members, cells), "state", split_axis=0, concat_axis=0, tiled=True
    )
    return result.transpose(1, 0, 2).reshape(own_members, all_cells)


def body(
    background_draws_table,
    measurement_reading,
    measurement_precision,
    sensed_point_position,
    measurement_tally,
    adjacent_tile_number,
):
    devices = lax.axis_size("state")
    observations = (
        measurement_reading,
        measurement_precision,
        sensed_point_position,
        measurement_tally,
        adjacent_tile_number,
    )
    way = in_stages if devices == INNER * INNER else by_all_to_all
    return way(background_draws_table, observations, devices)


def solution(mesh):
    return jax.shard_map(
        body,
        mesh=mesh,
        in_specs=(
            P("state", "groups"),
            P("groups", None),
            P("groups", None),
            P("groups", None),
            P("groups"),
            P(("groups", "state"), None),
        ),
        out_specs=P("state", "groups"),
        check_vma=False,
    )
```

```python
import functools

import jax
import jax.numpy as jnp
from jax import lax
from jax.experimental import pallas as pl
from jax.experimental.pallas import tpu as pltpu
from jax.sharding import PartitionSpec as P

PARTITION_SPAN = 128
OB = 32
R = 2
NS_ITERS = 5
LOC = 128

QUAD = PARTITION_SPAN // OB
INNER = 4
NN = (((1,), (0,)), ((), ()))
NT = (((1,), (1,)), ((), ()))


def halves(values):
    high = values.astype(jnp.bfloat16)
    return high, (values - high.astype(jnp.float32)).astype(jnp.bfloat16)


def times(left, right, dims):
    (left_high, left_low), (right_high, right_low) = left, right
    return lax.dot_general(
        jnp.concatenate([left_high, left_high, left_low], axis=1),
        jnp.concatenate([right_high, right_low, right_high], axis=dims[0][1][0]),
        dims,
        preferred_element_type=jnp.float32,
    )


def updated(blocks):
    turns = [analysis(*block) for block in blocks]
    results = [None] * len(turns)
    while None in results:
        for index, turn in enumerate(turns):
            if results[index] is None:
                results[index] = next(turn)
    return results


def analysis(fields, seen, root_weight, reading):
    seen_mean = jnp.mean(seen, axis=0, keepdims=True)
    pull = (reading - seen_mean) * root_weight
    root = halves((seen - seen_mean) * root_weight)
    spread = times(root, root, NT)
    pull = times(halves(jnp.broadcast_to(pull, (16, pull.shape[1]))), root, NT)
    yield None
    squares = jnp.sum(jnp.sum(spread * spread, axis=0, keepdims=True), axis=1, keepdims=True)
    norm_size = 1.0 + jnp.sqrt(squares)
    unit = 1.0 / norm_size
    rest = spread * (-0.5 * unit)
    cells = fields.T
    centre = jnp.mean(cells, axis=1, keepdims=True)
    chain = jnp.concatenate([cells - centre, pull], axis=0)
    for sweep in range(NS_ITERS - 1):
        parts = halves(rest)
        gain = 1.5 - 0.5 * unit
        if sweep < NS_ITERS - 2:
            square = times(parts, parts, NN)
        moved = times(halves(chain), parts, NN)
        yield None
        if sweep < NS_ITERS - 2:
            once = (gain - 0.5 * unit) * rest + square
            cubic = times(halves(once), parts, NN)
        chain = gain * chain + moved
        if sweep < NS_ITERS - 2:
            yield None
            rest = gain * once - (0.5 * unit * gain) * rest + cubic
            unit = unit * gain * gain
    moved = times(halves(chain), parts, NN)
    yield None
    end = (-0.5 * unit) * chain + moved
    for _ in range(2):
        moved = times(halves(end), parts, NN)
        yield None
        end = gain * end + moved
    chain = (1.5 * chain + end) * lax.rsqrt(norm_size)
    moved = chain[:PARTITION_SPAN]
    shift = jnp.sum(moved * chain[PARTITION_SPAN : PARTITION_SPAN + 1], axis=1, keepdims=True)
    yield (moved + (centre + shift)).T


def picked(fields, position):
    members = fields[0].shape[0]
    span = PARTITION_SPAN
    index = jnp.broadcast_to(position, (members, span))
    lanes = lax.broadcasted_iota(jnp.int32, (members, span), 1)
    total = None
    for spot, field in enumerate(fields):
        found = jnp.take_along_axis(field, index, axis=1)
        total = found if spot == 0 else jnp.where(lanes // OB == spot, found, total)
    return total


def pick_kernel(fields_ref, position_ref, seen_ref):
    span = PARTITION_SPAN
    quads = position_ref.shape[0]
    amount = quads * QUAD
    for quad in range(quads):
        blocks = [(quad * QUAD + spot - R) % amount for spot in range(QUAD)]
        fields = [fields_ref[:, block * span : (block + 1) * span] for block in blocks]
        seen_ref[:, quad * span : (quad + 1) * span] = picked(fields, position_ref[quad : quad + 1, :])


def pick_first_kernel(fields_ref, position_ref, seen_ref):
    span = PARTITION_SPAN
    amount = fields_ref.shape[1] // span - 1
    beyond = fields_ref[:, amount * span :]
    low = lax.broadcasted_iota(jnp.int32, beyond.shape, 1) < R * OB
    for quad in range(seen_ref.shape[1] // span):
        blocks = [max(quad * QUAD + spot - R, 0) for spot in range(QUAD)]
        fields = [fields_ref[:, block * span : (block + 1) * span] for block in blocks]
        found = picked(fields, position_ref[quad : quad + 1, :])
        seen_ref[:, quad * span : (quad + 1) * span] = found if quad else jnp.where(low, beyond, found)


def second_kernel(devices, beyond_ref, position_ref, *refs):
    *parts, fields_ref, seen_ref = refs
    parts = parts[::-1]
    place = lax.axis_index("state")
    span = PARTITION_SPAN
    quads = position_ref.shape[0]
    rows = fields_ref.shape[0] // devices
    for distance in range(devices):
        far, near = divmod(distance, INNER)
        start = pl.multiple_of((place ^ distance) * rows, rows)
        fields_ref[pl.ds(start, rows), :] = parts[far][near * rows : (near + 1) * rows, :]
    amount = fields_ref.shape[1] // span
    low = lax.broadcasted_iota(jnp.int32, beyond_ref.shape, 1) < R * OB
    for index in range(seen_ref.shape[1] // span):
        blocks = [min(index * QUAD + spot, amount - 1) for spot in range(QUAD)]
        fields = [fields_ref[:, block * span : (block + 1) * span] for block in blocks]
        quad = (quads - seen_ref.shape[1] // span + 1 + index) % quads
        found = picked(fields, position_ref[quad : quad + 1, :])
        seen_ref[:, index * span : (index + 1) * span] = found if quad else jnp.where(low, found, beyond_ref[...])


def update_kernel(fields_ref, before_ref, own_ref, after_ref, weight_ref, reading_ref, result_ref):
    members, span = before_ref.shape
    step = pl.program_id(0)
    steps = pl.num_programs(0)
    lanes = lax.broadcasted_iota(jnp.int32, (members, span), 1)
    here = own_ref[:, pl.ds(pl.multiple_of(step * span, span), span)]
    following = own_ref[:, pl.ds(pl.multiple_of(lax.rem(step + 1, steps) * span, span), span)]
    first = jnp.where((step == 0) & (lanes < R * OB), before_ref[...], here)
    second = jnp.where((step == steps - 1) & (lanes >= R * OB), after_ref[...], following)
    seen = jnp.concatenate([first, second], axis=1)
    blocks = [
        (
            fields_ref[:, spot * span : (spot + 1) * span],
            seen,
            weight_ref[pl.ds(step * QUAD + spot, 1), :],
            reading_ref[pl.ds(step * QUAD + spot, 1), :],
        )
        for spot in range(QUAD)
    ]
    for spot, result in enumerate(updated(blocks)):
        result_ref[:, spot * span : (spot + 1) * span] = result


def terms_kernel(
    amount, members, reading_ref, precision_ref, position_ref, tally_ref, adjacent_ref, terms_ref, quad_ref
):
    first_block = lax.axis_index("state") * amount
    total = tally_ref.shape[0]
    quads = amount // QUAD
    span = PARTITION_SPAN
    lane = lax.broadcasted_iota(jnp.int32, (1, span), 1)
    low = lane < R * OB

    def tile(ref, quad):
        row = first_block // QUAD + quad
        before = ref[pl.ds(jnp.maximum(row - 1, 0), 1), :]
        after = ref[pl.ds(jnp.minimum(row, total // QUAD - 1), 1), :]
        return pltpu.roll(jnp.where(low, after, before), R * OB, 1)

    def counts(quad):
        found = jnp.zeros((1, span), jnp.int32)
        for spot in range(QUAD):
            block = jnp.clip(first_block + quad * QUAD + spot - R, 0, total - 1)
            found = jnp.where(lane // OB == spot, tally_ref[block], found)
        return found

    def pair(tiles, quad):
        return jnp.concatenate(tiles[quad : quad + 2], axis=1)

    positions = [tile(position_ref, quad) for quad in range(quads + 1)]
    readings = [tile(reading_ref, quad) for quad in range(quads + 1)]
    precisions = [tile(precision_ref, quad) for quad in range(quads + 1)]
    tallies = [counts(quad) for quad in range(quads + 1)]
    wide = lax.broadcasted_iota(jnp.int32, (1, 2 * span), 1)
    for block in range(amount):
        quad, spot = divmod(block, QUAD)
        neighbour = wide // OB - spot
        usable = jnp.zeros((1, 2 * span), jnp.float32)
        for j in range(2 * R + 1):
            there = jnp.where(adjacent_ref[block, j] >= 0, 1.0, 0.0)
            usable = jnp.where(neighbour == j, there, usable)
        distance = (
            ((neighbour - R) * span).astype(jnp.float32)
            + pair(positions, quad).astype(jnp.float32)
            - 0.5 * (span - 1)
        )
        decay = jnp.exp(-0.5 * (distance / LOC) ** 2)
        active = jnp.where(wide % OB < pair(tallies, quad), usable, 0.0)
        weight = pair(precisions, quad) * decay * active
        terms_ref[0, block : block + 1, :] = jnp.sqrt(weight / (members - 1.0))
        terms_ref[1, block : block + 1, :] = pair(readings, quad)
    edge = jnp.where(low, positions[quads], positions[0])
    for quad in range(quads):
        quad_ref[quad : quad + 1, :] = positions[quad] if quad else edge


def window_terms(reading, precision, position, tally, adjacent, members):
    amount = adjacent.shape[0]
    lanes = QUAD * OB
    vmem = pl.BlockSpec(memory_space=pltpu.VMEM)
    smem = pl.BlockSpec(memory_space=pltpu.SMEM)
    terms = jax.ShapeDtypeStruct((2, amount, 2 * lanes), jnp.float32)
    return pl.pallas_call(
        functools.partial(terms_kernel, amount, members),
        out_shape=[terms, jax.ShapeDtypeStruct((amount // QUAD, lanes), jnp.int32)],
        in_specs=[vmem, vmem, vmem, smem, smem],
        out_specs=[vmem, vmem],
    )(*(array.reshape(-1, lanes) for array in (reading, precision, position)), tally, adjacent)


def copied(copies):
    for copy in copies:
        copy.start()
    return copies


def first_part_kernel(fields_ref, given_ref, sent_ref, held_ref, edges_ref, position_ref, sems):
    devices, rows, size = sent_ref.shape
    cells = fields_ref.shape[1] // devices
    span = PARTITION_SPAN
    half = R * span
    split = size - span
    amount = cells // span
    copies = []

    def add(start, length, target):
        source = fields_ref.at[:, pl.ds(start, length)]
        copies.append(pltpu.make_async_copy(source, target, sems.at[len(copies)]))

    for border in range(devices + 1):
        start = min(max(border * cells - half, 0), devices * cells - 2 * half)
        add(start, 2 * half, edges_ref.at[border])
    copies.append(pltpu.make_async_copy(given_ref, position_ref, sems.at[len(copies)]))
    ahead = len(copies)
    for device in range(devices):
        add(device * cells, split, held_ref.at[device, :, pl.ds(0, split)])
    copied(copies)
    for copy in copies[:ahead]:
        copy.wait()

    def shifted(array, distance):
        if distance > 0:
            return jnp.concatenate([array[:distance], array[:-distance]], axis=0)
        return jnp.concatenate([array[-distance:], array[distance:]], axis=0)

    beyond = [(amount - R + spot, 1) for spot in range(R)] + [(spot, -1) for spot in range(R)]
    positions = position_ref[...].T.reshape(devices, amount, OB)
    position = jnp.concatenate([shifted(positions[:, block], distance) for block, distance in beyond], axis=1)
    position = jnp.broadcast_to(position[:, None], (devices, rows, span)).reshape(devices * rows, span)
    fields = []
    for spot, (_, distance) in enumerate(beyond):
        first = 0 if distance > 0 else 1
        found = edges_ref[first : first + devices, :, spot * span : (spot + 1) * span]
        fields.append(found.reshape(devices * rows, span))
    held_ref[:, :, split:] = picked(fields, position).reshape(devices, rows, span)
    out = []
    for device, copy in enumerate(copies[ahead:]):
        copy.wait()
        if device % INNER == INNER - 1:
            some = pl.ds(device + 1 - INNER, INNER)
            sem = sems.at[len(copies) + len(out)]
            out += copied([pltpu.make_async_copy(held_ref.at[some], sent_ref.at[some], sem)])
    for copy in out:
        copy.wait()


def second_part_kernel(split, fields_ref, *refs):
    *sent, sems = refs
    place = lax.axis_index("state")
    rows = fields_ref.shape[0]
    size = sent[0].shape[1]
    cells = split + size
    copies = []
    for near, array in enumerate(sent):
        for far in range(array.shape[0] // rows):
            start = (place ^ (far * INNER + near)) * cells + split
            source = fields_ref.at[:, pl.ds(pl.multiple_of(start, PARTITION_SPAN), size)]
            target = array.at[pl.ds(far * rows, rows), :]
            copies.append(pltpu.make_async_copy(source, target, sems.at[len(copies)]))
    for copy in copied(copies):
        copy.wait()


def turn_kernel(rows, *refs):
    given, made = refs[: len(refs) // 2][::-1], refs[len(refs) // 2 :]
    for i, source in enumerate(given):
        for j, target in enumerate(made):
            target[i * rows : (i + 1) * rows, :] = source[j * rows : (j + 1) * rows, :]


def place_moves(moves, sems):
    started = [pltpu.make_async_copy(*move, sems.at[index]) for index, move in enumerate(moves)]
    for copy in started:
        copy.start()
    for copy in started:
        copy.wait()


def place_kernel(cells, *refs):
    *parts, result_ref, sems = refs
    firsts, seconds = parts[:-INNER], parts[-INNER:]
    place = lax.axis_index("state")
    rows = result_ref.shape[0]
    width = QUAD * PARTITION_SPAN
    moves = []

    def add(source, distance, start):
        target = result_ref.at[:, pl.ds(pl.multiple_of((place ^ distance) * cells + start, width), width)]
        moves.append((source, target))

    for far, part in enumerate(firsts):
        for near in range(INNER):
            add(part.at[pl.ds(near * rows, rows), pl.ds(0, width)], far * INNER + near, 0)
    for near, part in enumerate(seconds):
        for far in range(len(firsts)):
            add(part.at[pl.ds(far * rows, rows), :], far * INNER + near, width)
    place_moves(moves, sems)


def place_last_kernel(cells, last_ref, _, result_ref, sems):
    rows = result_ref.shape[0]
    size = last_ref.shape[1]
    moves = []
    for device in range(last_ref.shape[0] // rows):
        target = result_ref.at[:, pl.ds((device + 1) * cells - size, size)]
        moves.append((last_ref.at[pl.ds(device * rows, rows), :], target))
    place_moves(moves, sems)


def join_kernel(rows, *refs):
    near, refs = refs[:INNER], refs[INNER:]
    given, made = refs[: len(refs) // 2], refs[len(refs) // 2 :]
    width = near[0].shape[1]
    for far, (source, target) in enumerate(zip(given, made)):
        for i, part in enumerate(near):
            target[i * rows : (i + 1) * rows, :width] = part[far * rows : (far + 1) * rows, :]
        target[:, width:] = source[...]


def reordered(ref, devices, near_first):
    place = lax.axis_index("state")
    rows = ref.shape[0] // devices
    order = list(range(devices))
    if near_first:
        order.sort(key=lambda distance: (distance % INNER, distance // INNER))
    starts = [pl.multiple_of((place ^ distance) * rows, rows) for distance in order]
    return jnp.concatenate([ref[pl.ds(start, rows), :] for start in starts], axis=0)


def blocks_of(fields, here, there, first, terms_ref):
    span = PARTITION_SPAN
    seen = jnp.concatenate([here, there], axis=1)
    blocks = []
    for spot in range(QUAD):
        root_weight, reading = (terms_ref[term, pl.ds(first + spot, 1), :] for term in range(2))
        blocks.append((fields[:, spot * span : (spot + 1) * span], seen, root_weight, reading))
    return blocks


def head_kernel(quad, devices, fields_ref, here_ref, there_ref, terms_ref, *results):
    span = PARTITION_SPAN
    fields, here, there = [reordered(ref, devices, quad == 0) for ref in (fields_ref, here_ref, there_ref)]
    for spot, result in enumerate(updated(blocks_of(fields, here, there, quad * QUAD, terms_ref))):
        start = 0
        for result_ref in results:
            rows = result_ref.shape[0]
            result_ref[:, spot * span : (spot + 1) * span] = result[start : start + rows]
            start += rows


def tail_kernel(first_ref, begin_ref, end_ref, here_ref, tiles_ref, terms_ref, result_ref):
    span = PARTITION_SPAN
    step = pl.program_id(0)
    begin = jnp.where(step == 0, first_ref[...], begin_ref[...])
    fields = jnp.concatenate([begin, end_ref[...]], axis=1)
    here = jnp.where(step == 0, here_ref[...], tiles_ref[:, :span])
    there = jnp.where(step == 0, tiles_ref[:, :span], tiles_ref[:, span:])
    first = terms_ref.shape[1] + (step - 2) * QUAD
    for spot, result in enumerate(updated(blocks_of(fields, here, there, first, terms_ref))):
        result_ref[:, spot * span : (spot + 1) * span] = result


def in_stages(fields, observations, devices):
    own_members, all_cells = fields.shape
    cells = all_cells // devices
    amount = cells // PARTITION_SPAN
    members = own_members * devices
    outer = devices // INNER
    quads = amount // QUAD
    width = QUAD * PARTITION_SPAN
    lanes = QUAD * OB
    early = quads - 2
    late = 2
    half = R * PARTITION_SPAN
    anywhere = pl.BlockSpec(memory_space=pl.ANY)
    vmem = pl.BlockSpec(memory_space=pltpu.VMEM)

    def call(kernel, inputs, outputs, grant=16, cost=1, **options):
        return pl.pallas_call(
            kernel,
            out_shape=outputs,
            in_specs=inputs,
            compiler_params=pltpu.CompilerParams(vmem_limit_bytes=grant << 20),
            cost_estimate=pl.CostEstimate(flops=cost, bytes_accessed=1, transcendentals=0),
            **options,
        )

    def columns(size, index):
        return pl.BlockSpec((members, size), lambda step: (0, index))

    def full(array):
        return pl.BlockSpec(array.shape, lambda step: (0,) * array.ndim)

    def group(parts, size):
        return jax.ShapeDtypeStruct((members // parts, size), jnp.float32)

    def swapped(arrays, unit):
        pairs = [[(i, i ^ (unit * k)) for i in range(devices)] for k in range(len(arrays))]
        far_first = [lax.ppermute(arrays[k], "state", pairs[k]) for k in reversed(range(1, len(arrays)))]
        return [arrays[0]] + far_first[::-1]

    def second_parts():
        return call(
            functools.partial(second_part_kernel, split),
            [anywhere],
            [group(INNER, cells - split)] * INNER,
            out_specs=[vmem] * INNER,
            scratch_shapes=[pltpu.SemaphoreType.DMA((devices,))],
        )(fields)

    def turned(arrays, parts, cost=1):
        return call(
            functools.partial(turn_kernel, own_members),
            [vmem] * len(arrays),
            [group(parts, arrays[0].shape[1])] * parts,
            cost=cost,
            out_specs=[vmem] * parts,
        )(*arrays[::-1])

    def exchanged(array):
        return lax.all_to_all(array, "state", split_axis=0, concat_axis=0, tiled=True)

    split = early * width + half
    sent = call(
        first_part_kernel,
        [anywhere, anywhere],
        jax.ShapeDtypeStruct((devices, own_members, split + lanes), jnp.float32),
        grant=56,
        out_specs=anywhere,
        scratch_shapes=[
            pltpu.VMEM((devices, own_members, split + lanes), jnp.float32),
            pltpu.VMEM((devices + 1, own_members, 2 * half), jnp.float32),
            pltpu.VMEM(observations[2].shape[::-1], jnp.int32),
            pltpu.SemaphoreType.DMA((3 * devices + outer + 1,)),
        ],
    )(fields, observations[2].T)
    first = exchanged(sent).reshape(members, split + lanes)
    second = turned(swapped(second_parts(), 1), outer)
    second, tied = lax.optimization_barrier((second, [observations[0],observations[3]]))
    observations = [tied[0], observations[1], observations[2], tied[1], observations[4]]
    terms, quad_position = window_terms(*observations, members)
    second, terms, quad_position = lax.optimization_barrier((second, terms, quad_position))
    second = swapped(second, INNER)
    seen = call(
        pick_first_kernel,
        [vmem, vmem],
        jax.ShapeDtypeStruct((members, (early + 1) * lanes), jnp.float32),
        out_specs=vmem,
    )(first, quad_position)

    def head(quad, parts, seen):
        return call(
            functools.partial(head_kernel, quad, devices),
            [columns(width, quad), columns(lanes, quad), columns(lanes, quad + 1), full(terms)],
            [group(parts, width)] * parts,
            grant=40,
            grid=(1,),
            out_specs=[pl.BlockSpec((members // parts, width), lambda step: (0, 0))] * parts,
        )(first, seen, seen, terms)

    groups = head(0, INNER, seen)
    seen, groups, second[1] = lax.optimization_barrier((seen, groups, second[1]))
    near = swapped(groups, 1)
    groups = head(1, outer, seen)
    away = call(
        functools.partial(join_kernel, own_members),
        [vmem] * (INNER + outer),
        [group(outer, 2 * width)] * outer,
        out_specs=[vmem] * outer,
    )(*near, *groups)
    away, second = lax.optimization_barrier((away, second))
    away = swapped(away, INNER)

    second, tiles = call(
        functools.partial(second_kernel, devices),
        [columns(lanes, split // lanes), *[full(array) for array in (quad_position, *second[::-1])]],
        [
            jax.ShapeDtypeStruct((members, cells - split), jnp.float32),
            jax.ShapeDtypeStruct((members, 2 * lanes), jnp.float32),
        ],
        grid=(1,),
        out_specs=[columns(cells - split, 0), columns(2 * lanes, 0)],
    )(first, quad_position, *second[::-1])
    ends = call(
        tail_kernel,
        [
            columns(half, split // half - 1),
            columns(half, 1),
            pl.BlockSpec((members, half), lambda step: (0, 2 * step)),
            columns(lanes, early),
            full(tiles),
            full(terms),
        ],
        jax.ShapeDtypeStruct((members, late * width), jnp.float32),
        grant=40,
        grid=(late,),
        out_specs=pl.BlockSpec((members, width), lambda step: (0, step)),
    )(first, second, second, seen, tiles, terms)
    ends = exchanged(ends.reshape(devices, own_members, late * width)).reshape(members, late * width)

    near = call(
        functools.partial(turn_kernel, own_members),
        [pl.BlockSpec((members // outer, width), lambda step: (0, 1))] * outer,
        [group(INNER, width)] * INNER,
        cost=1 << 36,
        grid=(1,),
        out_specs=[pl.BlockSpec((members // INNER, width), lambda step: (0, 0))] * INNER,
    )(*away[::-1])
    whole = jax.ShapeDtypeStruct((own_members, all_cells), jnp.float32)
    result = call(
        functools.partial(place_kernel, cells),
        [vmem] * (outer + INNER),
        whole,
        out_specs=anywhere,
        scratch_shapes=[pltpu.SemaphoreType.DMA((2 * devices,))],
    )(*away, *swapped(near, 1))
    return call(
        functools.partial(place_last_kernel, cells),
        [vmem, anywhere],
        whole,
        input_output_aliases={1: 0},
        out_specs=anywhere,
        scratch_shapes=[pltpu.SemaphoreType.DMA((devices,))],
    )(ends, result)


def by_all_to_all(fields, observations, devices):
    own_members, all_cells = fields.shape
    cells = all_cells // devices
    amount = cells // PARTITION_SPAN
    members = own_members * devices
    span = PARTITION_SPAN
    (root_weight, reading), quad_position = window_terms(*observations, members)
    sent = fields.reshape(own_members, devices, cells).transpose(1, 0, 2)
    fields = lax.all_to_all(sent, "state", split_axis=0, concat_axis=0, tiled=True).reshape(members, cells)
    vmem = pl.BlockSpec(memory_space=pltpu.VMEM)
    own_seen = pl.pallas_call(
        pick_kernel,
        out_shape=jax.ShapeDtypeStruct((members, amount * OB), jnp.float32),
        in_specs=[vmem, vmem],
        out_specs=vmem,
        compiler_params=pltpu.CompilerParams(vmem_limit_bytes=16 << 20),
    )(fields, quad_position)
    edge = own_seen[:, : QUAD * OB]
    before = lax.ppermute(edge, "state", [(i, i + 1) for i in range(devices - 1)])
    after = lax.ppermute(edge, "state", [(i + 1, i) for i in range(devices - 1)])
    steps = amount // QUAD

    def whole(*shape):
        return pl.BlockSpec(shape, lambda step: (0, 0))

    analysis = pl.pallas_call(
        update_kernel,
        grid=(steps,),
        out_shape=jax.ShapeDtypeStruct((members, cells), jnp.float32),
        in_specs=[
            pl.BlockSpec((members, QUAD * span), lambda step: (0, step)),
            whole(members, QUAD * OB),
            whole(members, amount * OB),
            whole(members, QUAD * OB),
            whole(amount, 2 * QUAD * OB),
            whole(amount, 2 * QUAD * OB),
        ],
        out_specs=pl.BlockSpec((members, QUAD * span), lambda step: (0, step)),
        compiler_params=pltpu.CompilerParams(vmem_limit_bytes=40 << 20),
    )(fields, before, own_seen, after, root_weight, reading)
    result = lax.all_to_all(
        analysis.reshape(devices, own_members, cells), "state", split_axis=0, concat_axis=0, tiled=True
    )
    return result.transpose(1, 0, 2).reshape(own_members, all_cells)


def body(
    background_draws_table,
    measurement_reading,
    measurement_precision,
    sensed_point_position,
    measurement_tally,
    adjacent_tile_number,
):
    devices = lax.axis_size("state")
    observations = (
        measurement_reading,
        measurement_precision,
        sensed_point_position,
        measurement_tally,
        adjacent_tile_number,
    )
    way = in_stages if devices == INNER * INNER else by_all_to_all
    return way(background_draws_table, observations, devices)


def solution(mesh):
    return jax.shard_map(
        body,
        mesh=mesh,
        in_specs=(
            P("state", "groups"),
            P("groups", None),
            P("groups", None),
            P("groups", None),
            P("groups"),
            P(("groups", "state"), None),
        ),
        out_specs=P("state", "groups"),
        check_vma=False,
    )
```

```python
import functools

import jax
import jax.numpy as jnp
from jax import lax
from jax.experimental import pallas as pl
from jax.experimental.pallas import tpu as pltpu
from jax.sharding import PartitionSpec as P

PARTITION_SPAN = 128
OB = 32
R = 2
NS_ITERS = 5
LOC = 128

QUAD = PARTITION_SPAN // OB
INNER = 4
NN = (((1,), (0,)), ((), ()))
NT = (((1,), (1,)), ((), ()))


def halves(values):
    high = values.astype(jnp.bfloat16)
    return high, (values - high.astype(jnp.float32)).astype(jnp.bfloat16)


def times(left, right, dims):
    (left_high, left_low), (right_high, right_low) = left, right
    return lax.dot_general(
        jnp.concatenate([left_high, left_high, left_low], axis=1),
        jnp.concatenate([right_high, right_low, right_high], axis=dims[0][1][0]),
        dims,
        preferred_element_type=jnp.float32,
    )


def updated(blocks):
    turns = [analysis(*block) for block in blocks]
    results = [None] * len(turns)
    while None in results:
        for index, turn in enumerate(turns):
            if results[index] is None:
                results[index] = next(turn)
    return results


def analysis(fields, seen, root_weight, reading):
    seen_mean = jnp.mean(seen, axis=0, keepdims=True)
    pull = (reading - seen_mean) * root_weight
    root = halves((seen - seen_mean) * root_weight)
    spread = times(root, root, NT)
    pull = times(halves(jnp.broadcast_to(pull, (16, pull.shape[1]))), root, NT)
    yield None
    squares = jnp.sum(jnp.sum(spread * spread, axis=0, keepdims=True), axis=1, keepdims=True)
    norm_size = 1.0 + jnp.sqrt(squares)
    unit = 1.0 / norm_size
    rest = spread * (-0.5 * unit)
    cells = fields.T
    centre = jnp.mean(cells, axis=1, keepdims=True)
    chain = jnp.concatenate([cells - centre, pull], axis=0)
    for sweep in range(NS_ITERS - 1):
        parts = halves(rest)
        gain = 1.5 - 0.5 * unit
        if sweep < NS_ITERS - 2:
            square = times(parts, parts, NN)
        moved = times(halves(chain), parts, NN)
        yield None
        if sweep < NS_ITERS - 2:
            once = (gain - 0.5 * unit) * rest + square
            cubic = times(halves(once), parts, NN)
        chain = gain * chain + moved
        if sweep < NS_ITERS - 2:
            yield None
            rest = gain * once - (0.5 * unit * gain) * rest + cubic
            unit = unit * gain * gain
    moved = times(halves(chain), parts, NN)
    yield None
    end = (-0.5 * unit) * chain + moved
    for _ in range(2):
        moved = times(halves(end), parts, NN)
        yield None
        end = gain * end + moved
    chain = (1.5 * chain + end) * lax.rsqrt(norm_size)
    moved = chain[:PARTITION_SPAN]
    shift = jnp.sum(moved * chain[PARTITION_SPAN : PARTITION_SPAN + 1], axis=1, keepdims=True)
    yield (moved + (centre + shift)).T


def picked(fields, position):
    members = fields[0].shape[0]
    span = PARTITION_SPAN
    index = jnp.broadcast_to(position, (members, span))
    lanes = lax.broadcasted_iota(jnp.int32, (members, span), 1)
    total = None
    for spot, field in enumerate(fields):
        found = jnp.take_along_axis(field, index, axis=1)
        total = found if spot == 0 else jnp.where(lanes // OB == spot, found, total)
    return total


def pick_kernel(fields_ref, position_ref, seen_ref):
    span = PARTITION_SPAN
    quads = position_ref.shape[0]
    amount = quads * QUAD
    for quad in range(quads):
        blocks = [(quad * QUAD + spot - R) % amount for spot in range(QUAD)]
        fields = [fields_ref[:, block * span : (block + 1) * span] for block in blocks]
        seen_ref[:, quad * span : (quad + 1) * span] = picked(fields, position_ref[quad : quad + 1, :])


def pick_first_kernel(fields_ref, position_ref, seen_ref):
    span = PARTITION_SPAN
    amount = fields_ref.shape[1] // span - 1
    beyond = fields_ref[:, amount * span :]
    low = lax.broadcasted_iota(jnp.int32, beyond.shape, 1) < R * OB
    for quad in range(seen_ref.shape[1] // span):
        blocks = [max(quad * QUAD + spot - R, 0) for spot in range(QUAD)]
        fields = [fields_ref[:, block * span : (block + 1) * span] for block in blocks]
        found = picked(fields, position_ref[quad : quad + 1, :])
        seen_ref[:, quad * span : (quad + 1) * span] = found if quad else jnp.where(low, beyond, found)


def second_kernel(devices, beyond_ref, position_ref, *refs):
    *parts, fields_ref, seen_ref = refs
    parts = parts[::-1]
    place = lax.axis_index("state")
    span = PARTITION_SPAN
    quads = position_ref.shape[0]
    rows = fields_ref.shape[0] // devices
    for distance in range(devices):
        far, near = divmod(distance, INNER)
        start = pl.multiple_of((place ^ distance) * rows, rows)
        fields_ref[pl.ds(start, rows), :] = parts[far][near * rows : (near + 1) * rows, :]
    amount = fields_ref.shape[1] // span
    low = lax.broadcasted_iota(jnp.int32, beyond_ref.shape, 1) < R * OB
    for index in range(seen_ref.shape[1] // span):
        blocks = [min(index * QUAD + spot, amount - 1) for spot in range(QUAD)]
        fields = [fields_ref[:, block * span : (block + 1) * span] for block in blocks]
        quad = (quads - seen_ref.shape[1] // span + 1 + index) % quads
        found = picked(fields, position_ref[quad : quad + 1, :])
        seen_ref[:, index * span : (index + 1) * span] = found if quad else jnp.where(low, found, beyond_ref[...])


def update_kernel(fields_ref, before_ref, own_ref, after_ref, weight_ref, reading_ref, result_ref):
    members, span = before_ref.shape
    step = pl.program_id(0)
    steps = pl.num_programs(0)
    lanes = lax.broadcasted_iota(jnp.int32, (members, span), 1)
    here = own_ref[:, pl.ds(pl.multiple_of(step * span, span), span)]
    following = own_ref[:, pl.ds(pl.multiple_of(lax.rem(step + 1, steps) * span, span), span)]
    first = jnp.where((step == 0) & (lanes < R * OB), before_ref[...], here)
    second = jnp.where((step == steps - 1) & (lanes >= R * OB), after_ref[...], following)
    seen = jnp.concatenate([first, second], axis=1)
    blocks = [
        (
            fields_ref[:, spot * span : (spot + 1) * span],
            seen,
            weight_ref[pl.ds(step * QUAD + spot, 1), :],
            reading_ref[pl.ds(step * QUAD + spot, 1), :],
        )
        for spot in range(QUAD)
    ]
    for spot, result in enumerate(updated(blocks)):
        result_ref[:, spot * span : (spot + 1) * span] = result


def terms_kernel(
    amount, members, reading_ref, precision_ref, position_ref, tally_ref, adjacent_ref, terms_ref, quad_ref
):
    first_block = lax.axis_index("state") * amount
    total = tally_ref.shape[0]
    quads = amount // QUAD
    span = PARTITION_SPAN
    lane = lax.broadcasted_iota(jnp.int32, (1, span), 1)
    low = lane < R * OB

    def tile(ref, quad):
        row = first_block // QUAD + quad
        before = ref[pl.ds(jnp.maximum(row - 1, 0), 1), :]
        after = ref[pl.ds(jnp.minimum(row, total // QUAD - 1), 1), :]
        return pltpu.roll(jnp.where(low, after, before), R * OB, 1)

    def counts(quad):
        found = jnp.zeros((1, span), jnp.int32)
        for spot in range(QUAD):
            block = jnp.clip(first_block + quad * QUAD + spot - R, 0, total - 1)
            found = jnp.where(lane // OB == spot, tally_ref[block], found)
        return found

    def pair(tiles, quad):
        return jnp.concatenate(tiles[quad : quad + 2], axis=1)

    positions = [tile(position_ref, quad) for quad in range(quads + 1)]
    readings = [tile(reading_ref, quad) for quad in range(quads + 1)]
    precisions = [tile(precision_ref, quad) for quad in range(quads + 1)]
    tallies = [counts(quad) for quad in range(quads + 1)]
    wide = lax.broadcasted_iota(jnp.int32, (1, 2 * span), 1)
    for block in range(amount):
        quad, spot = divmod(block, QUAD)
        neighbour = wide // OB - spot
        usable = jnp.zeros((1, 2 * span), jnp.float32)
        for j in range(2 * R + 1):
            there = jnp.where(adjacent_ref[block, j] >= 0, 1.0, 0.0)
            usable = jnp.where(neighbour == j, there, usable)
        distance = (
            ((neighbour - R) * span).astype(jnp.float32)
            + pair(positions, quad).astype(jnp.float32)
            - 0.5 * (span - 1)
        )
        decay = jnp.exp(-0.5 * (distance / LOC) ** 2)
        active = jnp.where(wide % OB < pair(tallies, quad), usable, 0.0)
        weight = pair(precisions, quad) * decay * active
        terms_ref[0, block : block + 1, :] = jnp.sqrt(weight / (members - 1.0))
        terms_ref[1, block : block + 1, :] = pair(readings, quad)
    edge = jnp.where(low, positions[quads], positions[0])
    for quad in range(quads):
        quad_ref[quad : quad + 1, :] = positions[quad] if quad else edge


def window_terms(reading, precision, position, tally, adjacent, members):
    amount = adjacent.shape[0]
    lanes = QUAD * OB
    vmem = pl.BlockSpec(memory_space=pltpu.VMEM)
    smem = pl.BlockSpec(memory_space=pltpu.SMEM)
    terms = jax.ShapeDtypeStruct((2, amount, 2 * lanes), jnp.float32)
    return pl.pallas_call(
        functools.partial(terms_kernel, amount, members),
        out_shape=[terms, jax.ShapeDtypeStruct((amount // QUAD, lanes), jnp.int32)],
        in_specs=[vmem, vmem, vmem, smem, smem],
        out_specs=[vmem, vmem],
    )(*(array.reshape(-1, lanes) for array in (reading, precision, position)), tally, adjacent)


def copied(copies):
    for copy in copies:
        copy.start()
    return copies


def first_part_kernel(fields_ref, given_ref, sent_ref, held_ref, edges_ref, position_ref, sems):
    devices, rows, size = sent_ref.shape
    cells = fields_ref.shape[1] // devices
    span = PARTITION_SPAN
    half = R * span
    split = size - span
    amount = cells // span
    copies = []

    def add(start, length, target):
        source = fields_ref.at[:, pl.ds(start, length)]
        copies.append(pltpu.make_async_copy(source, target, sems.at[len(copies)]))

    for border in range(devices + 1):
        start = min(max(border * cells - half, 0), devices * cells - 2 * half)
        add(start, 2 * half, edges_ref.at[border])
    copies.append(pltpu.make_async_copy(given_ref, position_ref, sems.at[len(copies)]))
    ahead = len(copies)
    for device in range(devices):
        add(device * cells, split, held_ref.at[device, :, pl.ds(0, split)])
    copied(copies)
    for copy in copies[:ahead]:
        copy.wait()

    def shifted(array, distance):
        if distance > 0:
            return jnp.concatenate([array[:distance], array[:-distance]], axis=0)
        return jnp.concatenate([array[-distance:], array[distance:]], axis=0)

    beyond = [(amount - R + spot, 1) for spot in range(R)] + [(spot, -1) for spot in range(R)]
    positions = position_ref[...].T.reshape(devices, amount, OB)
    position = jnp.concatenate([shifted(positions[:, block], distance) for block, distance in beyond], axis=1)
    position = jnp.broadcast_to(position[:, None], (devices, rows, span)).reshape(devices * rows, span)
    fields = []
    for spot, (_, distance) in enumerate(beyond):
        first = 0 if distance > 0 else 1
        found = edges_ref[first : first + devices, :, spot * span : (spot + 1) * span]
        fields.append(found.reshape(devices * rows, span))
    held_ref[:, :, split:] = picked(fields, position).reshape(devices, rows, span)
    out = []
    for device, copy in enumerate(copies[ahead:]):
        copy.wait()
        if device % INNER == INNER - 1:
            some = pl.ds(device + 1 - INNER, INNER)
            sem = sems.at[len(copies) + len(out)]
            out += copied([pltpu.make_async_copy(held_ref.at[some], sent_ref.at[some], sem)])
    for copy in out:
        copy.wait()


def second_part_kernel(split, fields_ref, *refs):
    *sent, sems = refs
    place = lax.axis_index("state")
    rows = fields_ref.shape[0]
    size = sent[0].shape[1]
    cells = split + size
    copies = []
    for near, array in enumerate(sent):
        for far in range(array.shape[0] // rows):
            start = (place ^ (far * INNER + near)) * cells + split
            source = fields_ref.at[:, pl.ds(pl.multiple_of(start, PARTITION_SPAN), size)]
            target = array.at[pl.ds(far * rows, rows), :]
            copies.append(pltpu.make_async_copy(source, target, sems.at[len(copies)]))
    for copy in copied(copies):
        copy.wait()


def turn_kernel(rows, *refs):
    given, made = refs[: len(refs) // 2][::-1], refs[len(refs) // 2 :]
    for i, source in enumerate(given):
        for j, target in enumerate(made):
            target[i * rows : (i + 1) * rows, :] = source[j * rows : (j + 1) * rows, :]


def place_moves(moves, sems):
    started = [pltpu.make_async_copy(*move, sems.at[index]) for index, move in enumerate(moves)]
    for copy in started:
        copy.start()
    for copy in started:
        copy.wait()


def place_kernel(cells, *refs):
    *parts, result_ref, sems = refs
    firsts, seconds = parts[:-INNER], parts[-INNER:]
    place = lax.axis_index("state")
    rows = result_ref.shape[0]
    width = QUAD * PARTITION_SPAN
    moves = []

    def add(source, distance, start):
        target = result_ref.at[:, pl.ds(pl.multiple_of((place ^ distance) * cells + start, width), width)]
        moves.append((source, target))

    for far, part in enumerate(firsts):
        for near in range(INNER):
            add(part.at[pl.ds(near * rows, rows), pl.ds(0, width)], far * INNER + near, 0)
    for near, part in enumerate(seconds):
        for far in range(len(firsts)):
            add(part.at[pl.ds(far * rows, rows), :], far * INNER + near, width)
    place_moves(moves, sems)


def place_last_kernel(cells, last_ref, _, result_ref, sems):
    rows = result_ref.shape[0]
    size = last_ref.shape[1]
    moves = []
    for device in range(last_ref.shape[0] // rows):
        target = result_ref.at[:, pl.ds((device + 1) * cells - size, size)]
        moves.append((last_ref.at[pl.ds(device * rows, rows), :], target))
    place_moves(moves, sems)


def join_kernel(rows, *refs):
    near, refs = refs[:INNER], refs[INNER:]
    given, made = refs[: len(refs) // 2], refs[len(refs) // 2 :]
    width = near[0].shape[1]
    for far, (source, target) in enumerate(zip(given, made)):
        for i, part in enumerate(near):
            target[i * rows : (i + 1) * rows, :width] = part[far * rows : (far + 1) * rows, :]
        target[:, width:] = source[...]


def reordered(ref, devices, near_first):
    place = lax.axis_index("state")
    rows = ref.shape[0] // devices
    order = list(range(devices))
    if near_first:
        order.sort(key=lambda distance: (distance % INNER, distance // INNER))
    starts = [pl.multiple_of((place ^ distance) * rows, rows) for distance in order]
    return jnp.concatenate([ref[pl.ds(start, rows), :] for start in starts], axis=0)


def blocks_of(fields, here, there, first, terms_ref):
    span = PARTITION_SPAN
    seen = jnp.concatenate([here, there], axis=1)
    blocks = []
    for spot in range(QUAD):
        root_weight, reading = (terms_ref[term, pl.ds(first + spot, 1), :] for term in range(2))
        blocks.append((fields[:, spot * span : (spot + 1) * span], seen, root_weight, reading))
    return blocks


def head_kernel(quad, devices, fields_ref, here_ref, there_ref, terms_ref, *results):
    span = PARTITION_SPAN
    fields, here, there = [reordered(ref, devices, quad == 0) for ref in (fields_ref, here_ref, there_ref)]
    for spot, result in enumerate(updated(blocks_of(fields, here, there, quad * QUAD, terms_ref))):
        start = 0
        for result_ref in results:
            rows = result_ref.shape[0]
            result_ref[:, spot * span : (spot + 1) * span] = result[start : start + rows]
            start += rows


def tail_kernel(first_ref, begin_ref, end_ref, here_ref, tiles_ref, terms_ref, result_ref):
    span = PARTITION_SPAN
    step = pl.program_id(0)
    begin = jnp.where(step == 0, first_ref[...], begin_ref[...])
    fields = jnp.concatenate([begin, end_ref[...]], axis=1)
    here = jnp.where(step == 0, here_ref[...], tiles_ref[:, :span])
    there = jnp.where(step == 0, tiles_ref[:, :span], tiles_ref[:, span:])
    first = terms_ref.shape[1] + (step - 2) * QUAD
    for spot, result in enumerate(updated(blocks_of(fields, here, there, first, terms_ref))):
        result_ref[:, spot * span : (spot + 1) * span] = result


def in_stages(fields, observations, devices):
    own_members, all_cells = fields.shape
    cells = all_cells // devices
    amount = cells // PARTITION_SPAN
    members = own_members * devices
    outer = devices // INNER
    quads = amount // QUAD
    width = QUAD * PARTITION_SPAN
    lanes = QUAD * OB
    early = quads - 2
    late = 2
    half = R * PARTITION_SPAN
    anywhere = pl.BlockSpec(memory_space=pl.ANY)
    vmem = pl.BlockSpec(memory_space=pltpu.VMEM)

    def call(kernel, inputs, outputs, grant=16, cost=1, **options):
        return pl.pallas_call(
            kernel,
            out_shape=outputs,
            in_specs=inputs,
            compiler_params=pltpu.CompilerParams(vmem_limit_bytes=grant << 20),
            cost_estimate=pl.CostEstimate(flops=cost, bytes_accessed=1, transcendentals=0),
            **options,
        )

    def columns(size, index):
        return pl.BlockSpec((members, size), lambda step: (0, index))

    def full(array):
        return pl.BlockSpec(array.shape, lambda step: (0,) * array.ndim)

    def group(parts, size):
        return jax.ShapeDtypeStruct((members // parts, size), jnp.float32)

    def swapped(arrays, unit):
        pairs = [[(i, i ^ (unit * k)) for i in range(devices)] for k in range(len(arrays))]
        far_first = [lax.ppermute(arrays[k], "state", pairs[k]) for k in reversed(range(1, len(arrays)))]
        return [arrays[0]] + far_first[::-1]

    def second_parts():
        return call(
            functools.partial(second_part_kernel, split),
            [anywhere],
            [group(INNER, cells - split)] * INNER,
            out_specs=[vmem] * INNER,
            scratch_shapes=[pltpu.SemaphoreType.DMA((devices,))],
        )(fields)

    def turned(arrays, parts, cost=1):
        return call(
            functools.partial(turn_kernel, own_members),
            [vmem] * len(arrays),
            [group(parts, arrays[0].shape[1])] * parts,
            cost=cost,
            out_specs=[vmem] * parts,
        )(*arrays[::-1])

    def exchanged(array):
        return lax.all_to_all(array, "state", split_axis=0, concat_axis=0, tiled=True)

    split = early * width + half
    sent = call(
        first_part_kernel,
        [anywhere, anywhere],
        jax.ShapeDtypeStruct((devices, own_members, split + lanes), jnp.float32),
        grant=56,
        out_specs=anywhere,
        scratch_shapes=[
            pltpu.VMEM((devices, own_members, split + lanes), jnp.float32),
            pltpu.VMEM((devices + 1, own_members, 2 * half), jnp.float32),
            pltpu.VMEM(observations[2].shape[::-1], jnp.int32),
            pltpu.SemaphoreType.DMA((3 * devices + outer + 1,)),
        ],
    )(fields, observations[2].T)
    first = exchanged(sent).reshape(members, split + lanes)
    second = turned(swapped(second_parts(), 1), outer)
    second, reading = lax.optimization_barrier((second, observations[0]))
    observations = [reading, *observations[1:]]
    terms, quad_position = window_terms(*observations, members)
    second, terms, quad_position = lax.optimization_barrier((second, terms, quad_position))
    second = swapped(second, INNER)
    seen = call(
        pick_first_kernel,
        [vmem, vmem],
        jax.ShapeDtypeStruct((members, (early + 1) * lanes), jnp.float32),
        out_specs=vmem,
    )(first, quad_position)

    def head(quad, parts, seen):
        return call(
            functools.partial(head_kernel, quad, devices),
            [columns(width, quad), columns(lanes, quad), columns(lanes, quad + 1), full(terms)],
            [group(parts, width)] * parts,
            grant=40,
            grid=(1,),
            out_specs=[pl.BlockSpec((members // parts, width), lambda step: (0, 0))] * parts,
        )(first, seen, seen, terms)

    groups = head(0, INNER, seen)
    seen, groups, second[1] = lax.optimization_barrier((seen, groups, second[1]))
    near = swapped(groups, 1)
    groups = head(1, outer, seen)
    away = call(
        functools.partial(join_kernel, own_members),
        [vmem] * (INNER + outer),
        [group(outer, 2 * width)] * outer,
        out_specs=[vmem] * outer,
    )(*near, *groups)
    away, second = lax.optimization_barrier((away, second))
    away = swapped(away, INNER)

    second, tiles = call(
        functools.partial(second_kernel, devices),
        [columns(lanes, split // lanes), *[full(array) for array in (quad_position, *second[::-1])]],
        [
            jax.ShapeDtypeStruct((members, cells - split), jnp.float32),
            jax.ShapeDtypeStruct((members, 2 * lanes), jnp.float32),
        ],
        grid=(1,),
        out_specs=[columns(cells - split, 0), columns(2 * lanes, 0)],
    )(first, quad_position, *second[::-1])
    ends = call(
        tail_kernel,
        [
            columns(half, split // half - 1),
            columns(half, 1),
            pl.BlockSpec((members, half), lambda step: (0, 2 * step)),
            columns(lanes, early),
            full(tiles),
            full(terms),
        ],
        jax.ShapeDtypeStruct((members, late * width), jnp.float32),
        grant=40,
        grid=(late,),
        out_specs=pl.BlockSpec((members, width), lambda step: (0, step)),
    )(first, second, second, seen, tiles, terms)
    ends = exchanged(ends.reshape(devices, own_members, late * width)).reshape(members, late * width)

    near = call(
        functools.partial(turn_kernel, own_members),
        [pl.BlockSpec((members // outer, width), lambda step: (0, 1))] * outer,
        [group(INNER, width)] * INNER,
        cost=1 << 36,
        grid=(1,),
        out_specs=[pl.BlockSpec((members // INNER, width), lambda step: (0, 0))] * INNER,
    )(*away[::-1])
    whole = jax.ShapeDtypeStruct((own_members, all_cells), jnp.float32)
    result = call(
        functools.partial(place_kernel, cells),
        [vmem] * (outer + INNER),
        whole,
        out_specs=anywhere,
        scratch_shapes=[pltpu.SemaphoreType.DMA((2 * devices,))],
    )(*away, *swapped(near, 1))
    return call(
        functools.partial(place_last_kernel, cells),
        [vmem, anywhere],
        whole,
        input_output_aliases={1: 0},
        out_specs=anywhere,
        scratch_shapes=[pltpu.SemaphoreType.DMA((devices,))],
    )(ends, result)


def by_all_to_all(fields, observations, devices):
    own_members, all_cells = fields.shape
    cells = all_cells // devices
    amount = cells // PARTITION_SPAN
    members = own_members * devices
    span = PARTITION_SPAN
    (root_weight, reading), quad_position = window_terms(*observations, members)
    sent = fields.reshape(own_members, devices, cells).transpose(1, 0, 2)
    fields = lax.all_to_all(sent, "state", split_axis=0, concat_axis=0, tiled=True).reshape(members, cells)
    vmem = pl.BlockSpec(memory_space=pltpu.VMEM)
    own_seen = pl.pallas_call(
        pick_kernel,
        out_shape=jax.ShapeDtypeStruct((members, amount * OB), jnp.float32),
        in_specs=[vmem, vmem],
        out_specs=vmem,
        compiler_params=pltpu.CompilerParams(vmem_limit_bytes=16 << 20),
    )(fields, quad_position)
    edge = own_seen[:, : QUAD * OB]
    before = lax.ppermute(edge, "state", [(i, i + 1) for i in range(devices - 1)])
    after = lax.ppermute(edge, "state", [(i + 1, i) for i in range(devices - 1)])
    steps = amount // QUAD

    def whole(*shape):
        return pl.BlockSpec(shape, lambda step: (0, 0))

    analysis = pl.pallas_call(
        update_kernel,
        grid=(steps,),
        out_shape=jax.ShapeDtypeStruct((members, cells), jnp.float32),
        in_specs=[
            pl.BlockSpec((members, QUAD * span), lambda step: (0, step)),
            whole(members, QUAD * OB),
            whole(members, amount * OB),
            whole(members, QUAD * OB),
            whole(amount, 2 * QUAD * OB),
            whole(amount, 2 * QUAD * OB),
        ],
        out_specs=pl.BlockSpec((members, QUAD * span), lambda step: (0, step)),
        compiler_params=pltpu.CompilerParams(vmem_limit_bytes=40 << 20),
    )(fields, before, own_seen, after, root_weight, reading)
    result = lax.all_to_all(
        analysis.reshape(devices, own_members, cells), "state", split_axis=0, concat_axis=0, tiled=True
    )
    return result.transpose(1, 0, 2).reshape(own_members, all_cells)


def body(
    background_draws_table,
    measurement_reading,
    measurement_precision,
    sensed_point_position,
    measurement_tally,
    adjacent_tile_number,
):
    devices = lax.axis_size("state")
    observations = (
        measurement_reading,
        measurement_precision,
        sensed_point_position,
        measurement_tally,
        adjacent_tile_number,
    )
    way = in_stages if devices == INNER * INNER else by_all_to_all
    return way(background_draws_table, observations, devices)


def solution(mesh):
    return jax.shard_map(
        body,
        mesh=mesh,
        in_specs=(
            P("state", "groups"),
            P("groups", None),
            P("groups", None),
            P("groups", None),
            P("groups"),
            P(("groups", "state"), None),
        ),
        out_specs=P("state", "groups"),
        check_vma=False,
    )
```
